32 devices in a mesh: lon: 8 (over z, x), lat: 4 (over y, core).
Axes of the slice: x: 2, y: 2, z: 4, core: 2. Of those that a mesh axis runs over, the one named last changes fastest.
Arguments:
- piece_height: float32 [64, 128, 128], P('lon', 'lat')
- piece_weight: float32 [64, 128, 128], P('lon', 'lat'), may hold values from 0.05 to 2
- piece_column: int32 [64], P('lon'), may hold values from 0 to 32640, as said below
- piece_width: int32 [64], P('lon'), may hold values from 64 to 128
Outputs:
- solution_field: float32 [128, 32768], P('lat', 'lon')
- residual: float32 [128, 32768], P('lat', 'lon')
The draws below stay inside these ranges and needn't reach their ends.
Inputs may be any that keep to these rules, and one draw needn't show every extreme that they name: Every value is a multiple of 128 and a piece lies inside one tile of 4096 columns, tile piece_column // 4096. The pieces of one device name each tile at most 2 times; one tile is named exactly 2 times by the pieces of every device.
All inputs are finite; a program needn't handle non-finite values.
Results may differ from the reference program's by a relative error of at most 0.0007.
Values sent between devices are 32-bit elements; how exact they have to be, the bound alone decides.
A program may use at most 128 MiB of HBM per device.

```python
import math
import jax
import jax.numpy as jnp

ROWS = 128
COLS_DEV = 4096
BW = 128
CAPACITY = 2
ITERS = 4
PIECES_DEV = 8
PIECES = 64
N_LON = 8


def piece_columns(key):
    key = jax.random.fold_in(key, 11)
    key_common, key_order, key_block = jax.random.split(key, 3)
    slot_total = N_LON * CAPACITY
    common_tile = jax.random.randint(key_common, (), 0, N_LON)

    def one_owner(owner_key):
        first_key, second_key = jax.random.split(owner_key)
        others = jax.random.permutation(first_key, slot_total - CAPACITY).astype(jnp.int32)
        others = jnp.where(others >= CAPACITY * common_tile, others + CAPACITY, others)
        leading = CAPACITY * common_tile + jnp.arange(CAPACITY, dtype=jnp.int32)
        chosen = jnp.concatenate([leading, others])[:PIECES_DEV]
        chosen = jax.random.permutation(second_key, chosen)
        return chosen // CAPACITY
    tiles = jax.vmap(one_owner)(jax.random.split(key_order, N_LON)).reshape(-1)
    blocks = jax.random.randint(key_block, (PIECES,), 0, COLS_DEV // BW)
    return (tiles * COLS_DEV + blocks * BW).astype(jnp.int32)


def draw_piece_column(key, part):
    return piece_columns(key)


def draw_piece_height(key, part):
    columns = piece_columns(key)
    key = jax.random.fold_in(key, 3)
    key_cell, key_offset = jax.random.split(key, 2)
    ramp = jnp.exp(math.log(3.0) * columns.astype(jnp.float32) / (COLS_DEV * N_LON))
    cells = jax.random.normal(key_cell, (PIECES, ROWS, BW), jnp.float32)
    offset = 2.0 * jax.random.normal(key_offset, (PIECES, 1, 1), jnp.float32)
    return ((cells + offset) * ramp[:, None, None]).astype(jnp.float32)


def set_ends(array, key, least, high):
    longest = array.shape.index(max(array.shape))
    spots = []
    for shift in (0, 1):
        where = [jax.random.randint(jax.random.fold_in(key, axis), (), 0, length) for axis, length in enumerate(array.shape)]
        where[longest] = (where[longest] + shift) % array.shape[longest]
        spots.append(tuple(where))
    return array.at[spots[0]].set(least).at[spots[1]].set(high)


def block_levels(own_key, dims, shards, least, top_value):
    def one(axis_at, shards_of):
        steps = jax.random.uniform(jax.random.fold_in(jax.random.fold_in(own_key, 6), axis_at), (shards_of,), jnp.float32, least / len(shards), top_value / len(shards))
        return jnp.repeat(jnp.exp(steps), dims[axis_at] // shards_of).reshape((-1,) + (1,) * (len(dims) - axis_at - 1))

    level = one(*shards[0])
    for cut in shards[1:]:
        level = level * one(*cut)
    return level


def setup_inputs(seed: int = 0) -> dict:
    arg_keys = jax.random.split(jax.random.key(seed), 5)
    return {
        "piece_height": draw_piece_height(jax.random.fold_in(arg_keys[4], 71), 0),
        "piece_weight": jnp.clip(jnp.exp(math.log(2.0) - 3.6888794 * jax.random.uniform(arg_keys[1], (PIECES, ROWS, BW), jnp.float32) ** block_levels(arg_keys[1], (PIECES, ROWS, BW), ((0, 8), (1, 4)), -0.2, 0.2)), 0.05, 2.0),
        "piece_column": draw_piece_column(jax.random.fold_in(arg_keys[4], 71), 0),
        "piece_width": set_ends(jax.random.randint(arg_keys[3], (PIECES,), BW // 2, BW + 1), jax.random.fold_in(arg_keys[3], 1), BW // 2, BW).astype(jnp.int32),
    }


MU_DATA = 0.5
DAMPING = 0.5
RIDGE = 0.05


def piece_terms(height, weight, width, north_step, row_global):
    column = jnp.arange(height.shape[2], dtype=jnp.int32)
    valid_cell = column[None, None, :] < width[:, None, None]
    east_edge = (column[None, None, :] + 1) < width[:, None, None]
    north_edge = valid_cell & (row_global[None, :, None] < ROWS - 1)
    weights_full = weight.astype(jnp.float32)
    east_step = jnp.concatenate([height[:, :, 1:] - height[:, :, :-1], jnp.zeros_like(height[:, :, :1])], axis=2)
    cell_weight = jnp.where(valid_cell, weights_full, jnp.float32(0.0))
    east_weight = jnp.where(east_edge, weights_full, jnp.float32(0.0))
    north_weight = jnp.where(north_edge, weights_full, jnp.float32(0.0))
    return (cell_weight, cell_weight * height, east_weight, east_weight * east_step,
            north_weight, north_weight * north_step)


def reference(piece_height, piece_weight, piece_column, piece_width):
    row_global = jnp.arange(ROWS, dtype=jnp.int32)
    north_step = jnp.concatenate([piece_height[:, 1:, :] - piece_height[:, :-1, :],
                                  jnp.zeros_like(piece_height[:, :1, :])], axis=1)
    terms = piece_terms(piece_height, piece_weight, piece_width, north_step, row_global)
    block_ids = (piece_column // BW).astype(jnp.int32)
    total_blocks = N_LON * COLS_DEV // BW
    fields = []
    for term in terms:
        summed = jax.ops.segment_sum(term, block_ids, num_segments=total_blocks)
        fields.append(jnp.transpose(summed, (1, 0, 2)).reshape(ROWS, total_blocks * BW))
    weight_sum, height_sum, east_weight_sum, east_sum, north_weight_sum, north_sum = fields
    target_east = east_sum / (east_weight_sum + DAMPING)
    target_north = north_sum / (north_weight_sum + DAMPING)
    south_target = jnp.concatenate([jnp.zeros_like(target_north[:1]), target_north[:-1]], axis=0)
    right_side = MU_DATA * height_sum - (target_east - jnp.roll(target_east, 1, axis=1)) - (target_north - south_target)
    diagonal = MU_DATA * weight_sum + RIDGE
    has_upper = (row_global < ROWS - 1)[:, None]
    has_lower = (row_global > 0)[:, None]

    def operate(field):
        coupling = 2.0 * field - jnp.roll(field, 1, axis=1) - jnp.roll(field, -1, axis=1)
        coupling = coupling + jnp.where(has_upper, field - jnp.roll(field, -1, axis=0), jnp.float32(0.0))
        coupling = coupling + jnp.where(has_lower, field - jnp.roll(field, 1, axis=0), jnp.float32(0.0))
        return diagonal * field + coupling

    solution_field = jnp.zeros_like(right_side)
    residual = right_side
    direction = right_side
    norm_now = jnp.sum(residual * residual)
    for iteration in range(ITERS):
        image = operate(direction)
        alpha = norm_now / jnp.sum(direction * image)
        solution_field = solution_field + alpha * direction
        residual = residual - alpha * image
        norm_next = jnp.sum(residual * residual)
        direction = residual + (norm_next / norm_now) * direction
        norm_now = norm_next
    return solution_field, residual
```

```python
import functools

import jax
import jax.numpy as jnp
from jax import lax
from jax.experimental import pallas as pl
from jax.experimental.pallas import tpu as pltpu
from jax.sharding import PartitionSpec as P

COLS_DEV = 4096
ITERS = 4
MU_DATA = 0.5
DAMPING = 0.5
RIDGE = 0.05
SHIFT = 5.0
SCALE = 5.0

LANES = 128
MESH = pl.DeviceIdType.MESH
F32 = jnp.float32


def remote(src, dst, send, recv, device):
    return pltpu.make_async_remote_copy(
        src_ref=src, dst_ref=dst, send_sem=send, recv_sem=recv,
        device_id=device, device_id_type=MESH,
    )


def cg_coefficients(mu):
    def inner(a, b):
        total = None
        for i, x in enumerate(a):
            for j, y in enumerate(b):
                term = x * y * mu[i + j]
                total = term if total is None else total + term
        return total

    def apply(c):
        out = [SHIFT * x for x in c] + [jnp.zeros_like(c[0])]
        for i, x in enumerate(c):
            out[i + 1] = out[i + 1] + SCALE * x
        return out

    def add_scaled(y, a, x):
        out = []
        for i in range(max(len(x), len(y))):
            if i >= len(y):
                out.append(a * x[i])
            elif i >= len(x):
                out.append(y[i])
            else:
                out.append(y[i] + a * x[i])
        return out

    one = jnp.ones_like(mu[0])
    residual, direction, field = [one], [one], []
    norm = mu[0]
    for step in range(ITERS):
        image = apply(direction)
        alpha = norm / inner(direction, image)
        field = add_scaled(field, alpha, direction)
        residual = add_scaled(residual, -alpha, image)
        if step < ITERS - 1:
            fresh = inner(residual, residual)
            direction = add_scaled(residual, fresh / norm, direction)
            norm = fresh
    return field, residual


def kernel(
    n, lats, pieces, rows,
    col_ref, wid_ref, h_ref, w_ref, x_ref, r_ref,
    hs, ws, hr, wr, ms, mr, msm, idx_s, up_s, up_r, dn_s, dn_r,
    blk_s, prev_s, last_v, last_s, S,
    V, D, east_s, east_r, west_s, west_r, lat_up_s, lat_up_r, lat_dn_s, lat_dn_r,
    red, ra, rb,
    sem_m, sem_h, sem_w, sem_e, sem_l, sem_t, sem_a, sem_b, sem_loc,
):
    lon = lax.axis_index("lon")
    lat = lax.axis_index("lat")
    blocks = COLS_DEV // LANES
    ext = blocks + 2
    top = rows + 8
    slots = 2 * n
    lane = lax.broadcasted_iota(jnp.int32, (rows, LANES), 1)
    lane1 = lax.broadcasted_iota(jnp.int32, (1, LANES), 1)

    def lon_at(k):
        return lax.rem(lon + k, n)

    def lat_at(k):
        return lax.rem(lat + k, lats)

    barrier = pltpu.get_barrier_semaphore()

    @pl.loop(1, n)
    def _(k):
        pl.semaphore_signal(barrier, inc=1, device_id=(lon_at(k), lat), device_id_type=MESH)

    @pl.loop(1, lats)
    def _(k):
        pl.semaphore_signal(barrier, inc=1, device_id=(lon, lat_at(k)), device_id_type=MESH)

    @pl.loop(0, pieces)
    def _(i):
        up_s[0, pl.ds(i, 1), :] = h_ref[i, rows - 1 : rows, :]
        up_s[1, pl.ds(i, 1), :] = w_ref[i, rows - 1 : rows, :]
        dn_s[pl.ds(i, 1), :] = h_ref[i, 0:1, :]

    def fill(k, h_to, w_to, m_to):
        dest = lon_at(k)

        def scan(i, found):
            first, second = found
            match = (col_ref[i] >> 12) == dest
            second = jnp.where(match & (first >= 0) & (second < 0), i, second)
            first = jnp.where(match & (first < 0), i, first)
            return first, second

        found = lax.fori_loop(0, pieces, scan, (jnp.int32(-1), jnp.int32(-1)), unroll=8)
        tags = []
        for q in range(2):
            at = jnp.maximum(found[q], 0)
            limit = jnp.where(found[q] >= 0, wid_ref[at], 0)
            tags.append(jnp.where(found[q] >= 0, (col_ref[at] >> 7) & (blocks - 1), -1))
            idx_s[k, q] = at
            idx_s[k, 2 + q] = limit
            h_to[k, q * rows : (q + 1) * rows, :] = h_ref[at]
            w_to[k, q * rows : (q + 1) * rows, :] = jnp.where(lane < limit, w_ref[at], 0.0)
        m_to[k] = jnp.where(lane1 == 0, tags[0], jnp.where(lane1 == 1, tags[1], -1))

    fill(0, hr, wr, mr)

    @pl.loop(1, n)
    def _(k):
        fill(k, hs, ws, ms)

    pl.semaphore_wait(barrier, n - 1 + lats - 1)

    def edge_up():
        return remote(up_s, up_r, sem_e.at[0], sem_e.at[1], (lon, lat_at(1)))

    def edge_dn():
        return remote(dn_s, dn_r, sem_e.at[2], sem_e.at[3], (lon, lat_at(lats - 1)))

    def meta(k):
        return remote(ms.at[k], mr.at[k], sem_m.at[0, k], sem_m.at[1, k], (lon_at(k), lat))

    def heights(k):
        return remote(hs.at[k], hr.at[k], sem_h.at[0, k], sem_h.at[1, k], (lon_at(k), lat))

    def weights(k):
        return remote(ws.at[k], wr.at[k], sem_w.at[0, k], sem_w.at[1, k], (lon_at(k), lat))

    @pl.when(lat < lats - 1)
    def _():
        edge_up().start()

    @pl.when(lat > 0)
    def _():
        edge_dn().start()

    @pl.loop(1, n)
    def _(k):
        meta(k).start()

    @pl.loop(1, n)
    def _(k):
        heights(k).start()

    @pl.when(lat > 0)
    def _():
        edge_up().wait_recv()

    @pl.when(lat == 0)
    def _():
        up_r[...] = jnp.zeros_like(up_r)

    @pl.when(lat < lats - 1)
    def _():
        edge_dn().wait_recv()

    @pl.when(lat == lats - 1)
    def _():
        dn_r[...] = jnp.zeros_like(dn_r)

    def extras(k, w_to):
        for q in range(2):
            at, limit = idx_s[k, q], idx_s[k, 2 + q]
            base = 2 * rows + q
            w_to[k, base : base + 1, :] = dn_r[pl.ds(at, 1), :]
            w_to[k, base + 2 : base + 3, :] = up_r[0, pl.ds(at, 1), :]
            w_to[k, base + 4 : base + 5, :] = jnp.where(lane1 < limit, up_r[1, pl.ds(at, 1), :], 0.0)
        w_to[k, 2 * rows + 6 : 2 * rows + 8, :] = jnp.zeros((2, LANES), F32)

    @pl.loop(1, n)
    def _(k):
        extras(k, ws)
        weights(k).start()

    extras(0, wr)

    @pl.loop(1, n)
    def _(k):
        meta(k).wait_recv()

    tags_in = pltpu.make_async_copy(mr, msm, sem_loc.at[0])
    tags_in.start()
    tags_in.wait()

    @pl.loop(0, n)
    def _(k):
        blk_s[2 * k] = msm[k, 0, 0]
        blk_s[2 * k + 1] = msm[k, 0, 1]

    def latest(p, last):
        tag = blk_s[p]

        def scan(j, found):
            return jnp.where((j < p) & (blk_s[j] == tag), j, found)

        prev_s[p] = lax.fori_loop(0, slots, scan, jnp.int32(slots), unroll=8)
        return jnp.where(lane1 == tag, p, last)

    last_v[...] = lax.fori_loop(0, slots, latest, jnp.full((1, LANES), slots, jnp.int32))
    last_in = pltpu.make_async_copy(last_v, last_s, sem_loc.at[1])
    last_in.start()
    last_in.wait()

    S[slots] = jnp.zeros((6 * rows + 8, LANES), F32)
    row_global = lat * rows + lax.broadcasted_iota(jnp.int32, (rows, LANES), 0)
    has_north = row_global < lats * rows - 1
    row_in = lax.broadcasted_iota(jnp.int32, (rows, LANES), 0)

    def terms(k):
        for q in range(2):
            p = 2 * k + q
            before = prev_s[p]
            h = hr[k, q * rows : (q + 1) * rows, :]
            w = wr[k, q * rows : (q + 1) * rows, :]
            base = 2 * rows + q
            above = wr[k, base : base + 1, :]
            below_h = wr[k, base + 2 : base + 3, :]
            below_w = wr[k, base + 4 : base + 5, :]
            h_north = jnp.where(row_in == rows - 1, above, pltpu.roll(h, rows - 1, 0))
            h_east = pltpu.roll(h, LANES - 1, 1)
            w_east = jnp.where((pltpu.roll(w, LANES - 1, 1) > 0.0) & (lane < LANES - 1), w, 0.0)
            w_north = jnp.where(has_north, w, 0.0)
            parts = (w, w * h, w_east, w_east * (h_east - h), w_north, w_north * (h_north - h))
            for t, part in enumerate(parts):
                at = pl.ds(t * rows, rows)
                S[p, at, :] = part + S[before, at, :]
            at = 6 * rows
            S[p, at : at + 1, :] = below_w + S[before, at : at + 1, :]
            S[p, at + 1 : at + 2, :] = below_w * (h[0:1, :] - below_h) + S[before, at + 1 : at + 2, :]

    terms(0)

    @pl.loop(1, n)
    def _(k):
        heights(k).wait_recv()
        weights(k).wait_recv()
        terms(k)

    inv = 1.0 / SCALE

    def assemble(b, before):
        p = last_s[0, b]

        def field(t):
            return S[p, t * rows : (t + 1) * rows, :]

        at = 6 * rows
        t_east = field(3) / (field(2) + DAMPING)
        t_north = field(5) / (field(4) + DAMPING)
        t_below = S[p, at + 1 : at + 2, :] / (S[p, at : at + 1, :] + DAMPING)
        t_south = jnp.where(row_in == 0, t_below, pltpu.roll(t_north, 1, 0))
        rolled = pltpu.roll(t_east, 1, 1)
        t_west = jnp.where(lane == 0, before, rolled)
        right = MU_DATA * field(1) - (t_east - t_west) - (t_north - t_south)
        cols = pl.ds(pl.multiple_of((b + 1) * LANES, LANES), LANES)
        V[0, 8:top, cols] = right
        D[8:top, cols] = (MU_DATA * field(0) + (RIDGE + 4.0 - SHIFT)) * inv
        return rolled

    east_last = lax.fori_loop(0, blocks, assemble, jnp.zeros((rows, LANES), F32), unroll=2)

    first = slice(LANES, 2 * LANES)
    final = slice(blocks * LANES, (blocks + 1) * LANES)
    east_s[0:rows, :] = V[0, 8:top, final]
    east_s[rows : 2 * rows, :] = D[8:top, final]
    east_s[2 * rows : 3 * rows, :] = east_last
    west_s[0:rows, :] = V[0, 8:top, first]
    west_s[rows : 2 * rows, :] = D[8:top, first]
    east = remote(east_s, east_r, sem_l.at[0], sem_l.at[1], (lon_at(1), lat))
    west = remote(west_s, west_r, sem_l.at[2], sem_l.at[3], (lon_at(n - 1), lat))
    east.start()
    west.start()
    east.wait_recv()
    halo_w = slice(0, LANES)
    halo_e = slice((blocks + 1) * LANES, (blocks + 2) * LANES)
    V[0, 8:top, halo_w] = east_r[0:rows, :]
    D[8:top, halo_w] = east_r[rows : 2 * rows, :]
    V[0, 8:top, first] = V[0, 8:top, first] + jnp.where(lane == 0, east_r[2 * rows : 3 * rows, :], 0.0)
    west.wait_recv()
    V[0, 8:top, halo_e] = west_r[0:rows, :] + jnp.where(lane == 0, east_last, 0.0)
    D[8:top, halo_e] = west_r[rows : 2 * rows, :]

    lat_up_s[0:4, :] = D[top - 4 : top, :]
    lat_up_s[4:8, :] = V[0, top - 4 : top, :]
    lat_dn_s[0:4, :] = V[0, 8:12, :]
    lat_dn_s[4:8, :] = D[8:12, :]

    def rows_up():
        return remote(lat_up_s, lat_up_r, sem_t.at[0], sem_t.at[1], (lon, lat_at(1)))

    def rows_dn():
        return remote(lat_dn_s, lat_dn_r, sem_t.at[2], sem_t.at[3], (lon, lat_at(lats - 1)))

    @pl.when(lat < lats - 1)
    def _():
        rows_up().start()

    @pl.when(lat > 0)
    def _():
        rows_dn().start()

    def mirror(k):
        @pl.when(lat == 0)
        def _():
            V[k, 7:8, :] = V[k, 8:9, :]

        @pl.when(lat == lats - 1)
        def _():
            V[k, top : top + 1, :] = V[k, top - 1 : top, :]

    @pl.when(lat > 0)
    def _():
        rows_up().wait_recv()
        got = lat_up_r[...]
        V[0, 0:8, :] = got
        D[0:8, :] = pltpu.roll(got, 4, 0)

    @pl.when(lat == 0)
    def _():
        V[0, 0:8, :] = jnp.zeros((8, ext * LANES), F32)
        D[0:8, :] = jnp.zeros((8, ext * LANES), F32)

    @pl.when(lat < lats - 1)
    def _():
        rows_dn().wait_recv()
        got = lat_dn_r[...]
        V[0, top : top + 8, :] = got
        D[top : top + 8, :] = pltpu.roll(got, 4, 0)

    @pl.when(lat == lats - 1)
    def _():
        V[0, top : top + 8, :] = jnp.zeros((8, ext * LANES), F32)
        D[top : top + 8, :] = jnp.zeros((8, ext * LANES), F32)

    mirror(0)

    tall = rows + 16
    lane_t = lax.broadcasted_iota(jnp.int32, (tall, LANES), 1)

    def at_block(b):
        return pl.ds(pl.multiple_of(b * LANES, LANES), LANES)

    def fold(value):
        total = value[0:8]
        for i in range(1, rows // 8):
            total = total + value[8 * i : 8 * i + 8]
        return total

    def apply(k):
        def one(b, here, before, ahead):
            nxt = V[k, :, at_block(jnp.minimum(b + 1, ext - 1))]
            ahead_next = pltpu.roll(nxt, LANES - 1, 1)
            rolled = pltpu.roll(here, 1, 1)
            sides = jnp.where(lane_t == 0, before, rolled)
            sides = sides + jnp.where(lane_t == LANES - 1, ahead_next, ahead)
            sides = sides + pltpu.roll(here, 1, 0) + pltpu.roll(here, tall - 1, 0)
            out = D[:, at_block(b)] * here - inv * sides
            V[k + 1, :, at_block(b)] = out
            return out, nxt, rolled, ahead_next

        def step(b, carry):
            here, before, ahead, cross, own, base = carry
            out, nxt, rolled, ahead_next = one(b, here, before, ahead)
            mine, image = here[8:top], out[8:top]
            cross = cross + fold(mine * image)
            own = own + fold(image * image)
            if k == 0:
                base = base + fold(mine * mine)
            return nxt, rolled, ahead_next, cross, own, base

        here = V[k, :, 0:LANES]
        ahead = pltpu.roll(here, LANES - 1, 1)
        _, here, before, ahead = one(0, here, ahead, ahead)
        zero = jnp.zeros((8, LANES), F32)
        here, before, ahead, cross, own, base = lax.fori_loop(
            1, blocks + 1, step, (here, before, ahead, zero, zero, zero), unroll=2
        )
        if k < ITERS - 1:
            one(ext - 1, here, before, ahead)
            mirror(k + 1)
        return cross, own, base

    sums = []
    for k in range(ITERS):
        cross, own, base = apply(k)
        if k == 0:
            sums.append(base)
        sums += [cross, own]

    red[...] = jnp.zeros_like(red)
    for i, value in enumerate(sums):
        red[i : i + 1, :] = jnp.sum(value, axis=0, keepdims=True)

    def over_lat(k):
        return remote(red, ra.at[lat], sem_a.at[0, k], sem_a.at[1, k], (lon, lat_at(k)))

    def over_lon(k):
        return remote(red, rb.at[lon], sem_b.at[0, k], sem_b.at[1, k], (lon_at(k), lat))

    @pl.loop(1, lats)
    def _(k):
        over_lat(k).start()

    ra[lat] = red[...]

    @pl.loop(1, lats)
    def _(k):
        over_lat(k).wait()

    total = ra[0]
    for i in range(1, lats):
        total = total + ra[i]
    red[...] = total

    @pl.loop(1, n)
    def _(k):
        over_lon(k).start()

    rb[lon] = red[...]

    @pl.loop(1, n)
    def _(k):
        over_lon(k).wait()

    total = rb[0]
    for i in range(1, n):
        total = total + rb[i]

    mu = [
        jnp.broadcast_to(jnp.sum(total[i : i + 1, :], axis=1, keepdims=True), (8, LANES))
        for i in range(2 * ITERS + 1)
    ]
    field, residual = cg_coefficients(mu)
    field = [jnp.concatenate([c] * (rows // 8), axis=0) for c in field]
    residual = [jnp.concatenate([c] * (rows // 8), axis=0) for c in residual]

    def combine(b, carry):
        cols = at_block(b + 1)
        v = V[0, 8:top, cols]
        x, r = field[0] * v, residual[0] * v
        for k in range(1, ITERS + 1):
            v = V[k, 8:top, cols]
            r = r + residual[k] * v
            if k < ITERS:
                x = x + field[k] * v
        x_ref[:, at_block(b)] = x
        r_ref[:, at_block(b)] = r
        return carry

    lax.fori_loop(0, blocks, combine, 0, unroll=2)

    @pl.loop(1, n)
    def _(k):
        meta(k).wait_send()
        heights(k).wait_send()
        weights(k).wait_send()

    east.wait_send()
    west.wait_send()

    @pl.when(lat < lats - 1)
    def _():
        edge_up().wait_send()
        rows_up().wait_send()

    @pl.when(lat > 0)
    def _():
        edge_dn().wait_send()
        rows_dn().wait_send()


def body(n, lats, piece_height, piece_weight, piece_column, piece_width):
    pieces, rows, width = piece_height.shape
    ext = COLS_DEV + 2 * LANES
    vmem = pltpu.VMEM
    dma = pltpu.SemaphoreType.DMA
    scratch = [
        vmem((n, 2 * rows, LANES), F32),
        vmem((n, 2 * rows + 8, LANES), F32),
        vmem((n, 2 * rows, LANES), F32),
        vmem((n, 2 * rows + 8, LANES), F32),
        vmem((n, 1, LANES), jnp.int32),
        vmem((n, 1, LANES), jnp.int32),
        pltpu.SMEM((n, 1, LANES), jnp.int32),
        pltpu.SMEM((n, 4), jnp.int32),
        vmem((2, pieces, LANES), F32),
        vmem((2, pieces, LANES), F32),
        vmem((pieces, LANES), F32),
        vmem((pieces, LANES), F32),
        pltpu.SMEM((2 * n,), jnp.int32),
        pltpu.SMEM((2 * n,), jnp.int32),
        vmem((1, LANES), jnp.int32),
        pltpu.SMEM((1, LANES), jnp.int32),
        vmem((2 * n + 1, 6 * rows + 8, LANES), F32),
        vmem((ITERS + 1, rows + 16, ext), F32),
        vmem((rows + 16, ext), F32),
        vmem((3 * rows, LANES), F32),
        vmem((3 * rows, LANES), F32),
        vmem((2 * rows, LANES), F32),
        vmem((2 * rows, LANES), F32),
        vmem((8, ext), F32),
        vmem((8, ext), F32),
        vmem((8, ext), F32),
        vmem((8, ext), F32),
        vmem((16, LANES), F32),
        vmem((lats, 16, LANES), F32),
        vmem((n, 16, LANES), F32),
        dma((2, n)),
        dma((2, n)),
        dma((2, n)),
        dma((4,)),
        dma((4,)),
        dma((4,)),
        dma((2, lats)),
        dma((2, n)),
        dma((2,)),
    ]
    out = jax.ShapeDtypeStruct((rows, COLS_DEV), F32)
    return pl.pallas_call(
        functools.partial(kernel, n, lats, pieces, rows),
        out_shape=(out, out),
        in_specs=[pl.BlockSpec(memory_space=pltpu.SMEM)] * 2 + [pl.BlockSpec(memory_space=pltpu.VMEM)] * 2,
        out_specs=(pl.BlockSpec(memory_space=pltpu.VMEM),) * 2,
        scratch_shapes=scratch,
        compiler_params=pltpu.CompilerParams(
            collective_id=0, has_side_effects=True, vmem_limit_bytes=48 * 1024 * 1024
        ),
    )(piece_column, piece_width, piece_height, piece_weight)


def solution(mesh):
    return jax.shard_map(
        functools.partial(body, mesh.shape["lon"], mesh.shape["lat"]),
        mesh=mesh,
        in_specs=(P("lon", "lat", None), P("lon", "lat", None), P("lon"), P("lon")),
        out_specs=(P("lat", "lon"), P("lat", "lon")),
        check_vma=False,
    )
```

```python
import functools

import jax
import jax.numpy as jnp
from jax import lax
from jax.experimental import pallas as pl
from jax.experimental.pallas import tpu as pltpu
from jax.sharding import PartitionSpec as P

COLS_DEV = 4096
ITERS = 4
MU_DATA = 0.5
DAMPING = 0.5
RIDGE = 0.05
SHIFT = 5.0
SCALE = 5.0

LANES = 128
CHUNKS = 4
MESH = pl.DeviceIdType.MESH
F32 = jnp.float32


def remote(src, dst, send, recv, device):
    return pltpu.make_async_remote_copy(
        src_ref=src, dst_ref=dst, send_sem=send, recv_sem=recv,
        device_id=device, device_id_type=MESH,
    )


def cg_coefficients(mu):
    def inner(a, b):
        total = None
        for i, x in enumerate(a):
            for j, y in enumerate(b):
                term = x * y * mu[i + j]
                total = term if total is None else total + term
        return total

    def apply(c):
        out = [SHIFT * x for x in c] + [jnp.zeros_like(c[0])]
        for i, x in enumerate(c):
            out[i + 1] = out[i + 1] + SCALE * x
        return out

    def add_scaled(y, a, x):
        out = []
        for i in range(max(len(x), len(y))):
            if i >= len(y):
                out.append(a * x[i])
            elif i >= len(x):
                out.append(y[i])
            else:
                out.append(y[i] + a * x[i])
        return out

    one = jnp.ones_like(mu[0])
    residual, direction, field = [one], [one], []
    norm = mu[0]
    for step in range(ITERS):
        image = apply(direction)
        alpha = norm / inner(direction, image)
        field = add_scaled(field, alpha, direction)
        residual = add_scaled(residual, -alpha, image)
        if step < ITERS - 1:
            fresh = inner(residual, residual)
            direction = add_scaled(residual, fresh / norm, direction)
            norm = fresh
    return field, residual


def kernel(
    n, lats, pieces, rows,
    col_in, wid_in, h_in, w_in, V, coef_ref,
    col_ref, wid_ref, h_ref, w_ref,
    hs, ws, hr, wr, ms, mr, msm, idx_s, up_s, up_r, dn_s, dn_r,
    blk_s, prev_s, last_v, last_s, S,
    D, east_s, east_r, west_s, west_r, lat_up_s, lat_up_r, lat_dn_s, lat_dn_r,
    red, ra, rb,
    sem_m, sem_h, sem_w, sem_e, sem_l, sem_t, sem_a, sem_b, sem_loc,
):
    lon = lax.axis_index("lon")
    lat = lax.axis_index("lat")
    blocks = COLS_DEV // LANES
    ext = blocks + 2
    top = rows + 8
    slots = 2 * n
    lane = lax.broadcasted_iota(jnp.int32, (rows, LANES), 1)
    lane1 = lax.broadcasted_iota(jnp.int32, (1, LANES), 1)

    def lon_at(k):
        return lax.rem(lon + k, n)

    def lat_at(k):
        return lax.rem(lat + k, lats)

    barrier = pltpu.get_barrier_semaphore()
    loads = [
        pltpu.make_async_copy(src, dst, sem_loc.at[2 + i])
        for i, (src, dst) in enumerate(
            ((col_in, col_ref), (wid_in, wid_ref), (h_in, h_ref), (w_in, w_ref))
        )
    ]
    for load in loads:
        load.start()

    @pl.loop(1, n)
    def _(k):
        pl.semaphore_signal(barrier, inc=1, device_id=(lon_at(k), lat), device_id_type=MESH)

    @pl.loop(1, lats)
    def _(k):
        pl.semaphore_signal(barrier, inc=1, device_id=(lon, lat_at(k)), device_id_type=MESH)

    for load in loads:
        load.wait()

    @pl.loop(0, pieces)
    def _(i):
        up_s[0, pl.ds(i, 1), :] = h_ref[i, rows - 1 : rows, :]
        up_s[1, pl.ds(i, 1), :] = w_ref[i, rows - 1 : rows, :]
        dn_s[pl.ds(i, 1), :] = h_ref[i, 0:1, :]

    def fill(k, h_to, w_to, m_to):
        dest = lon_at(k)

        def scan(i, found):
            first, second = found
            match = (col_ref[i] >> 12) == dest
            second = jnp.where(match & (first >= 0) & (second < 0), i, second)
            first = jnp.where(match & (first < 0), i, first)
            return first, second

        found = lax.fori_loop(0, pieces, scan, (jnp.int32(-1), jnp.int32(-1)), unroll=8)
        tags = []
        for q in range(2):
            at = jnp.maximum(found[q], 0)
            limit = jnp.where(found[q] >= 0, wid_ref[at], 0)
            tags.append(jnp.where(found[q] >= 0, (col_ref[at] >> 7) & (blocks - 1), -1))
            idx_s[k, q] = at
            idx_s[k, 2 + q] = limit
            h_to[k, q * rows : (q + 1) * rows, :] = h_ref[at]
            w_to[k, q * rows : (q + 1) * rows, :] = jnp.where(lane < limit, w_ref[at], 0.0)
        m_to[k] = jnp.where(lane1 == 0, tags[0], jnp.where(lane1 == 1, tags[1], -1))

    fill(0, hr, wr, mr)

    @pl.loop(1, n)
    def _(k):
        fill(k, hs, ws, ms)

    pl.semaphore_wait(barrier, n - 1 + lats - 1)

    def edge_up():
        return remote(up_s, up_r, sem_e.at[0], sem_e.at[1], (lon, lat_at(1)))

    def edge_dn():
        return remote(dn_s, dn_r, sem_e.at[2], sem_e.at[3], (lon, lat_at(lats - 1)))

    def meta(k):
        return remote(ms.at[k], mr.at[k], sem_m.at[0, k], sem_m.at[1, k], (lon_at(k), lat))

    def heights(k):
        return remote(hs.at[k], hr.at[k], sem_h.at[0, k], sem_h.at[1, k], (lon_at(k), lat))

    def weights(k):
        return remote(ws.at[k], wr.at[k], sem_w.at[0, k], sem_w.at[1, k], (lon_at(k), lat))

    @pl.when(lat < lats - 1)
    def _():
        edge_up().start()

    @pl.when(lat > 0)
    def _():
        edge_dn().start()

    @pl.loop(1, n)
    def _(k):
        meta(k).start()

    @pl.loop(1, n)
    def _(k):
        heights(k).start()

    @pl.when(lat > 0)
    def _():
        edge_up().wait_recv()

    @pl.when(lat == 0)
    def _():
        up_r[...] = jnp.zeros_like(up_r)

    @pl.when(lat < lats - 1)
    def _():
        edge_dn().wait_recv()

    @pl.when(lat == lats - 1)
    def _():
        dn_r[...] = jnp.zeros_like(dn_r)

    def extras(k, w_to):
        for q in range(2):
            at, limit = idx_s[k, q], idx_s[k, 2 + q]
            base = 2 * rows + q
            w_to[k, base : base + 1, :] = dn_r[pl.ds(at, 1), :]
            w_to[k, base + 2 : base + 3, :] = up_r[0, pl.ds(at, 1), :]
            w_to[k, base + 4 : base + 5, :] = jnp.where(lane1 < limit, up_r[1, pl.ds(at, 1), :], 0.0)
        w_to[k, 2 * rows + 6 : 2 * rows + 8, :] = jnp.zeros((2, LANES), F32)

    @pl.loop(1, n)
    def _(k):
        extras(k, ws)
        weights(k).start()

    extras(0, wr)

    @pl.loop(1, n)
    def _(k):
        meta(k).wait_recv()

    tags_in = pltpu.make_async_copy(mr, msm, sem_loc.at[0])
    tags_in.start()
    tags_in.wait()

    @pl.loop(0, n)
    def _(k):
        blk_s[2 * k] = msm[k, 0, 0]
        blk_s[2 * k + 1] = msm[k, 0, 1]

    def latest(p, last):
        tag = blk_s[p]

        def scan(j, found):
            return jnp.where((j < p) & (blk_s[j] == tag), j, found)

        prev_s[p] = lax.fori_loop(0, slots, scan, jnp.int32(slots), unroll=8)
        return jnp.where(lane1 == tag, p, last)

    last_v[...] = lax.fori_loop(0, slots, latest, jnp.full((1, LANES), slots, jnp.int32))
    last_in = pltpu.make_async_copy(last_v, last_s, sem_loc.at[1])
    last_in.start()
    last_in.wait()

    S[slots] = jnp.zeros((6 * rows + 8, LANES), F32)
    row_global = lat * rows + lax.broadcasted_iota(jnp.int32, (rows, LANES), 0)
    has_north = row_global < lats * rows - 1
    row_in = lax.broadcasted_iota(jnp.int32, (rows, LANES), 0)

    def terms(k):
        for q in range(2):
            p = 2 * k + q
            before = prev_s[p]
            h = hr[k, q * rows : (q + 1) * rows, :]
            w = wr[k, q * rows : (q + 1) * rows, :]
            base = 2 * rows + q
            above = wr[k, base : base + 1, :]
            below_h = wr[k, base + 2 : base + 3, :]
            below_w = wr[k, base + 4 : base + 5, :]
            h_north = jnp.where(row_in == rows - 1, above, pltpu.roll(h, rows - 1, 0))
            h_east = pltpu.roll(h, LANES - 1, 1)
            w_east = jnp.where((pltpu.roll(w, LANES - 1, 1) > 0.0) & (lane < LANES - 1), w, 0.0)
            w_north = jnp.where(has_north, w, 0.0)
            parts = (w, w * h, w_east, w_east * (h_east - h), w_north, w_north * (h_north - h))
            for t, part in enumerate(parts):
                at = pl.ds(t * rows, rows)
                S[p, at, :] = part + S[before, at, :]
            at = 6 * rows
            S[p, at : at + 1, :] = below_w + S[before, at : at + 1, :]
            S[p, at + 1 : at + 2, :] = below_w * (h[0:1, :] - below_h) + S[before, at + 1 : at + 2, :]

    terms(0)

    @pl.loop(1, n)
    def _(k):
        heights(k).wait_recv()
        weights(k).wait_recv()
        terms(k)

    inv = 1.0 / SCALE

    def assemble(b, before):
        p = last_s[0, b]

        def field(t):
            return S[p, t * rows : (t + 1) * rows, :]

        at = 6 * rows
        t_east = field(3) / (field(2) + DAMPING)
        t_north = field(5) / (field(4) + DAMPING)
        t_below = S[p, at + 1 : at + 2, :] / (S[p, at : at + 1, :] + DAMPING)
        t_south = jnp.where(row_in == 0, t_below, pltpu.roll(t_north, 1, 0))
        rolled = pltpu.roll(t_east, 1, 1)
        t_west = jnp.where(lane == 0, before, rolled)
        right = MU_DATA * field(1) - (t_east - t_west) - (t_north - t_south)
        cols = pl.ds(pl.multiple_of((b + 1) * LANES, LANES), LANES)
        V[0, 8:top, cols] = right
        D[8:top, cols] = (MU_DATA * field(0) + (RIDGE + 4.0 - SHIFT)) * inv
        return rolled

    east_last = lax.fori_loop(0, blocks, assemble, jnp.zeros((rows, LANES), F32), unroll=2)

    first = slice(LANES, 2 * LANES)
    final = slice(blocks * LANES, (blocks + 1) * LANES)
    east_s[0:rows, :] = V[0, 8:top, final]
    east_s[rows : 2 * rows, :] = D[8:top, final]
    east_s[2 * rows : 3 * rows, :] = east_last
    west_s[0:rows, :] = V[0, 8:top, first]
    west_s[rows : 2 * rows, :] = D[8:top, first]
    east = remote(east_s, east_r, sem_l.at[0], sem_l.at[1], (lon_at(1), lat))
    west = remote(west_s, west_r, sem_l.at[2], sem_l.at[3], (lon_at(n - 1), lat))
    east.start()
    west.start()
    east.wait_recv()
    halo_w = slice(0, LANES)
    halo_e = slice((blocks + 1) * LANES, (blocks + 2) * LANES)
    V[0, 8:top, halo_w] = east_r[0:rows, :]
    D[8:top, halo_w] = east_r[rows : 2 * rows, :]
    V[0, 8:top, first] = V[0, 8:top, first] + jnp.where(lane == 0, east_r[2 * rows : 3 * rows, :], 0.0)
    west.wait_recv()
    V[0, 8:top, halo_e] = west_r[0:rows, :] + jnp.where(lane == 0, east_last, 0.0)
    D[8:top, halo_e] = west_r[rows : 2 * rows, :]

    lat_up_s[0:4, :] = D[top - 4 : top, :]
    lat_up_s[4:8, :] = V[0, top - 4 : top, :]
    lat_dn_s[0:4, :] = V[0, 8:12, :]
    lat_dn_s[4:8, :] = D[8:12, :]

    def rows_up():
        return remote(lat_up_s, lat_up_r, sem_t.at[0], sem_t.at[1], (lon, lat_at(1)))

    def rows_dn():
        return remote(lat_dn_s, lat_dn_r, sem_t.at[2], sem_t.at[3], (lon, lat_at(lats - 1)))

    @pl.when(lat < lats - 1)
    def _():
        rows_up().start()

    @pl.when(lat > 0)
    def _():
        rows_dn().start()

    def mirror(k):
        @pl.when(lat == 0)
        def _():
            V[k, 7:8, :] = V[k, 8:9, :]

        @pl.when(lat == lats - 1)
        def _():
            V[k, top : top + 1, :] = V[k, top - 1 : top, :]

    @pl.when(lat > 0)
    def _():
        rows_up().wait_recv()
        got = lat_up_r[...]
        V[0, 0:8, :] = got
        D[0:8, :] = pltpu.roll(got, 4, 0)

    @pl.when(lat == 0)
    def _():
        V[0, 0:8, :] = jnp.zeros((8, ext * LANES), F32)
        D[0:8, :] = jnp.zeros((8, ext * LANES), F32)

    @pl.when(lat < lats - 1)
    def _():
        rows_dn().wait_recv()
        got = lat_dn_r[...]
        V[0, top : top + 8, :] = got
        D[top : top + 8, :] = pltpu.roll(got, 4, 0)

    @pl.when(lat == lats - 1)
    def _():
        V[0, top : top + 8, :] = jnp.zeros((8, ext * LANES), F32)
        D[top : top + 8, :] = jnp.zeros((8, ext * LANES), F32)

    mirror(0)

    tall = rows + 16
    lane_t = lax.broadcasted_iota(jnp.int32, (tall, LANES), 1)

    def at_block(b):
        return pl.ds(pl.multiple_of(b * LANES, LANES), LANES)

    def fold(value):
        total = value[0:8]
        for i in range(1, rows // 8):
            total = total + value[8 * i : 8 * i + 8]
        return total

    def apply(k):
        def one(b, here, before, ahead):
            nxt = V[k, :, at_block(jnp.minimum(b + 1, ext - 1))]
            ahead_next = pltpu.roll(nxt, LANES - 1, 1)
            rolled = pltpu.roll(here, 1, 1)
            sides = jnp.where(lane_t == 0, before, rolled)
            sides = sides + jnp.where(lane_t == LANES - 1, ahead_next, ahead)
            sides = sides + pltpu.roll(here, 1, 0) + pltpu.roll(here, tall - 1, 0)
            out = D[:, at_block(b)] * here - inv * sides
            V[k + 1, :, at_block(b)] = out
            return out, nxt, rolled, ahead_next

        def step(b, carry):
            here, before, ahead, cross, own, base = carry
            out, nxt, rolled, ahead_next = one(b, here, before, ahead)
            mine, image = here[8:top], out[8:top]
            cross = cross + fold(mine * image)
            own = own + fold(image * image)
            if k == 0:
                base = base + fold(mine * mine)
            return nxt, rolled, ahead_next, cross, own, base

        here = V[k, :, 0:LANES]
        ahead = pltpu.roll(here, LANES - 1, 1)
        _, here, before, ahead = one(0, here, ahead, ahead)
        zero = jnp.zeros((8, LANES), F32)
        here, before, ahead, cross, own, base = lax.fori_loop(
            1, blocks + 1, step, (here, before, ahead, zero, zero, zero), unroll=2
        )
        if k < ITERS - 1:
            one(ext - 1, here, before, ahead)
            mirror(k + 1)
        return cross, own, base

    sums = []
    for k in range(ITERS):
        cross, own, base = apply(k)
        if k == 0:
            sums.append(base)
        sums += [cross, own]

    red[...] = jnp.zeros_like(red)
    for i, value in enumerate(sums):
        red[i : i + 1, :] = jnp.sum(value, axis=0, keepdims=True)

    def over_lat(k):
        return remote(red, ra.at[lat], sem_a.at[0, k], sem_a.at[1, k], (lon, lat_at(k)))

    def over_lon(k):
        return remote(red, rb.at[lon], sem_b.at[0, k], sem_b.at[1, k], (lon_at(k), lat))

    @pl.loop(1, lats)
    def _(k):
        over_lat(k).start()

    ra[lat] = red[...]

    @pl.loop(1, lats)
    def _(k):
        over_lat(k).wait()

    total = ra[0]
    for i in range(1, lats):
        total = total + ra[i]
    red[...] = total

    @pl.loop(1, n)
    def _(k):
        over_lon(k).start()

    rb[lon] = red[...]

    @pl.loop(1, n)
    def _(k):
        over_lon(k).wait()

    total = rb[0]
    for i in range(1, n):
        total = total + rb[i]

    mu = [
        jnp.broadcast_to(jnp.sum(total[i : i + 1, :], axis=1, keepdims=True), (8, LANES))
        for i in range(2 * ITERS + 1)
    ]
    field, residual = cg_coefficients(mu)
    for i, c in enumerate(field + residual):
        coef_ref[i : i + 1, :] = c[0:1, :]

    @pl.loop(1, n)
    def _(k):
        meta(k).wait_send()
        heights(k).wait_send()
        weights(k).wait_send()

    east.wait_send()
    west.wait_send()

    @pl.when(lat < lats - 1)
    def _():
        edge_up().wait_send()
        rows_up().wait_send()

    @pl.when(lat > 0)
    def _():
        edge_dn().wait_send()
        rows_dn().wait_send()


def combine(rows, V, coef_ref, x_out, r_out, x_ref, r_ref, sem):
    coef = [coef_ref[i : i + 1, :] for i in range(2 * ITERS + 1)]
    coef = [jnp.broadcast_to(c, (rows, LANES)) for c in coef]
    field, residual = coef[:ITERS], coef[ITERS:]
    width = COLS_DEV // CHUNKS

    def copies(c):
        cols = pl.ds(c * width, width)
        return (
            pltpu.make_async_copy(x_ref.at[:, cols], x_out.at[:, cols], sem.at[0, c]),
            pltpu.make_async_copy(r_ref.at[:, cols], r_out.at[:, cols], sem.at[1, c]),
        )

    for c in range(CHUNKS):

        def one(b, carry):
            v = V[0, 8 : rows + 8, pl.ds(pl.multiple_of((b + 1) * LANES, LANES), LANES)]
            x, r = field[0] * v, residual[0] * v
            for k in range(1, ITERS + 1):
                v = V[k, 8 : rows + 8, pl.ds(pl.multiple_of((b + 1) * LANES, LANES), LANES)]
                r = r + residual[k] * v
                if k < ITERS:
                    x = x + field[k] * v
            cols = pl.ds(pl.multiple_of(b * LANES, LANES), LANES)
            x_ref[:, cols] = x
            r_ref[:, cols] = r
            return carry

        per = width // LANES
        lax.fori_loop(c * per, (c + 1) * per, one, 0, unroll=4)
        for copy in copies(c):
            copy.start()
    for c in range(CHUNKS):
        for copy in copies(c):
            copy.wait()


def body(n, lats, piece_height, piece_weight, piece_column, piece_width):
    pieces, rows, width = piece_height.shape
    ext = COLS_DEV + 2 * LANES
    vmem = pltpu.VMEM
    dma = pltpu.SemaphoreType.DMA
    scratch = [
        pltpu.SMEM((pieces,), jnp.int32),
        pltpu.SMEM((pieces,), jnp.int32),
        vmem((pieces, rows, LANES), F32),
        vmem((pieces, rows, LANES), F32),
        vmem((n, 2 * rows, LANES), F32),
        vmem((n, 2 * rows + 8, LANES), F32),
        vmem((n, 2 * rows, LANES), F32),
        vmem((n, 2 * rows + 8, LANES), F32),
        vmem((n, 1, LANES), jnp.int32),
        vmem((n, 1, LANES), jnp.int32),
        pltpu.SMEM((n, 1, LANES), jnp.int32),
        pltpu.SMEM((n, 4), jnp.int32),
        vmem((2, pieces, LANES), F32),
        vmem((2, pieces, LANES), F32),
        vmem((pieces, LANES), F32),
        vmem((pieces, LANES), F32),
        pltpu.SMEM((2 * n,), jnp.int32),
        pltpu.SMEM((2 * n,), jnp.int32),
        vmem((1, LANES), jnp.int32),
        pltpu.SMEM((1, LANES), jnp.int32),
        vmem((2 * n + 1, 6 * rows + 8, LANES), F32),
        vmem((rows + 16, ext), F32),
        vmem((3 * rows, LANES), F32),
        vmem((3 * rows, LANES), F32),
        vmem((2 * rows, LANES), F32),
        vmem((2 * rows, LANES), F32),
        vmem((8, ext), F32),
        vmem((8, ext), F32),
        vmem((8, ext), F32),
        vmem((8, ext), F32),
        vmem((16, LANES), F32),
        vmem((lats, 16, LANES), F32),
        vmem((n, 16, LANES), F32),
        dma((2, n)),
        dma((2, n)),
        dma((2, n)),
        dma((4,)),
        dma((4,)),
        dma((4,)),
        dma((2, lats)),
        dma((2, n)),
        dma((6,)),
    ]
    basis, coef = pl.pallas_call(
        functools.partial(kernel, n, lats, pieces, rows),
        out_shape=(
            jax.ShapeDtypeStruct((ITERS + 1, rows + 16, ext), F32),
            jax.ShapeDtypeStruct((16, LANES), F32),
        ),
        in_specs=[pl.BlockSpec(memory_space=pltpu.HBM)] * 4,
        out_specs=(pl.BlockSpec(memory_space=pltpu.VMEM),) * 2,
        scratch_shapes=scratch,
        compiler_params=pltpu.CompilerParams(
            collective_id=0, has_side_effects=True, vmem_limit_bytes=48 * 1024 * 1024
        ),
    )(*(pltpu.with_memory_space_constraint(a, pltpu.HBM) for a in (piece_column, piece_width, piece_height, piece_weight)))
    out = jax.ShapeDtypeStruct((rows, COLS_DEV), F32)
    return pl.pallas_call(
        functools.partial(combine, rows),
        out_shape=(out, out),
        in_specs=[pl.BlockSpec(memory_space=pltpu.VMEM)] * 2,
        out_specs=(pl.BlockSpec(memory_space=pltpu.HBM),) * 2,
        scratch_shapes=[
            vmem((rows, COLS_DEV), F32),
            vmem((rows, COLS_DEV), F32),
            dma((2, CHUNKS)),
        ],
        compiler_params=pltpu.CompilerParams(vmem_limit_bytes=16 * 1024 * 1024),
    )(basis, coef)


def solution(mesh):
    return jax.shard_map(
        functools.partial(body, mesh.shape["lon"], mesh.shape["lat"]),
        mesh=mesh,
        in_specs=(P("lon", "lat", None), P("lon", "lat", None), P("lon"), P("lon")),
        out_specs=(P("lat", "lon"), P("lat", "lon")),
        check_vma=False,
    )
```

```python
import functools

import jax
import jax.numpy as jnp
from jax import lax
from jax.experimental import pallas as pl
from jax.experimental.pallas import tpu as pltpu
from jax.sharding import PartitionSpec as P

COLS_DEV = 4096
ITERS = 4
MU_DATA = 0.5
DAMPING = 0.5
RIDGE = 0.05
SHIFT = 5.0
SCALE = 5.0

LANES = 128
CHUNKS = 4
MESH = pl.DeviceIdType.MESH
F32 = jnp.float32


def remote(src, dst, send, recv, device):
    return pltpu.make_async_remote_copy(
        src_ref=src, dst_ref=dst, send_sem=send, recv_sem=recv,
        device_id=device, device_id_type=MESH,
    )


def cg_coefficients(mu):
    def inner(a, b):
        total = None
        for i, x in enumerate(a):
            for j, y in enumerate(b):
                term = x * y * mu[i + j]
                total = term if total is None else total + term
        return total

    def apply(c):
        out = [SHIFT * x for x in c] + [jnp.zeros_like(c[0])]
        for i, x in enumerate(c):
            out[i + 1] = out[i + 1] + SCALE * x
        return out

    def add_scaled(y, a, x):
        out = []
        for i in range(max(len(x), len(y))):
            if i >= len(y):
                out.append(a * x[i])
            elif i >= len(x):
                out.append(y[i])
            else:
                out.append(y[i] + a * x[i])
        return out

    one = jnp.ones_like(mu[0])
    residual, direction, field = [one], [one], []
    norm = mu[0]
    for step in range(ITERS):
        image = apply(direction)
        alpha = norm / inner(direction, image)
        field = add_scaled(field, alpha, direction)
        residual = add_scaled(residual, -alpha, image)
        if step < ITERS - 1:
            fresh = inner(residual, residual)
            direction = add_scaled(residual, fresh / norm, direction)
            norm = fresh
    return field, residual


def kernel(
    n, lats, pieces, rows,
    col_in, wid_in, h_in, w_in, V, coef_ref,
    col_ref, wid_ref, h_ref, w_ref,
    hs, ws, hr, wr, ms, mr, msm, idx_s, up_s, up_r, dn_s, dn_r,
    blk_s, prev_s, last_v, last_s, S,
    D, east_s, east_r, west_s, west_r, lat_up_s, lat_up_r, lat_dn_s, lat_dn_r,
    red, ra, rb,
    sem_m, sem_h, sem_w, sem_e, sem_l, sem_t, sem_a, sem_b, sem_loc,
):
    lon = lax.axis_index("lon")
    lat = lax.axis_index("lat")
    blocks = COLS_DEV // LANES
    ext = blocks + 2
    top = rows + 8
    slots = 2 * n
    lane = lax.broadcasted_iota(jnp.int32, (rows, LANES), 1)
    lane1 = lax.broadcasted_iota(jnp.int32, (1, LANES), 1)

    def lon_at(k):
        return lax.rem(lon + k, n)

    def partner(k):
        other, bit = jnp.int32(0), 1
        while bit < n:
            other = other + (lon // bit + k // bit) % 2 * bit
            bit *= 2
        return other

    def lat_at(k):
        return lax.rem(lat + k, lats)

    barrier = pltpu.get_barrier_semaphore()
    loads = [
        pltpu.make_async_copy(src, dst, sem_loc.at[2 + i])
        for i, (src, dst) in enumerate(
            ((col_in, col_ref), (wid_in, wid_ref), (h_in, h_ref), (w_in, w_ref))
        )
    ]
    for load in loads:
        load.start()

    @pl.loop(1, n)
    def _(k):
        pl.semaphore_signal(barrier, inc=1, device_id=(partner(k), lat), device_id_type=MESH)

    @pl.loop(1, lats)
    def _(k):
        pl.semaphore_signal(barrier, inc=1, device_id=(lon, lat_at(k)), device_id_type=MESH)

    for load in loads:
        load.wait()

    @pl.loop(0, pieces)
    def _(i):
        up_s[0, pl.ds(i, 1), :] = h_ref[i, rows - 1 : rows, :]
        up_s[1, pl.ds(i, 1), :] = w_ref[i, rows - 1 : rows, :]
        dn_s[pl.ds(i, 1), :] = h_ref[i, 0:1, :]

    def fill(k, h_to, w_to, m_to):
        dest = partner(k)

        def scan(i, found):
            first, second = found
            match = (col_ref[i] >> 12) == dest
            second = jnp.where(match & (first >= 0) & (second < 0), i, second)
            first = jnp.where(match & (first < 0), i, first)
            return first, second

        found = lax.fori_loop(0, pieces, scan, (jnp.int32(-1), jnp.int32(-1)), unroll=8)
        tags = []
        for q in range(2):
            at = jnp.maximum(found[q], 0)
            limit = jnp.where(found[q] >= 0, wid_ref[at], 0)
            tags.append(jnp.where(found[q] >= 0, (col_ref[at] >> 7) & (blocks - 1), -1))
            idx_s[k, q] = at
            idx_s[k, 2 + q] = limit
            h_to[k, q * rows : (q + 1) * rows, :] = h_ref[at]
            w_to[k, q * rows : (q + 1) * rows, :] = jnp.where(lane < limit, w_ref[at], 0.0)
        m_to[k] = jnp.where(lane1 == 0, tags[0], jnp.where(lane1 == 1, tags[1], -1))

    fill(0, hr, wr, mr)

    @pl.loop(1, n)
    def _(k):
        fill(n - k, hs, ws, ms)

    pl.semaphore_wait(barrier, n - 1 + lats - 1)

    def edge_up():
        return remote(up_s, up_r, sem_e.at[0], sem_e.at[1], (lon, lat_at(1)))

    def edge_dn():
        return remote(dn_s, dn_r, sem_e.at[2], sem_e.at[3], (lon, lat_at(lats - 1)))

    def meta(k):
        return remote(ms.at[k], mr.at[k], sem_m.at[0, k], sem_m.at[1, k], (partner(k), lat))

    def heights(k):
        return remote(hs.at[k], hr.at[k], sem_h.at[0, k], sem_h.at[1, k], (partner(k), lat))

    def weights(k):
        return remote(ws.at[k], wr.at[k], sem_w.at[0, k], sem_w.at[1, k], (partner(k), lat))

    @pl.when(lat < lats - 1)
    def _():
        edge_up().start()

    @pl.when(lat > 0)
    def _():
        edge_dn().start()

    @pl.loop(1, n)
    def _(k):
        meta(k).start()

    @pl.loop(1, n)
    def _(k):
        heights(n - k).start()

    @pl.when(lat > 0)
    def _():
        edge_up().wait_recv()

    @pl.when(lat == 0)
    def _():
        up_r[...] = jnp.zeros_like(up_r)

    @pl.when(lat < lats - 1)
    def _():
        edge_dn().wait_recv()

    @pl.when(lat == lats - 1)
    def _():
        dn_r[...] = jnp.zeros_like(dn_r)

    def extras(k, w_to):
        for q in range(2):
            at, limit = idx_s[k, q], idx_s[k, 2 + q]
            base = 2 * rows + q
            w_to[k, base : base + 1, :] = dn_r[pl.ds(at, 1), :]
            w_to[k, base + 2 : base + 3, :] = up_r[0, pl.ds(at, 1), :]
            w_to[k, base + 4 : base + 5, :] = jnp.where(lane1 < limit, up_r[1, pl.ds(at, 1), :], 0.0)
        w_to[k, 2 * rows + 6 : 2 * rows + 8, :] = jnp.zeros((2, LANES), F32)

    @pl.loop(1, n)
    def _(k):
        extras(n - k, ws)
        weights(n - k).start()

    extras(0, wr)

    @pl.loop(1, n)
    def _(k):
        meta(k).wait_recv()

    tags_in = pltpu.make_async_copy(mr, msm, sem_loc.at[0])
    tags_in.start()
    tags_in.wait()

    @pl.loop(0, n)
    def _(k):
        blk_s[2 * k] = msm[k, 0, 0]
        blk_s[2 * k + 1] = msm[k, 0, 1]

    def latest(p, last):
        tag = blk_s[p]

        def scan(j, found):
            return jnp.where((j < p) & (blk_s[j] == tag), j, found)

        prev_s[p] = lax.fori_loop(0, slots, scan, jnp.int32(slots), unroll=8)
        return jnp.where(lane1 == tag, p, last)

    last_v[...] = lax.fori_loop(0, slots, latest, jnp.full((1, LANES), slots, jnp.int32))
    last_in = pltpu.make_async_copy(last_v, last_s, sem_loc.at[1])
    last_in.start()
    last_in.wait()

    S[slots] = jnp.zeros((6 * rows + 8, LANES), F32)
    row_global = lat * rows + lax.broadcasted_iota(jnp.int32, (rows, LANES), 0)
    has_north = row_global < lats * rows - 1
    row_in = lax.broadcasted_iota(jnp.int32, (rows, LANES), 0)

    def terms(k):
        for q in range(2):
            p = 2 * k + q
            before = prev_s[p]
            h = hr[k, q * rows : (q + 1) * rows, :]
            w = wr[k, q * rows : (q + 1) * rows, :]
            base = 2 * rows + q
            above = wr[k, base : base + 1, :]
            below_h = wr[k, base + 2 : base + 3, :]
            below_w = wr[k, base + 4 : base + 5, :]
            h_north = jnp.where(row_in == rows - 1, above, pltpu.roll(h, rows - 1, 0))
            h_east = pltpu.roll(h, LANES - 1, 1)
            w_east = jnp.where((pltpu.roll(w, LANES - 1, 1) > 0.0) & (lane < LANES - 1), w, 0.0)
            w_north = jnp.where(has_north, w, 0.0)
            parts = (w, w * h, w_east, w_east * (h_east - h), w_north, w_north * (h_north - h))
            for t, part in enumerate(parts):
                at = pl.ds(t * rows, rows)
                S[p, at, :] = part + S[before, at, :]
            at = 6 * rows
            S[p, at : at + 1, :] = below_w + S[before, at : at + 1, :]
            S[p, at + 1 : at + 2, :] = below_w * (h[0:1, :] - below_h) + S[before, at + 1 : at + 2, :]

    terms(0)

    @pl.loop(1, n)
    def _(k):
        heights(k).wait_recv()
        weights(k).wait_recv()
        terms(k)

    inv = 1.0 / SCALE

    def assemble(b, before):
        p = last_s[0, b]

        def field(t):
            return S[p, t * rows : (t + 1) * rows, :]

        at = 6 * rows
        t_east = field(3) / (field(2) + DAMPING)
        t_north = field(5) / (field(4) + DAMPING)
        t_below = S[p, at + 1 : at + 2, :] / (S[p, at : at + 1, :] + DAMPING)
        t_south = jnp.where(row_in == 0, t_below, pltpu.roll(t_north, 1, 0))
        rolled = pltpu.roll(t_east, 1, 1)
        t_west = jnp.where(lane == 0, before, rolled)
        right = MU_DATA * field(1) - (t_east - t_west) - (t_north - t_south)
        cols = pl.ds(pl.multiple_of((b + 1) * LANES, LANES), LANES)
        V[0, 8:top, cols] = right
        D[8:top, cols] = (MU_DATA * field(0) + (RIDGE + 4.0 - SHIFT)) * inv
        return rolled

    east_last = lax.fori_loop(0, blocks, assemble, jnp.zeros((rows, LANES), F32), unroll=8)

    first = slice(LANES, 2 * LANES)
    final = slice(blocks * LANES, (blocks + 1) * LANES)
    east_s[0:rows, :] = V[0, 8:top, final]
    east_s[rows : 2 * rows, :] = D[8:top, final]
    east_s[2 * rows : 3 * rows, :] = east_last
    west_s[0:rows, :] = V[0, 8:top, first]
    west_s[rows : 2 * rows, :] = D[8:top, first]
    east = remote(east_s, east_r, sem_l.at[0], sem_l.at[1], (lon_at(1), lat))
    west = remote(west_s, west_r, sem_l.at[2], sem_l.at[3], (lon_at(n - 1), lat))
    east.start()
    west.start()
    east.wait_recv()
    halo_w = slice(0, LANES)
    halo_e = slice((blocks + 1) * LANES, (blocks + 2) * LANES)
    V[0, 8:top, halo_w] = east_r[0:rows, :]
    D[8:top, halo_w] = east_r[rows : 2 * rows, :]
    V[0, 8:top, first] = V[0, 8:top, first] + jnp.where(lane == 0, east_r[2 * rows : 3 * rows, :], 0.0)
    west.wait_recv()
    V[0, 8:top, halo_e] = west_r[0:rows, :] + jnp.where(lane == 0, east_last, 0.0)
    D[8:top, halo_e] = west_r[rows : 2 * rows, :]

    lat_up_s[0:4, :] = D[top - 4 : top, :]
    lat_up_s[4:8, :] = V[0, top - 4 : top, :]
    lat_dn_s[0:4, :] = V[0, 8:12, :]
    lat_dn_s[4:8, :] = D[8:12, :]

    def rows_up():
        return remote(lat_up_s, lat_up_r, sem_t.at[0], sem_t.at[1], (lon, lat_at(1)))

    def rows_dn():
        return remote(lat_dn_s, lat_dn_r, sem_t.at[2], sem_t.at[3], (lon, lat_at(lats - 1)))

    @pl.when(lat < lats - 1)
    def _():
        rows_up().start()

    @pl.when(lat > 0)
    def _():
        rows_dn().start()

    def mirror(k):
        @pl.when(lat == 0)
        def _():
            V[k, 7:8, :] = V[k, 8:9, :]

        @pl.when(lat == lats - 1)
        def _():
            V[k, top : top + 1, :] = V[k, top - 1 : top, :]

    @pl.when(lat > 0)
    def _():
        rows_up().wait_recv()
        got = lat_up_r[...]
        V[0, 0:8, :] = got
        D[0:8, :] = pltpu.roll(got, 4, 0)

    @pl.when(lat == 0)
    def _():
        V[0, 0:8, :] = jnp.zeros((8, ext * LANES), F32)
        D[0:8, :] = jnp.zeros((8, ext * LANES), F32)

    @pl.when(lat < lats - 1)
    def _():
        rows_dn().wait_recv()
        got = lat_dn_r[...]
        V[0, top : top + 8, :] = got
        D[top : top + 8, :] = pltpu.roll(got, 4, 0)

    @pl.when(lat == lats - 1)
    def _():
        V[0, top : top + 8, :] = jnp.zeros((8, ext * LANES), F32)
        D[top : top + 8, :] = jnp.zeros((8, ext * LANES), F32)

    mirror(0)

    tall = rows + 16
    lane_t = lax.broadcasted_iota(jnp.int32, (tall, LANES), 1)

    def at_block(b):
        return pl.ds(pl.multiple_of(b * LANES, LANES), LANES)

    def fold(value):
        total = value[0:8]
        for i in range(1, rows // 8):
            total = total + value[8 * i : 8 * i + 8]
        return total

    def apply(k):
        def one(b, here, before, ahead):
            nxt = V[k, :, at_block(jnp.minimum(b + 1, ext - 1))]
            ahead_next = pltpu.roll(nxt, LANES - 1, 1)
            rolled = pltpu.roll(here, 1, 1)
            sides = jnp.where(lane_t == 0, before, rolled)
            sides = sides + jnp.where(lane_t == LANES - 1, ahead_next, ahead)
            sides = sides + pltpu.roll(here, 1, 0) + pltpu.roll(here, tall - 1, 0)
            out = D[:, at_block(b)] * here - inv * sides
            V[k + 1, :, at_block(b)] = out
            return out, nxt, rolled, ahead_next

        def step(b, carry):
            here, before, ahead, cross, own, base = carry
            out, nxt, rolled, ahead_next = one(b, here, before, ahead)
            mine, image = here[8:top], out[8:top]
            cross = cross + fold(mine * image)
            own = own + fold(image * image)
            if k == 0:
                base = base + fold(mine * mine)
            return nxt, rolled, ahead_next, cross, own, base

        here = V[k, :, 0:LANES]
        ahead = pltpu.roll(here, LANES - 1, 1)
        _, here, before, ahead = one(0, here, ahead, ahead)
        zero = jnp.zeros((8, LANES), F32)
        here, before, ahead, cross, own, base = lax.fori_loop(
            1, blocks + 1, step, (here, before, ahead, zero, zero, zero), unroll=8
        )
        if k < ITERS - 1:
            one(ext - 1, here, before, ahead)
            mirror(k + 1)
        return cross, own, base

    sums = []
    for k in range(ITERS):
        cross, own, base = apply(k)
        if k == 0:
            sums.append(base)
        sums += [cross, own]

    red[...] = jnp.zeros_like(red)
    for i, value in enumerate(sums):
        red[i : i + 1, :] = jnp.sum(value, axis=0, keepdims=True)

    def over_lat(k):
        return remote(red, ra.at[lat], sem_a.at[0, k], sem_a.at[1, k], (lon, lat_at(k)))

    def over_lon(k):
        return remote(red, rb.at[lon], sem_b.at[0, k], sem_b.at[1, k], (lon_at(k), lat))

    @pl.loop(1, lats)
    def _(k):
        over_lat(k).start()

    ra[lat] = red[...]

    @pl.loop(1, lats)
    def _(k):
        over_lat(k).wait()

    total = ra[0]
    for i in range(1, lats):
        total = total + ra[i]
    red[...] = total

    @pl.loop(1, n)
    def _(k):
        over_lon(k).start()

    rb[lon] = red[...]

    @pl.loop(1, n)
    def _(k):
        over_lon(k).wait()

    total = rb[0]
    for i in range(1, n):
        total = total + rb[i]

    mu = [
        jnp.broadcast_to(jnp.sum(total[i : i + 1, :], axis=1, keepdims=True), (8, LANES))
        for i in range(2 * ITERS + 1)
    ]
    field, residual = cg_coefficients(mu)
    for i, c in enumerate(field + residual):
        coef_ref[i : i + 1, :] = c[0:1, :]

    @pl.loop(1, n)
    def _(k):
        meta(k).wait_send()
        heights(k).wait_send()
        weights(k).wait_send()

    east.wait_send()
    west.wait_send()

    @pl.when(lat < lats - 1)
    def _():
        edge_up().wait_send()
        rows_up().wait_send()

    @pl.when(lat > 0)
    def _():
        edge_dn().wait_send()
        rows_dn().wait_send()


def combine(rows, V, coef_ref, x_out, r_out, x_ref, r_ref, sem):
    coef = [coef_ref[i : i + 1, :] for i in range(2 * ITERS + 1)]
    coef = [jnp.broadcast_to(c, (rows, LANES)) for c in coef]
    field, residual = coef[:ITERS], coef[ITERS:]
    width = COLS_DEV // CHUNKS

    def copies(c):
        cols = pl.ds(c * width, width)
        return (
            pltpu.make_async_copy(x_ref.at[:, cols], x_out.at[:, cols], sem.at[0, c]),
            pltpu.make_async_copy(r_ref.at[:, cols], r_out.at[:, cols], sem.at[1, c]),
        )

    for c in range(CHUNKS):

        def one(b, carry):
            v = V[0, 8 : rows + 8, pl.ds(pl.multiple_of((b + 1) * LANES, LANES), LANES)]
            x, r = field[0] * v, residual[0] * v
            for k in range(1, ITERS + 1):
                v = V[k, 8 : rows + 8, pl.ds(pl.multiple_of((b + 1) * LANES, LANES), LANES)]
                r = r + residual[k] * v
                if k < ITERS:
                    x = x + field[k] * v
            cols = pl.ds(pl.multiple_of(b * LANES, LANES), LANES)
            x_ref[:, cols] = x
            r_ref[:, cols] = r
            return carry

        per = width // LANES
        lax.fori_loop(c * per, (c + 1) * per, one, 0, unroll=8)
        for copy in copies(c):
            copy.start()
    for c in range(CHUNKS):
        for copy in copies(c):
            copy.wait()


def body(n, lats, piece_height, piece_weight, piece_column, piece_width):
    pieces, rows, width = piece_height.shape
    ext = COLS_DEV + 2 * LANES
    vmem = pltpu.VMEM
    dma = pltpu.SemaphoreType.DMA
    scratch = [
        pltpu.SMEM((pieces,), jnp.int32),
        pltpu.SMEM((pieces,), jnp.int32),
        vmem((pieces, rows, LANES), F32),
        vmem((pieces, rows, LANES), F32),
        vmem((n, 2 * rows, LANES), F32),
        vmem((n, 2 * rows + 8, LANES), F32),
        vmem((n, 2 * rows, LANES), F32),
        vmem((n, 2 * rows + 8, LANES), F32),
        vmem((n, 1, LANES), jnp.int32),
        vmem((n, 1, LANES), jnp.int32),
        pltpu.SMEM((n, 1, LANES), jnp.int32),
        pltpu.SMEM((n, 4), jnp.int32),
        vmem((2, pieces, LANES), F32),
        vmem((2, pieces, LANES), F32),
        vmem((pieces, LANES), F32),
        vmem((pieces, LANES), F32),
        pltpu.SMEM((2 * n,), jnp.int32),
        pltpu.SMEM((2 * n,), jnp.int32),
        vmem((1, LANES), jnp.int32),
        pltpu.SMEM((1, LANES), jnp.int32),
        vmem((2 * n + 1, 6 * rows + 8, LANES), F32),
        vmem((rows + 16, ext), F32),
        vmem((3 * rows, LANES), F32),
        vmem((3 * rows, LANES), F32),
        vmem((2 * rows, LANES), F32),
        vmem((2 * rows, LANES), F32),
        vmem((8, ext), F32),
        vmem((8, ext), F32),
        vmem((8, ext), F32),
        vmem((8, ext), F32),
        vmem((16, LANES), F32),
        vmem((lats, 16, LANES), F32),
        vmem((n, 16, LANES), F32),
        dma((2, n)),
        dma((2, n)),
        dma((2, n)),
        dma((4,)),
        dma((4,)),
        dma((4,)),
        dma((2, lats)),
        dma((2, n)),
        dma((6,)),
    ]
    basis, coef = pl.pallas_call(
        functools.partial(kernel, n, lats, pieces, rows),
        out_shape=(
            jax.ShapeDtypeStruct((ITERS + 1, rows + 16, ext), F32),
            jax.ShapeDtypeStruct((16, LANES), F32),
        ),
        in_specs=[pl.BlockSpec(memory_space=pltpu.HBM)] * 4,
        out_specs=(pl.BlockSpec(memory_space=pltpu.VMEM),) * 2,
        scratch_shapes=scratch,
        compiler_params=pltpu.CompilerParams(
            collective_id=0, has_side_effects=True, vmem_limit_bytes=48 * 1024 * 1024
        ),
    )(*(pltpu.with_memory_space_constraint(a, pltpu.HBM) for a in (piece_column, piece_width, piece_height, piece_weight)))
    out = jax.ShapeDtypeStruct((rows, COLS_DEV), F32)
    return pl.pallas_call(
        functools.partial(combine, rows),
        out_shape=(out, out),
        in_specs=[pl.BlockSpec(memory_space=pltpu.VMEM)] * 2,
        out_specs=(pl.BlockSpec(memory_space=pltpu.HBM),) * 2,
        scratch_shapes=[
            vmem((rows, COLS_DEV), F32),
            vmem((rows, COLS_DEV), F32),
            dma((2, CHUNKS)),
        ],
        compiler_params=pltpu.CompilerParams(vmem_limit_bytes=16 * 1024 * 1024),
    )(basis, coef)


def solution(mesh):
    return jax.shard_map(
        functools.partial(body, mesh.shape["lon"], mesh.shape["lat"]),
        mesh=mesh,
        in_specs=(P("lon", "lat", None), P("lon", "lat", None), P("lon"), P("lon")),
        out_specs=(P("lat", "lon"), P("lat", "lon")),
        check_vma=False,
    )
```

```python
import functools

import jax
import jax.numpy as jnp
from jax import lax
from jax.experimental import pallas as pl
from jax.experimental.pallas import tpu as pltpu
from jax.sharding import PartitionSpec as P

COLS_DEV = 4096
ITERS = 4
MU_DATA = 0.5
DAMPING = 0.5
RIDGE = 0.05
SHIFT = 5.0
SCALE = 5.0

LANES = 128
CHUNKS = 4
MESH = pl.DeviceIdType.MESH
F32 = jnp.float32


def remote(src, dst, send, recv, device):
    return pltpu.make_async_remote_copy(
        src_ref=src, dst_ref=dst, send_sem=send, recv_sem=recv,
        device_id=device, device_id_type=MESH,
    )


def cg_coefficients(mu):
    def inner(a, b):
        total = None
        for i, x in enumerate(a):
            for j, y in enumerate(b):
                term = x * y * mu[i + j]
                total = term if total is None else total + term
        return total

    def apply(c):
        out = [SHIFT * x for x in c] + [jnp.zeros_like(c[0])]
        for i, x in enumerate(c):
            out[i + 1] = out[i + 1] + SCALE * x
        return out

    def add_scaled(y, a, x):
        out = []
        for i in range(max(len(x), len(y))):
            if i >= len(y):
                out.append(a * x[i])
            elif i >= len(x):
                out.append(y[i])
            else:
                out.append(y[i] + a * x[i])
        return out

    one = jnp.ones_like(mu[0])
    residual, direction, field = [one], [one], []
    norm = mu[0]
    for step in range(ITERS):
        image = apply(direction)
        alpha = norm / inner(direction, image)
        field = add_scaled(field, alpha, direction)
        residual = add_scaled(residual, -alpha, image)
        if step < ITERS - 1:
            fresh = inner(residual, residual)
            direction = add_scaled(residual, fresh / norm, direction)
            norm = fresh
    return field, residual


def kernel(
    n, lats, pieces, rows,
    col_in, wid_in, h_in, w_in, V, coef_ref,
    col_ref, wid_ref, h_ref, w_ref,
    hs, ws, hr, wr, ms, mr, msm, idx_s, up_s, up_r, dn_s, dn_r,
    blk_s, prev_s, last_v, last_s, S,
    D, east_s, east_r, west_s, west_r, lat_up_s, lat_up_r, lat_dn_s, lat_dn_r,
    side_up_s, side_up_r, side_dn_s, side_dn_r,
    red, ra, rb,
    sem_m, sem_h, sem_w, sem_e, sem_l, sem_t, sem_a, sem_b, sem_loc,
):
    lon = lax.axis_index("lon")
    lat = lax.axis_index("lat")
    blocks = COLS_DEV // LANES
    ext = blocks + 2
    top = rows + 8
    slots = 2 * n
    lane = lax.broadcasted_iota(jnp.int32, (rows, LANES), 1)
    lane1 = lax.broadcasted_iota(jnp.int32, (1, LANES), 1)

    def lon_at(k):
        return lax.rem(lon + k, n)

    def partner(k):
        other, bit = jnp.int32(0), 1
        while bit < n:
            other = other + (lon // bit + k // bit) % 2 * bit
            bit *= 2
        return other

    def lat_at(k):
        return lax.rem(lat + k, lats)

    barrier = pltpu.get_barrier_semaphore()
    loads = [
        pltpu.make_async_copy(src, dst, sem_loc.at[2 + i])
        for i, (src, dst) in enumerate(
            ((col_in, col_ref), (wid_in, wid_ref), (h_in, h_ref), (w_in, w_ref))
        )
    ]
    for load in loads:
        load.start()

    @pl.loop(1, n)
    def _(k):
        pl.semaphore_signal(barrier, inc=1, device_id=(partner(k), lat), device_id_type=MESH)

    @pl.loop(1, lats)
    def _(k):
        pl.semaphore_signal(barrier, inc=1, device_id=(lon, lat_at(k)), device_id_type=MESH)

    for load in loads:
        load.wait()

    @pl.loop(0, pieces)
    def _(i):
        up_s[0, pl.ds(i, 1), :] = h_ref[i, rows - 1 : rows, :]
        up_s[1, pl.ds(i, 1), :] = w_ref[i, rows - 1 : rows, :]
        dn_s[pl.ds(i, 1), :] = h_ref[i, 0:1, :]

    def fill(k, h_to, w_to, m_to):
        dest = partner(k)

        def scan(i, found):
            first, second = found
            match = (col_ref[i] >> 12) == dest
            second = jnp.where(match & (first >= 0) & (second < 0), i, second)
            first = jnp.where(match & (first < 0), i, first)
            return first, second

        found = lax.fori_loop(0, pieces, scan, (jnp.int32(-1), jnp.int32(-1)), unroll=8)
        tags = []
        for q in range(2):
            at = jnp.maximum(found[q], 0)
            limit = jnp.where(found[q] >= 0, wid_ref[at], 0)
            tags.append(jnp.where(found[q] >= 0, (col_ref[at] >> 7) & (blocks - 1), -1))
            idx_s[k, q] = at
            idx_s[k, 2 + q] = limit
            h_to[k, q * rows : (q + 1) * rows, :] = h_ref[at]
            w_to[k, q * rows : (q + 1) * rows, :] = jnp.where(lane < limit, w_ref[at], 0.0)
        m_to[k] = jnp.where(lane1 == 0, tags[0], jnp.where(lane1 == 1, tags[1], -1))

    far = n // 2

    @pl.loop(0, far)
    def _(i):
        fill(n - 1 - i, hs, ws, ms)

    pl.semaphore_wait(barrier, n - 1 + lats - 1)

    def edge_up():
        return remote(up_s, up_r, sem_e.at[0], sem_e.at[1], (lon, lat_at(1)))

    def edge_dn():
        return remote(dn_s, dn_r, sem_e.at[2], sem_e.at[3], (lon, lat_at(lats - 1)))

    def meta(k):
        return remote(ms.at[k], mr.at[k], sem_m.at[0, k], sem_m.at[1, k], (partner(k), lat))

    def heights(k):
        return remote(hs.at[k], hr.at[k], sem_h.at[0, k], sem_h.at[1, k], (partner(k), lat))

    def weights(k):
        return remote(ws.at[k], wr.at[k], sem_w.at[0, k], sem_w.at[1, k], (partner(k), lat))

    @pl.when(lat < lats - 1)
    def _():
        edge_up().start()

    @pl.when(lat > 0)
    def _():
        edge_dn().start()

    @pl.loop(0, far)
    def _(i):
        meta(n - 1 - i).start()
        heights(n - 1 - i).start()

    @pl.loop(far, n - 1)
    def _(i):
        fill(n - 1 - i, hs, ws, ms)
        meta(n - 1 - i).start()
        heights(n - 1 - i).start()

    fill(0, hr, wr, mr)

    @pl.when(lat > 0)
    def _():
        edge_up().wait_recv()

    @pl.when(lat == 0)
    def _():
        up_r[...] = jnp.zeros_like(up_r)

    @pl.when(lat < lats - 1)
    def _():
        edge_dn().wait_recv()

    @pl.when(lat == lats - 1)
    def _():
        dn_r[...] = jnp.zeros_like(dn_r)

    def extras(k, w_to):
        for q in range(2):
            at, limit = idx_s[k, q], idx_s[k, 2 + q]
            base = 2 * rows + q
            w_to[k, base : base + 1, :] = dn_r[pl.ds(at, 1), :]
            w_to[k, base + 2 : base + 3, :] = up_r[0, pl.ds(at, 1), :]
            w_to[k, base + 4 : base + 5, :] = jnp.where(lane1 < limit, up_r[1, pl.ds(at, 1), :], 0.0)
        w_to[k, 2 * rows + 6 : 2 * rows + 8, :] = jnp.zeros((2, LANES), F32)

    @pl.loop(1, n)
    def _(k):
        extras(n - k, ws)
        weights(n - k).start()

    extras(0, wr)

    @pl.loop(1, n)
    def _(k):
        meta(k).wait_recv()

    tags_in = pltpu.make_async_copy(mr, msm, sem_loc.at[0])
    tags_in.start()
    tags_in.wait()

    blk_s[0] = msm[0, 0, 0]
    blk_s[1] = msm[0, 0, 1]

    @pl.loop(1, n)
    def _(i):
        blk_s[2 * i] = msm[n - i, 0, 0]
        blk_s[2 * i + 1] = msm[n - i, 0, 1]

    def latest(p, last):
        tag = blk_s[p]

        def scan(j, found):
            return jnp.where((j < p) & (blk_s[j] == tag), j, found)

        prev_s[p] = lax.fori_loop(0, slots, scan, jnp.int32(slots), unroll=8)
        return jnp.where(lane1 == tag, p, last)

    last_v[...] = lax.fori_loop(0, slots, latest, jnp.full((1, LANES), slots, jnp.int32))
    last_in = pltpu.make_async_copy(last_v, last_s, sem_loc.at[1])
    last_in.start()
    last_in.wait()

    S[slots] = jnp.zeros((6 * rows + 8, LANES), F32)
    row_global = lat * rows + lax.broadcasted_iota(jnp.int32, (rows, LANES), 0)
    has_north = row_global < lats * rows - 1
    row_in = lax.broadcasted_iota(jnp.int32, (rows, LANES), 0)

    def terms(k, place):
        for q in range(2):
            p = 2 * place + q
            before = prev_s[p]
            h = hr[k, q * rows : (q + 1) * rows, :]
            w = wr[k, q * rows : (q + 1) * rows, :]
            base = 2 * rows + q
            above = wr[k, base : base + 1, :]
            below_h = wr[k, base + 2 : base + 3, :]
            below_w = wr[k, base + 4 : base + 5, :]
            h_north = jnp.where(row_in == rows - 1, above, pltpu.roll(h, rows - 1, 0))
            h_east = pltpu.roll(h, LANES - 1, 1)
            w_east = jnp.where((pltpu.roll(w, LANES - 1, 1) > 0.0) & (lane < LANES - 1), w, 0.0)
            w_north = jnp.where(has_north, w, 0.0)
            parts = (w, w * h, w_east, w_east * (h_east - h), w_north, w_north * (h_north - h))
            for t, part in enumerate(parts):
                at = pl.ds(t * rows, rows)
                S[p, at, :] = part + S[before, at, :]
            at = 6 * rows
            S[p, at : at + 1, :] = below_w + S[before, at : at + 1, :]
            S[p, at + 1 : at + 2, :] = below_w * (h[0:1, :] - below_h) + S[before, at + 1 : at + 2, :]

    terms(0, 0)

    @pl.loop(1, n)
    def _(i):
        heights(n - i).wait_recv()
        weights(n - i).wait_recv()
        terms(n - i, i)

    inv = 1.0 / SCALE

    def assemble(b, before):
        p = last_s[0, b]

        def field(t):
            return S[p, t * rows : (t + 1) * rows, :]

        at = 6 * rows
        t_east = field(3) / (field(2) + DAMPING)
        t_north = field(5) / (field(4) + DAMPING)
        t_below = S[p, at + 1 : at + 2, :] / (S[p, at : at + 1, :] + DAMPING)
        t_south = jnp.where(row_in == 0, t_below, pltpu.roll(t_north, 1, 0))
        rolled = pltpu.roll(t_east, 1, 1)
        t_west = jnp.where(lane == 0, before, rolled)
        right = MU_DATA * field(1) - (t_east - t_west) - (t_north - t_south)
        cols = pl.ds(pl.multiple_of((b + 1) * LANES, LANES), LANES)
        V[0, 8:top, cols] = right
        D[8:top, cols] = (MU_DATA * field(0) + (RIDGE + 4.0 - SHIFT)) * inv
        return rolled

    east_last = lax.fori_loop(0, blocks, assemble, jnp.zeros((rows, LANES), F32), unroll=8)

    first = slice(LANES, 2 * LANES)
    final = slice(blocks * LANES, (blocks + 1) * LANES)
    east_s[0:rows, :] = V[0, 8:top, final]
    east_s[rows : 2 * rows, :] = D[8:top, final]
    east_s[2 * rows : 3 * rows, :] = east_last
    west_s[0:rows, :] = V[0, 8:top, first]
    west_s[rows : 2 * rows, :] = D[8:top, first]
    east = remote(east_s, east_r, sem_l.at[0], sem_l.at[1], (lon_at(1), lat))
    west = remote(west_s, west_r, sem_l.at[2], sem_l.at[3], (lon_at(n - 1), lat))
    east.start()
    west.start()

    inner = slice(LANES, (blocks + 1) * LANES)
    lat_up_s[0:4, :] = D[top - 4 : top, inner]
    lat_up_s[4:8, :] = V[0, top - 4 : top, inner]
    lat_dn_s[0:4, :] = V[0, 8:12, inner]
    lat_dn_s[4:8, :] = D[8:12, inner]

    def rows_up():
        return remote(lat_up_s, lat_up_r, sem_t.at[0], sem_t.at[1], (lon, lat_at(1)))

    def rows_dn():
        return remote(lat_dn_s, lat_dn_r, sem_t.at[2], sem_t.at[3], (lon, lat_at(lats - 1)))

    def sides_up():
        return remote(side_up_s, side_up_r, sem_t.at[4], sem_t.at[5], (lon, lat_at(1)))

    def sides_dn():
        return remote(side_dn_s, side_dn_r, sem_t.at[6], sem_t.at[7], (lon, lat_at(lats - 1)))

    @pl.when(lat < lats - 1)
    def _():
        rows_up().start()

    @pl.when(lat > 0)
    def _():
        rows_dn().start()

    halo_w = slice(0, LANES)
    halo_e = slice((blocks + 1) * LANES, (blocks + 2) * LANES)
    east.wait_recv()
    V[0, 8:top, halo_w] = east_r[0:rows, :]
    D[8:top, halo_w] = east_r[rows : 2 * rows, :]
    V[0, 8:top, first] = V[0, 8:top, first] + jnp.where(lane == 0, east_r[2 * rows : 3 * rows, :], 0.0)
    west.wait_recv()
    V[0, 8:top, halo_e] = west_r[0:rows, :] + jnp.where(lane == 0, east_last, 0.0)
    D[8:top, halo_e] = west_r[rows : 2 * rows, :]
    side_blocks = (halo_w, first, halo_e)
    for i, cols in enumerate(side_blocks):
        to = slice(i * LANES, (i + 1) * LANES)
        side_up_s[0:4, to] = D[top - 4 : top, cols]
        side_up_s[4:8, to] = V[0, top - 4 : top, cols]
        side_dn_s[0:4, to] = V[0, 8:12, cols]
        side_dn_s[4:8, to] = D[8:12, cols]

    @pl.when(lat < lats - 1)
    def _():
        sides_up().start()

    @pl.when(lat > 0)
    def _():
        sides_dn().start()

    def mirror(k):
        @pl.when(lat == 0)
        def _():
            V[k, 7:8, :] = V[k, 8:9, :]

        @pl.when(lat == lats - 1)
        def _():
            V[k, top : top + 1, :] = V[k, top - 1 : top, :]

    @pl.when(lat > 0)
    def _():
        rows_up().wait_recv()
        got = lat_up_r[...]
        V[0, 0:8, inner] = got
        D[0:8, inner] = pltpu.roll(got, 4, 0)
        sides_up().wait_recv()
        for i, cols in enumerate(side_blocks):
            got = side_up_r[:, i * LANES : (i + 1) * LANES]
            V[0, 0:8, cols] = got
            D[0:8, cols] = pltpu.roll(got, 4, 0)

    @pl.when(lat == 0)
    def _():
        V[0, 0:8, :] = jnp.zeros((8, ext * LANES), F32)
        D[0:8, :] = jnp.zeros((8, ext * LANES), F32)

    @pl.when(lat < lats - 1)
    def _():
        rows_dn().wait_recv()
        got = lat_dn_r[...]
        V[0, top : top + 8, inner] = got
        D[top : top + 8, inner] = pltpu.roll(got, 4, 0)
        sides_dn().wait_recv()
        for i, cols in enumerate(side_blocks):
            got = side_dn_r[:, i * LANES : (i + 1) * LANES]
            V[0, top : top + 8, cols] = got
            D[top : top + 8, cols] = pltpu.roll(got, 4, 0)

    @pl.when(lat == lats - 1)
    def _():
        V[0, top : top + 8, :] = jnp.zeros((8, ext * LANES), F32)
        D[top : top + 8, :] = jnp.zeros((8, ext * LANES), F32)

    mirror(0)

    tall = rows + 16
    lane_t = lax.broadcasted_iota(jnp.int32, (tall, LANES), 1)

    def at_block(b):
        return pl.ds(pl.multiple_of(b * LANES, LANES), LANES)

    def fold(value):
        total = value[0:8]
        for i in range(1, rows // 8):
            total = total + value[8 * i : 8 * i + 8]
        return total

    def apply(k):
        def one(b, here, before, ahead):
            nxt = V[k, :, at_block(jnp.minimum(b + 1, ext - 1))]
            ahead_next = pltpu.roll(nxt, LANES - 1, 1)
            rolled = pltpu.roll(here, 1, 1)
            sides = jnp.where(lane_t == 0, before, rolled)
            sides = sides + jnp.where(lane_t == LANES - 1, ahead_next, ahead)
            sides = sides + pltpu.roll(here, 1, 0) + pltpu.roll(here, tall - 1, 0)
            out = D[:, at_block(b)] * here - inv * sides
            V[k + 1, :, at_block(b)] = out
            return out, nxt, rolled, ahead_next

        def step(b, carry):
            here, before, ahead, cross, own, base = carry
            out, nxt, rolled, ahead_next = one(b, here, before, ahead)
            mine, image = here[8:top], out[8:top]
            cross = cross + fold(mine * image)
            own = own + fold(image * image)
            if k == 0:
                base = base + fold(mine * mine)
            return nxt, rolled, ahead_next, cross, own, base

        here = V[k, :, 0:LANES]
        ahead = pltpu.roll(here, LANES - 1, 1)
        _, here, before, ahead = one(0, here, ahead, ahead)
        zero = jnp.zeros((8, LANES), F32)
        here, before, ahead, cross, own, base = lax.fori_loop(
            1, blocks + 1, step, (here, before, ahead, zero, zero, zero), unroll=8
        )
        if k < ITERS - 1:
            one(ext - 1, here, before, ahead)
            mirror(k + 1)
        return cross, own, base

    sums = []
    for k in range(ITERS):
        cross, own, base = apply(k)
        if k == 0:
            sums.append(base)
        sums += [cross, own]

    red[...] = jnp.zeros_like(red)
    for i, value in enumerate(sums):
        red[i : i + 1, :] = jnp.sum(value, axis=0, keepdims=True)

    def over_lat(k):
        return remote(red, ra.at[lat], sem_a.at[0, k], sem_a.at[1, k], (lon, lat_at(k)))

    def over_lon(k):
        return remote(red, rb.at[lon], sem_b.at[0, k], sem_b.at[1, k], (lon_at(k), lat))

    @pl.loop(1, lats)
    def _(k):
        over_lat(k).start()

    ra[lat] = red[...]

    @pl.loop(1, lats)
    def _(k):
        over_lat(k).wait()

    total = ra[0]
    for i in range(1, lats):
        total = total + ra[i]
    red[...] = total

    @pl.loop(1, n)
    def _(k):
        over_lon(k).start()

    rb[lon] = red[...]

    @pl.loop(1, n)
    def _(k):
        over_lon(k).wait()

    total = rb[0]
    for i in range(1, n):
        total = total + rb[i]

    mu = [
        jnp.broadcast_to(jnp.sum(total[i : i + 1, :], axis=1, keepdims=True), (8, LANES))
        for i in range(2 * ITERS + 1)
    ]
    field, residual = cg_coefficients(mu)
    for i, c in enumerate(field + residual):
        coef_ref[i : i + 1, :] = c[0:1, :]

    @pl.loop(1, n)
    def _(k):
        meta(k).wait_send()
        heights(k).wait_send()
        weights(k).wait_send()

    east.wait_send()
    west.wait_send()

    @pl.when(lat < lats - 1)
    def _():
        edge_up().wait_send()
        rows_up().wait_send()
        sides_up().wait_send()

    @pl.when(lat > 0)
    def _():
        edge_dn().wait_send()
        rows_dn().wait_send()
        sides_dn().wait_send()


def combine(rows, V, coef_ref, x_out, r_out, x_ref, r_ref, sem):
    coef = [coef_ref[i : i + 1, :] for i in range(2 * ITERS + 1)]
    coef = [jnp.broadcast_to(c, (rows, LANES)) for c in coef]
    field, residual = coef[:ITERS], coef[ITERS:]
    width = COLS_DEV // CHUNKS

    def copies(c):
        cols = pl.ds(c * width, width)
        return (
            pltpu.make_async_copy(x_ref.at[:, cols], x_out.at[:, cols], sem.at[0, c]),
            pltpu.make_async_copy(r_ref.at[:, cols], r_out.at[:, cols], sem.at[1, c]),
        )

    for c in range(CHUNKS):

        def one(b, carry):
            v = V[0, 8 : rows + 8, pl.ds(pl.multiple_of((b + 1) * LANES, LANES), LANES)]
            x, r = field[0] * v, residual[0] * v
            for k in range(1, ITERS + 1):
                v = V[k, 8 : rows + 8, pl.ds(pl.multiple_of((b + 1) * LANES, LANES), LANES)]
                r = r + residual[k] * v
                if k < ITERS:
                    x = x + field[k] * v
            cols = pl.ds(pl.multiple_of(b * LANES, LANES), LANES)
            x_ref[:, cols] = x
            r_ref[:, cols] = r
            return carry

        per = width // LANES
        lax.fori_loop(c * per, (c + 1) * per, one, 0, unroll=8)
        for copy in copies(c):
            copy.start()
    for c in range(CHUNKS):
        for copy in copies(c):
            copy.wait()


def body(n, lats, piece_height, piece_weight, piece_column, piece_width):
    pieces, rows, width = piece_height.shape
    ext = COLS_DEV + 2 * LANES
    vmem = pltpu.VMEM
    dma = pltpu.SemaphoreType.DMA
    scratch = [
        pltpu.SMEM((pieces,), jnp.int32),
        pltpu.SMEM((pieces,), jnp.int32),
        vmem((pieces, rows, LANES), F32),
        vmem((pieces, rows, LANES), F32),
        vmem((n, 2 * rows, LANES), F32),
        vmem((n, 2 * rows + 8, LANES), F32),
        vmem((n, 2 * rows, LANES), F32),
        vmem((n, 2 * rows + 8, LANES), F32),
        vmem((n, 1, LANES), jnp.int32),
        vmem((n, 1, LANES), jnp.int32),
        pltpu.SMEM((n, 1, LANES), jnp.int32),
        pltpu.SMEM((n, 4), jnp.int32),
        vmem((2, pieces, LANES), F32),
        vmem((2, pieces, LANES), F32),
        vmem((pieces, LANES), F32),
        vmem((pieces, LANES), F32),
        pltpu.SMEM((2 * n,), jnp.int32),
        pltpu.SMEM((2 * n,), jnp.int32),
        vmem((1, LANES), jnp.int32),
        pltpu.SMEM((1, LANES), jnp.int32),
        vmem((2 * n + 1, 6 * rows + 8, LANES), F32),
        vmem((rows + 16, ext), F32),
        vmem((3 * rows, LANES), F32),
        vmem((3 * rows, LANES), F32),
        vmem((2 * rows, LANES), F32),
        vmem((2 * rows, LANES), F32),
        vmem((8, COLS_DEV), F32),
        vmem((8, COLS_DEV), F32),
        vmem((8, COLS_DEV), F32),
        vmem((8, COLS_DEV), F32),
        vmem((8, 3 * LANES), F32),
        vmem((8, 3 * LANES), F32),
        vmem((8, 3 * LANES), F32),
        vmem((8, 3 * LANES), F32),
        vmem((16, LANES), F32),
        vmem((lats, 16, LANES), F32),
        vmem((n, 16, LANES), F32),
        dma((2, n)),
        dma((2, n)),
        dma((2, n)),
        dma((4,)),
        dma((4,)),
        dma((8,)),
        dma((2, lats)),
        dma((2, n)),
        dma((6,)),
    ]
    basis, coef = pl.pallas_call(
        functools.partial(kernel, n, lats, pieces, rows),
        out_shape=(
            jax.ShapeDtypeStruct((ITERS + 1, rows + 16, ext), F32),
            jax.ShapeDtypeStruct((16, LANES), F32),
        ),
        in_specs=[pl.BlockSpec(memory_space=pltpu.HBM)] * 4,
        out_specs=(pl.BlockSpec(memory_space=pltpu.VMEM),) * 2,
        scratch_shapes=scratch,
        compiler_params=pltpu.CompilerParams(
            collective_id=0, has_side_effects=True, vmem_limit_bytes=48 * 1024 * 1024
        ),
    )(*(pltpu.with_memory_space_constraint(a, pltpu.HBM) for a in (piece_column, piece_width, piece_height, piece_weight)))
    out = jax.ShapeDtypeStruct((rows, COLS_DEV), F32)
    return pl.pallas_call(
        functools.partial(combine, rows),
        out_shape=(out, out),
        in_specs=[pl.BlockSpec(memory_space=pltpu.VMEM)] * 2,
        out_specs=(pl.BlockSpec(memory_space=pltpu.HBM),) * 2,
        scratch_shapes=[
            vmem((rows, COLS_DEV), F32),
            vmem((rows, COLS_DEV), F32),
            dma((2, CHUNKS)),
        ],
        compiler_params=pltpu.CompilerParams(vmem_limit_bytes=16 * 1024 * 1024),
    )(basis, coef)


def solution(mesh):
    return jax.shard_map(
        functools.partial(body, mesh.shape["lon"], mesh.shape["lat"]),
        mesh=mesh,
        in_specs=(P("lon", "lat", None), P("lon", "lat", None), P("lon"), P("lon")),
        out_specs=(P("lat", "lon"), P("lat", "lon")),
        check_vma=False,
    )
```

```python
import functools

import jax
import jax.numpy as jnp
from jax import lax
from jax.experimental import pallas as pl
from jax.experimental.pallas import tpu as pltpu
from jax.sharding import PartitionSpec as P

COLS_DEV = 4096
ITERS = 4
MU_DATA = 0.5
DAMPING = 0.5
RIDGE = 0.05
SHIFT = 5.0
SCALE = 5.0

LANES = 128
CHUNKS = 4
MESH = pl.DeviceIdType.MESH
F32 = jnp.float32


def remote(src, dst, send, recv, device):
    return pltpu.make_async_remote_copy(
        src_ref=src, dst_ref=dst, send_sem=send, recv_sem=recv,
        device_id=device, device_id_type=MESH,
    )


def cg_coefficients(mu):
    def inner(a, b):
        total = None
        for i, x in enumerate(a):
            for j, y in enumerate(b):
                term = x * y * mu[i + j]
                total = term if total is None else total + term
        return total

    def apply(c):
        out = [SHIFT * x for x in c] + [jnp.zeros_like(c[0])]
        for i, x in enumerate(c):
            out[i + 1] = out[i + 1] + SCALE * x
        return out

    def add_scaled(y, a, x):
        out = []
        for i in range(max(len(x), len(y))):
            if i >= len(y):
                out.append(a * x[i])
            elif i >= len(x):
                out.append(y[i])
            else:
                out.append(y[i] + a * x[i])
        return out

    one = jnp.ones_like(mu[0])
    residual, direction, field = [one], [one], []
    norm = mu[0]
    for step in range(ITERS):
        image = apply(direction)
        alpha = norm / inner(direction, image)
        field = add_scaled(field, alpha, direction)
        residual = add_scaled(residual, -alpha, image)
        if step < ITERS - 1:
            fresh = inner(residual, residual)
            direction = add_scaled(residual, fresh / norm, direction)
            norm = fresh
    return field, residual


def kernel(
    n, lats, pieces, rows,
    col_in, wid_in, h_in, w_in, V, coef_ref,
    col_ref, wid_ref, h_ref, w_ref,
    hs, ws, hr, wr, ms, mr, msm, idx_s, up_s, up_r, dn_s, dn_r,
    blk_s, prev_s, last_v, last_s, S,
    D, east_s, east_r, west_s, west_r, lat_up_s, lat_up_r, lat_dn_s, lat_dn_r,
    side_up_s, side_up_r, side_dn_s, side_dn_r,
    red, rb,
    sem_m, sem_h, sem_w, sem_e, sem_l, sem_t, sem_b, sem_loc,
):
    lon = lax.axis_index("lon")
    lat = lax.axis_index("lat")
    blocks = COLS_DEV // LANES
    ext = blocks + 2
    top = rows + 8
    slots = 2 * n
    lane = lax.broadcasted_iota(jnp.int32, (rows, LANES), 1)
    lane1 = lax.broadcasted_iota(jnp.int32, (1, LANES), 1)

    def lon_at(k):
        return lax.rem(lon + k, n)

    def partner(k):
        other, bit = jnp.int32(0), 1
        while bit < n:
            other = other + (lon // bit + k // bit) % 2 * bit
            bit *= 2
        return other

    def lat_at(k):
        return lax.rem(lat + k, lats)

    barrier = pltpu.get_barrier_semaphore()
    loads = [
        pltpu.make_async_copy(src, dst, sem_loc.at[2 + i])
        for i, (src, dst) in enumerate(
            ((col_in, col_ref), (wid_in, wid_ref), (h_in, h_ref), (w_in, w_ref))
        )
    ]
    for load in loads:
        load.start()

    devices = n * lats

    def peer(j):
        return partner(j // lats), lat_at(j % lats)

    @pl.loop(1, devices)
    def _(j):
        pl.semaphore_signal(barrier, inc=1, device_id=peer(j), device_id_type=MESH)

    for load in loads:
        load.wait()

    @pl.loop(0, pieces)
    def _(i):
        up_s[0, pl.ds(i, 1), :] = h_ref[i, rows - 1 : rows, :]
        up_s[1, pl.ds(i, 1), :] = w_ref[i, rows - 1 : rows, :]
        dn_s[pl.ds(i, 1), :] = h_ref[i, 0:1, :]

    def fill(k, h_to, w_to, m_to):
        dest = partner(k)

        def scan(i, found):
            first, second = found
            match = (col_ref[i] >> 12) == dest
            second = jnp.where(match & (first >= 0) & (second < 0), i, second)
            first = jnp.where(match & (first < 0), i, first)
            return first, second

        found = lax.fori_loop(0, pieces, scan, (jnp.int32(-1), jnp.int32(-1)), unroll=8)
        tags = []
        for q in range(2):
            at = jnp.maximum(found[q], 0)
            limit = jnp.where(found[q] >= 0, wid_ref[at], 0)
            tags.append(jnp.where(found[q] >= 0, (col_ref[at] >> 7) & (blocks - 1), -1))
            idx_s[k, q] = at
            idx_s[k, 2 + q] = limit
            h_to[k, q * rows : (q + 1) * rows, :] = h_ref[at]
            w_to[k, q * rows : (q + 1) * rows, :] = jnp.where(lane < limit, w_ref[at], 0.0)
        m_to[k] = jnp.where(lane1 == 0, tags[0], jnp.where(lane1 == 1, tags[1], -1))

    far = n // 2

    @pl.loop(0, far)
    def _(i):
        fill(n - 1 - i, hs, ws, ms)

    pl.semaphore_wait(barrier, devices - 1)

    def edge_up():
        return remote(up_s, up_r, sem_e.at[0], sem_e.at[1], (lon, lat_at(1)))

    def edge_dn():
        return remote(dn_s, dn_r, sem_e.at[2], sem_e.at[3], (lon, lat_at(lats - 1)))

    def meta(k):
        return remote(ms.at[k], mr.at[k], sem_m.at[0, k], sem_m.at[1, k], (partner(k), lat))

    def heights(k):
        return remote(hs.at[k], hr.at[k], sem_h.at[0, k], sem_h.at[1, k], (partner(k), lat))

    def weights(k):
        return remote(ws.at[k], wr.at[k], sem_w.at[0, k], sem_w.at[1, k], (partner(k), lat))

    @pl.when(lat < lats - 1)
    def _():
        edge_up().start()

    @pl.when(lat > 0)
    def _():
        edge_dn().start()

    @pl.loop(0, far)
    def _(i):
        meta(n - 1 - i).start()
        heights(n - 1 - i).start()

    @pl.loop(far, n - 1)
    def _(i):
        fill(n - 1 - i, hs, ws, ms)
        meta(n - 1 - i).start()
        heights(n - 1 - i).start()

    fill(0, hr, wr, mr)

    @pl.when(lat > 0)
    def _():
        edge_up().wait_recv()

    @pl.when(lat == 0)
    def _():
        up_r[...] = jnp.zeros_like(up_r)

    @pl.when(lat < lats - 1)
    def _():
        edge_dn().wait_recv()

    @pl.when(lat == lats - 1)
    def _():
        dn_r[...] = jnp.zeros_like(dn_r)

    def extras(k, w_to):
        for q in range(2):
            at, limit = idx_s[k, q], idx_s[k, 2 + q]
            base = 2 * rows + q
            w_to[k, base : base + 1, :] = dn_r[pl.ds(at, 1), :]
            w_to[k, base + 2 : base + 3, :] = up_r[0, pl.ds(at, 1), :]
            w_to[k, base + 4 : base + 5, :] = jnp.where(lane1 < limit, up_r[1, pl.ds(at, 1), :], 0.0)
        w_to[k, 2 * rows + 6 : 2 * rows + 8, :] = jnp.zeros((2, LANES), F32)

    @pl.loop(1, n)
    def _(k):
        extras(n - k, ws)
        weights(n - k).start()

    extras(0, wr)

    @pl.loop(1, n)
    def _(k):
        meta(k).wait_recv()

    tags_in = pltpu.make_async_copy(mr, msm, sem_loc.at[0])
    tags_in.start()
    tags_in.wait()

    blk_s[0] = msm[0, 0, 0]
    blk_s[1] = msm[0, 0, 1]

    @pl.loop(1, n)
    def _(i):
        blk_s[2 * i] = msm[n - i, 0, 0]
        blk_s[2 * i + 1] = msm[n - i, 0, 1]

    def latest(p, last):
        tag = blk_s[p]

        def scan(j, found):
            return jnp.where((j < p) & (blk_s[j] == tag), j, found)

        prev_s[p] = lax.fori_loop(0, slots, scan, jnp.int32(slots), unroll=8)
        return jnp.where(lane1 == tag, p, last)

    last_v[...] = lax.fori_loop(0, slots, latest, jnp.full((1, LANES), slots, jnp.int32))
    last_in = pltpu.make_async_copy(last_v, last_s, sem_loc.at[1])
    last_in.start()
    last_in.wait()

    S[slots] = jnp.zeros((6 * rows + 8, LANES), F32)
    row_global = lat * rows + lax.broadcasted_iota(jnp.int32, (rows, LANES), 0)
    has_north = row_global < lats * rows - 1
    row_in = lax.broadcasted_iota(jnp.int32, (rows, LANES), 0)

    def terms(k, place):
        for q in range(2):
            p = 2 * place + q
            before = prev_s[p]
            h = hr[k, q * rows : (q + 1) * rows, :]
            w = wr[k, q * rows : (q + 1) * rows, :]
            base = 2 * rows + q
            above = wr[k, base : base + 1, :]
            below_h = wr[k, base + 2 : base + 3, :]
            below_w = wr[k, base + 4 : base + 5, :]
            h_north = jnp.where(row_in == rows - 1, above, pltpu.roll(h, rows - 1, 0))
            h_east = pltpu.roll(h, LANES - 1, 1)
            w_east = jnp.where((pltpu.roll(w, LANES - 1, 1) > 0.0) & (lane < LANES - 1), w, 0.0)
            w_north = jnp.where(has_north, w, 0.0)
            parts = (w, w * h, w_east, w_east * (h_east - h), w_north, w_north * (h_north - h))
            for t, part in enumerate(parts):
                at = pl.ds(t * rows, rows)
                S[p, at, :] = part + S[before, at, :]
            at = 6 * rows
            S[p, at : at + 1, :] = below_w + S[before, at : at + 1, :]
            S[p, at + 1 : at + 2, :] = below_w * (h[0:1, :] - below_h) + S[before, at + 1 : at + 2, :]

    terms(0, 0)

    @pl.loop(1, n)
    def _(i):
        heights(n - i).wait_recv()
        weights(n - i).wait_recv()
        terms(n - i, i)

    inv = 1.0 / SCALE

    def assemble(b, before):
        p = last_s[0, b]

        def field(t):
            return S[p, t * rows : (t + 1) * rows, :]

        at = 6 * rows
        t_east = field(3) / (field(2) + DAMPING)
        t_north = field(5) / (field(4) + DAMPING)
        t_below = S[p, at + 1 : at + 2, :] / (S[p, at : at + 1, :] + DAMPING)
        t_south = jnp.where(row_in == 0, t_below, pltpu.roll(t_north, 1, 0))
        rolled = pltpu.roll(t_east, 1, 1)
        t_west = jnp.where(lane == 0, before, rolled)
        right = MU_DATA * field(1) - (t_east - t_west) - (t_north - t_south)
        cols = pl.ds(pl.multiple_of((b + 1) * LANES, LANES), LANES)
        V[0, 8:top, cols] = right
        D[8:top, cols] = (MU_DATA * field(0) + (RIDGE + 4.0 - SHIFT)) * inv
        return rolled

    east_last = lax.fori_loop(0, blocks, assemble, jnp.zeros((rows, LANES), F32), unroll=8)

    first = slice(LANES, 2 * LANES)
    final = slice(blocks * LANES, (blocks + 1) * LANES)
    east_s[...] = jnp.where(
        lane >= LANES - 4,
        V[0, 8:top, final],
        jnp.where(
            lane >= LANES - 8,
            pltpu.roll(D[8:top, final], LANES - 4, 1),
            pltpu.roll(east_last, LANES - 9, 1),
        ),
    )
    west_s[...] = jnp.where(lane < 4, V[0, 8:top, first], pltpu.roll(D[8:top, first], 4, 1))
    east = remote(east_s, east_r, sem_l.at[0], sem_l.at[1], (lon_at(1), lat))
    west = remote(west_s, west_r, sem_l.at[2], sem_l.at[3], (lon_at(n - 1), lat))
    east.start()
    west.start()

    inner = slice(LANES, (blocks + 1) * LANES)
    lat_up_s[0:4, :] = D[top - 4 : top, inner]
    lat_up_s[4:8, :] = V[0, top - 4 : top, inner]
    lat_dn_s[0:4, :] = V[0, 8:12, inner]
    lat_dn_s[4:8, :] = D[8:12, inner]

    def rows_up():
        return remote(lat_up_s, lat_up_r, sem_t.at[0], sem_t.at[1], (lon, lat_at(1)))

    def rows_dn():
        return remote(lat_dn_s, lat_dn_r, sem_t.at[2], sem_t.at[3], (lon, lat_at(lats - 1)))

    def sides_up():
        return remote(side_up_s, side_up_r, sem_t.at[4], sem_t.at[5], (lon, lat_at(1)))

    def sides_dn():
        return remote(side_dn_s, side_dn_r, sem_t.at[6], sem_t.at[7], (lon, lat_at(lats - 1)))

    @pl.when(lat < lats - 1)
    def _():
        rows_up().start()

    @pl.when(lat > 0)
    def _():
        rows_dn().start()

    halo_w = slice(0, LANES)
    halo_e = slice((blocks + 1) * LANES, (blocks + 2) * LANES)
    east.wait_recv()
    got_east = east_r[...]
    V[0, 8:top, halo_w] = got_east
    D[8:top, halo_w] = pltpu.roll(got_east, 4, 1)
    V[0, 8:top, first] = V[0, 8:top, first] + jnp.where(lane == 0, pltpu.roll(got_east, 9, 1), 0.0)
    west.wait_recv()
    got_west = west_r[...]
    V[0, 8:top, halo_e] = got_west + jnp.where(lane == 0, east_last, 0.0)
    D[8:top, halo_e] = pltpu.roll(got_west, LANES - 4, 1)
    side_blocks = (halo_w, first, halo_e)
    for i, cols in enumerate(side_blocks):
        to = slice(i * LANES, (i + 1) * LANES)
        side_up_s[0:4, to] = D[top - 4 : top, cols]
        side_up_s[4:8, to] = V[0, top - 4 : top, cols]
        side_dn_s[0:4, to] = V[0, 8:12, cols]
        side_dn_s[4:8, to] = D[8:12, cols]

    @pl.when(lat < lats - 1)
    def _():
        sides_up().start()

    @pl.when(lat > 0)
    def _():
        sides_dn().start()

    def mirror(k):
        @pl.when(lat == 0)
        def _():
            V[k, 7:8, :] = V[k, 8:9, :]

        @pl.when(lat == lats - 1)
        def _():
            V[k, top : top + 1, :] = V[k, top - 1 : top, :]

    @pl.when(lat > 0)
    def _():
        rows_up().wait_recv()
        got = lat_up_r[...]
        V[0, 0:8, inner] = got
        D[0:8, inner] = pltpu.roll(got, 4, 0)
        sides_up().wait_recv()
        for i, cols in enumerate(side_blocks):
            got = side_up_r[:, i * LANES : (i + 1) * LANES]
            V[0, 0:8, cols] = got
            D[0:8, cols] = pltpu.roll(got, 4, 0)

    @pl.when(lat == 0)
    def _():
        V[0, 0:8, :] = jnp.zeros((8, ext * LANES), F32)
        D[0:8, :] = jnp.zeros((8, ext * LANES), F32)

    @pl.when(lat < lats - 1)
    def _():
        rows_dn().wait_recv()
        got = lat_dn_r[...]
        V[0, top : top + 8, inner] = got
        D[top : top + 8, inner] = pltpu.roll(got, 4, 0)
        sides_dn().wait_recv()
        for i, cols in enumerate(side_blocks):
            got = side_dn_r[:, i * LANES : (i + 1) * LANES]
            V[0, top : top + 8, cols] = got
            D[top : top + 8, cols] = pltpu.roll(got, 4, 0)

    @pl.when(lat == lats - 1)
    def _():
        V[0, top : top + 8, :] = jnp.zeros((8, ext * LANES), F32)
        D[top : top + 8, :] = jnp.zeros((8, ext * LANES), F32)

    mirror(0)

    tall = rows + 16
    lane_t = lax.broadcasted_iota(jnp.int32, (tall, LANES), 1)

    def at_block(b):
        return pl.ds(pl.multiple_of(b * LANES, LANES), LANES)

    def fold(value):
        total = value[0:8]
        for i in range(1, rows // 8):
            total = total + value[8 * i : 8 * i + 8]
        return total

    def apply(k):
        def one(b, here, before, ahead):
            nxt = V[k, :, at_block(jnp.minimum(b + 1, ext - 1))]
            ahead_next = pltpu.roll(nxt, LANES - 1, 1)
            rolled = pltpu.roll(here, 1, 1)
            sides = jnp.where(lane_t == 0, before, rolled)
            sides = sides + jnp.where(lane_t == LANES - 1, ahead_next, ahead)
            sides = sides + pltpu.roll(here, 1, 0) + pltpu.roll(here, tall - 1, 0)
            out = D[:, at_block(b)] * here - inv * sides
            V[k + 1, :, at_block(b)] = out
            return out, nxt, rolled, ahead_next

        def step(b, carry):
            here, before, ahead, cross, own, base = carry
            out, nxt, rolled, ahead_next = one(b, here, before, ahead)
            mine, image = here[8:top], out[8:top]
            cross = cross + fold(mine * image)
            own = own + fold(image * image)
            if k == 0:
                base = base + fold(mine * mine)
            return nxt, rolled, ahead_next, cross, own, base

        here = V[k, :, 0:LANES]
        ahead = pltpu.roll(here, LANES - 1, 1)
        _, here, before, ahead = one(0, here, ahead, ahead)
        zero = jnp.zeros((8, LANES), F32)
        here, before, ahead, cross, own, base = lax.fori_loop(
            1, blocks + 1, step, (here, before, ahead, zero, zero, zero), unroll=8
        )
        if k < ITERS - 1:
            one(ext - 1, here, before, ahead)
            mirror(k + 1)
        return cross, own, base

    sums = []
    for k in range(ITERS):
        cross, own, base = apply(k)
        if k == 0:
            sums.append(base)
        sums += [cross, own]

    mine = jnp.zeros((1, LANES), F32)
    for i, value in enumerate(sums):
        value = jnp.sum(jnp.sum(value, axis=0, keepdims=True), axis=1, keepdims=True)
        mine = jnp.where(lane1 == i, value, mine)
    red[...] = mine
    place = lon * lats + lat

    def share(j):
        return remote(red, rb.at[place], sem_b.at[0, j], sem_b.at[1, j], peer(j))

    @pl.loop(1, devices)
    def _(j):
        share(devices - j).start()

    rb[place] = mine

    @pl.loop(1, devices)
    def _(j):
        share(j).wait_recv()

    total = jnp.sum(rb[...], axis=0)
    mu = [
        jnp.broadcast_to(
            jnp.sum(jnp.where(lane1 == i, total, 0.0), axis=1, keepdims=True), (8, LANES)
        )
        for i in range(2 * ITERS + 1)
    ]
    field, residual = cg_coefficients(mu)
    for i, c in enumerate(field + residual):
        coef_ref[i : i + 1, :] = c[0:1, :]

    @pl.loop(1, n)
    def _(k):
        meta(k).wait_send()
        heights(k).wait_send()
        weights(k).wait_send()

    @pl.loop(1, devices)
    def _(j):
        share(j).wait_send()

    east.wait_send()
    west.wait_send()

    @pl.when(lat < lats - 1)
    def _():
        edge_up().wait_send()
        rows_up().wait_send()
        sides_up().wait_send()

    @pl.when(lat > 0)
    def _():
        edge_dn().wait_send()
        rows_dn().wait_send()
        sides_dn().wait_send()


def combine(rows, V, coef_ref, x_out, r_out, x_ref, r_ref, sem):
    coef = [coef_ref[i : i + 1, :] for i in range(2 * ITERS + 1)]
    coef = [jnp.broadcast_to(c, (rows, LANES)) for c in coef]
    field, residual = coef[:ITERS], coef[ITERS:]
    width = COLS_DEV // CHUNKS

    def copies(c):
        cols = pl.ds(c * width, width)
        return (
            pltpu.make_async_copy(x_ref.at[:, cols], x_out.at[:, cols], sem.at[0, c]),
            pltpu.make_async_copy(r_ref.at[:, cols], r_out.at[:, cols], sem.at[1, c]),
        )

    for c in range(CHUNKS):

        def one(b, carry):
            v = V[0, 8 : rows + 8, pl.ds(pl.multiple_of((b + 1) * LANES, LANES), LANES)]
            x, r = field[0] * v, residual[0] * v
            for k in range(1, ITERS + 1):
                v = V[k, 8 : rows + 8, pl.ds(pl.multiple_of((b + 1) * LANES, LANES), LANES)]
                r = r + residual[k] * v
                if k < ITERS:
                    x = x + field[k] * v
            cols = pl.ds(pl.multiple_of(b * LANES, LANES), LANES)
            x_ref[:, cols] = x
            r_ref[:, cols] = r
            return carry

        per = width // LANES
        lax.fori_loop(c * per, (c + 1) * per, one, 0, unroll=8)
        for copy in copies(c):
            copy.start()
    for c in range(CHUNKS):
        for copy in copies(c):
            copy.wait()


def body(n, lats, piece_height, piece_weight, piece_column, piece_width):
    pieces, rows, width = piece_height.shape
    ext = COLS_DEV + 2 * LANES
    vmem = pltpu.VMEM
    dma = pltpu.SemaphoreType.DMA
    scratch = [
        pltpu.SMEM((pieces,), jnp.int32),
        pltpu.SMEM((pieces,), jnp.int32),
        vmem((pieces, rows, LANES), F32),
        vmem((pieces, rows, LANES), F32),
        vmem((n, 2 * rows, LANES), F32),
        vmem((n, 2 * rows + 8, LANES), F32),
        vmem((n, 2 * rows, LANES), F32),
        vmem((n, 2 * rows + 8, LANES), F32),
        vmem((n, 1, LANES), jnp.int32),
        vmem((n, 1, LANES), jnp.int32),
        pltpu.SMEM((n, 1, LANES), jnp.int32),
        pltpu.SMEM((n, 4), jnp.int32),
        vmem((2, pieces, LANES), F32),
        vmem((2, pieces, LANES), F32),
        vmem((pieces, LANES), F32),
        vmem((pieces, LANES), F32),
        pltpu.SMEM((2 * n,), jnp.int32),
        pltpu.SMEM((2 * n,), jnp.int32),
        vmem((1, LANES), jnp.int32),
        pltpu.SMEM((1, LANES), jnp.int32),
        vmem((2 * n + 1, 6 * rows + 8, LANES), F32),
        vmem((rows + 16, ext), F32),
        vmem((rows, LANES), F32),
        vmem((rows, LANES), F32),
        vmem((rows, LANES), F32),
        vmem((rows, LANES), F32),
        vmem((8, COLS_DEV), F32),
        vmem((8, COLS_DEV), F32),
        vmem((8, COLS_DEV), F32),
        vmem((8, COLS_DEV), F32),
        vmem((8, 3 * LANES), F32),
        vmem((8, 3 * LANES), F32),
        vmem((8, 3 * LANES), F32),
        vmem((8, 3 * LANES), F32),
        vmem((1, LANES), F32),
        vmem((n * lats, 1, LANES), F32),
        dma((2, n)),
        dma((2, n)),
        dma((2, n)),
        dma((4,)),
        dma((4,)),
        dma((8,)),
        dma((2, n * lats)),
        dma((6,)),
    ]
    basis, coef = pl.pallas_call(
        functools.partial(kernel, n, lats, pieces, rows),
        out_shape=(
            jax.ShapeDtypeStruct((ITERS + 1, rows + 16, ext), F32),
            jax.ShapeDtypeStruct((16, LANES), F32),
        ),
        in_specs=[pl.BlockSpec(memory_space=pltpu.HBM)] * 4,
        out_specs=(pl.BlockSpec(memory_space=pltpu.VMEM),) * 2,
        scratch_shapes=scratch,
        compiler_params=pltpu.CompilerParams(
            collective_id=0, has_side_effects=True, vmem_limit_bytes=48 * 1024 * 1024
        ),
    )(*(pltpu.with_memory_space_constraint(a, pltpu.HBM) for a in (piece_column, piece_width, piece_height, piece_weight)))
    out = jax.ShapeDtypeStruct((rows, COLS_DEV), F32)
    return pl.pallas_call(
        functools.partial(combine, rows),
        out_shape=(out, out),
        in_specs=[pl.BlockSpec(memory_space=pltpu.VMEM)] * 2,
        out_specs=(pl.BlockSpec(memory_space=pltpu.HBM),) * 2,
        scratch_shapes=[
            vmem((rows, COLS_DEV), F32),
            vmem((rows, COLS_DEV), F32),
            dma((2, CHUNKS)),
        ],
        compiler_params=pltpu.CompilerParams(vmem_limit_bytes=16 * 1024 * 1024),
    )(basis, coef)


def solution(mesh):
    return jax.shard_map(
        functools.partial(body, mesh.shape["lon"], mesh.shape["lat"]),
        mesh=mesh,
        in_specs=(P("lon", "lat", None), P("lon", "lat", None), P("lon"), P("lon")),
        out_specs=(P("lat", "lon"), P("lat", "lon")),
        check_vma=False,
    )
```

```python
import functools

import jax
import jax.numpy as jnp
from jax import lax
from jax.experimental import pallas as pl
from jax.experimental.pallas import tpu as pltpu
from jax.sharding import PartitionSpec as P

COLS_DEV = 4096
ITERS = 4
MU_DATA = 0.5
DAMPING = 0.5
RIDGE = 0.05
SHIFT = 5.0
SCALE = 5.0

LANES = 128
CHUNKS = 4
MESH = pl.DeviceIdType.MESH
F32 = jnp.float32


def remote(src, dst, send, recv, device):
    return pltpu.make_async_remote_copy(
        src_ref=src, dst_ref=dst, send_sem=send, recv_sem=recv,
        device_id=device, device_id_type=MESH,
    )


def each(low, high):
    def run(step):
        if high - low <= 32:
            for i in range(low, high):
                step(i)
        else:
            pl.loop(low, high)(step)

    return run


def cg_coefficients(mu):
    def inner(a, b):
        total = None
        for i, x in enumerate(a):
            for j, y in enumerate(b):
                term = x * y * mu[i + j]
                total = term if total is None else total + term
        return total

    def apply(c):
        out = [SHIFT * x for x in c] + [jnp.zeros_like(c[0])]
        for i, x in enumerate(c):
            out[i + 1] = out[i + 1] + SCALE * x
        return out

    def add_scaled(y, a, x):
        out = []
        for i in range(max(len(x), len(y))):
            if i >= len(y):
                out.append(a * x[i])
            elif i >= len(x):
                out.append(y[i])
            else:
                out.append(y[i] + a * x[i])
        return out

    one = jnp.ones_like(mu[0])
    residual, direction, field = [one], [one], []
    norm = mu[0]
    for step in range(ITERS):
        image = apply(direction)
        alpha = norm / inner(direction, image)
        field = add_scaled(field, alpha, direction)
        residual = add_scaled(residual, -alpha, image)
        if step < ITERS - 1:
            fresh = inner(residual, residual)
            direction = add_scaled(residual, fresh / norm, direction)
            norm = fresh
    return field, residual


def kernel(
    n, lats, pieces, rows,
    col_in, wid_in, h_in, w_in, V, coef_ref,
    col_ref, wid_ref, h_ref, w_ref,
    hs, ws, hr, wr, ms, mr, msm, idx_s, up_s, up_r, dn_s, dn_r,
    blk_s, prev_s, last_v, last_s, S,
    D, east_s, east_r, west_s, west_r, lat_up_s, lat_up_r, lat_dn_s, lat_dn_r,
    side_up_s, side_up_r, side_dn_s, side_dn_r,
    red, rb,
    sem_m, sem_h, sem_w, sem_e, sem_l, sem_t, sem_b, sem_loc,
):
    lon = lax.axis_index("lon")
    lat = lax.axis_index("lat")
    blocks = COLS_DEV // LANES
    ext = blocks + 2
    top = rows + 8
    slots = 2 * n
    lane = lax.broadcasted_iota(jnp.int32, (rows, LANES), 1)
    lane1 = lax.broadcasted_iota(jnp.int32, (1, LANES), 1)

    def lon_at(k):
        return lax.rem(lon + k, n)

    turns, bit = [], 1
    while bit < n:
        turns.append((1 - 2 * (lon // bit % 2)) * bit)
        bit *= 2

    def partner(k):
        other = lon
        for i, turn in enumerate(turns):
            if isinstance(k, int):
                other = other + turn if k >> i & 1 else other
            else:
                other = other + k // 2**i % 2 * turn
        return other

    def lat_at(k):
        if isinstance(k, int) and k == 0:
            return lat
        moved = lat + k
        return jnp.where(moved >= lats, moved - lats, moved)

    barrier = pltpu.get_barrier_semaphore()
    loads = [
        pltpu.make_async_copy(src, dst, sem_loc.at[2 + i])
        for i, (src, dst) in enumerate(
            ((col_in, col_ref), (wid_in, wid_ref), (h_in, h_ref), (w_in, w_ref))
        )
    ]
    for load in loads:
        load.start()

    devices = n * lats

    def peer(j):
        return partner(j // lats), lat_at(j % lats)

    @each(1, devices)
    def _(j):
        pl.semaphore_signal(barrier, inc=1, device_id=peer(j), device_id_type=MESH)

    for load in loads:
        load.wait()

    @pl.loop(0, pieces)
    def _(i):
        up_s[0, pl.ds(i, 1), :] = h_ref[i, rows - 1 : rows, :]
        up_s[1, pl.ds(i, 1), :] = w_ref[i, rows - 1 : rows, :]
        dn_s[pl.ds(i, 1), :] = h_ref[i, 0:1, :]

    def fill(k, h_to, w_to, m_to):
        dest = partner(k)

        def scan(i, found):
            first, second = found
            match = (col_ref[i] >> 12) == dest
            second = jnp.where(match & (first >= 0) & (second < 0), i, second)
            first = jnp.where(match & (first < 0), i, first)
            return first, second

        found = lax.fori_loop(0, pieces, scan, (jnp.int32(-1), jnp.int32(-1)), unroll=8)
        tags = []
        for q in range(2):
            at = jnp.maximum(found[q], 0)
            limit = jnp.where(found[q] >= 0, wid_ref[at], 0)
            tags.append(jnp.where(found[q] >= 0, (col_ref[at] >> 7) & (blocks - 1), -1))
            idx_s[k, q] = at
            idx_s[k, 2 + q] = limit
            h_to[k, q * rows : (q + 1) * rows, :] = h_ref[at]
            w_to[k, q * rows : (q + 1) * rows, :] = jnp.where(lane < limit, w_ref[at], 0.0)
        m_to[k] = jnp.where(lane1 == 0, tags[0], jnp.where(lane1 == 1, tags[1], -1))

    far = n // 2

    @each(0, far)
    def _(i):
        fill(n - 1 - i, hs, ws, ms)

    pl.semaphore_wait(barrier, devices - 1)

    def edge_up():
        return remote(up_s, up_r, sem_e.at[0], sem_e.at[1], (lon, lat_at(1)))

    def edge_dn():
        return remote(dn_s, dn_r, sem_e.at[2], sem_e.at[3], (lon, lat_at(lats - 1)))

    def meta(k):
        return remote(ms.at[k], mr.at[k], sem_m.at[0, k], sem_m.at[1, k], (partner(k), lat))

    def heights(k):
        return remote(hs.at[k], hr.at[k], sem_h.at[0, k], sem_h.at[1, k], (partner(k), lat))

    def weights(k):
        return remote(ws.at[k], wr.at[k], sem_w.at[0, k], sem_w.at[1, k], (partner(k), lat))

    @pl.when(lat < lats - 1)
    def _():
        edge_up().start()

    @pl.when(lat > 0)
    def _():
        edge_dn().start()

    @each(0, far)
    def _(i):
        meta(n - 1 - i).start()
        heights(n - 1 - i).start()

    @each(far, n - 1)
    def _(i):
        fill(n - 1 - i, hs, ws, ms)
        meta(n - 1 - i).start()
        heights(n - 1 - i).start()

    fill(0, hr, wr, mr)

    @pl.when(lat > 0)
    def _():
        edge_up().wait_recv()

    @pl.when(lat == 0)
    def _():
        up_r[...] = jnp.zeros_like(up_r)

    @pl.when(lat < lats - 1)
    def _():
        edge_dn().wait_recv()

    @pl.when(lat == lats - 1)
    def _():
        dn_r[...] = jnp.zeros_like(dn_r)

    def extras(k, w_to):
        for q in range(2):
            at, limit = idx_s[k, q], idx_s[k, 2 + q]
            base = 2 * rows + q
            w_to[k, base : base + 1, :] = dn_r[pl.ds(at, 1), :]
            w_to[k, base + 2 : base + 3, :] = up_r[0, pl.ds(at, 1), :]
            w_to[k, base + 4 : base + 5, :] = jnp.where(lane1 < limit, up_r[1, pl.ds(at, 1), :], 0.0)
        w_to[k, 2 * rows + 6 : 2 * rows + 8, :] = jnp.zeros((2, LANES), F32)

    @each(1, n)
    def _(k):
        extras(n - k, ws)
        weights(n - k).start()

    extras(0, wr)

    @each(1, n)
    def _(k):
        meta(k).wait_recv()

    tags_in = pltpu.make_async_copy(mr, msm, sem_loc.at[0])
    tags_in.start()
    tags_in.wait()

    blk_s[0] = msm[0, 0, 0]
    blk_s[1] = msm[0, 0, 1]

    @each(1, n)
    def _(i):
        blk_s[2 * i] = msm[n - i, 0, 0]
        blk_s[2 * i + 1] = msm[n - i, 0, 1]

    def latest(p, last):
        tag = blk_s[p]

        def scan(j, found):
            return jnp.where((j < p) & (blk_s[j] == tag), j, found)

        prev_s[p] = lax.fori_loop(0, slots, scan, jnp.int32(slots), unroll=8)
        return jnp.where(lane1 == tag, p, last)

    nowhere = jnp.full((1, LANES), slots, jnp.int32)
    if slots <= 16:
        tags = [blk_s[p] for p in range(slots)]
        for p, tag in enumerate(tags):
            found = jnp.int32(slots)
            for j in range(p):
                found = jnp.where(tags[j] == tag, j, found)
            prev_s[p] = found
            nowhere = jnp.where(lane1 == tag, p, nowhere)
        last_v[...] = nowhere
    else:
        last_v[...] = lax.fori_loop(0, slots, latest, nowhere)
    last_in = pltpu.make_async_copy(last_v, last_s, sem_loc.at[1])
    last_in.start()
    last_in.wait()

    S[slots] = jnp.zeros((6 * rows + 8, LANES), F32)
    row_global = lat * rows + lax.broadcasted_iota(jnp.int32, (rows, LANES), 0)
    has_north = row_global < lats * rows - 1
    row_in = lax.broadcasted_iota(jnp.int32, (rows, LANES), 0)

    def terms(k, place):
        for q in range(2):
            p = 2 * place + q
            before = prev_s[p]
            h = hr[k, q * rows : (q + 1) * rows, :]
            w = wr[k, q * rows : (q + 1) * rows, :]
            base = 2 * rows + q
            above = wr[k, base : base + 1, :]
            below_h = wr[k, base + 2 : base + 3, :]
            below_w = wr[k, base + 4 : base + 5, :]
            h_north = jnp.where(row_in == rows - 1, above, pltpu.roll(h, rows - 1, 0))
            h_east = pltpu.roll(h, LANES - 1, 1)
            w_east = jnp.where((pltpu.roll(w, LANES - 1, 1) > 0.0) & (lane < LANES - 1), w, 0.0)
            w_north = jnp.where(has_north, w, 0.0)
            parts = (w, w * h, w_east, w_east * (h_east - h), w_north, w_north * (h_north - h))
            for t, part in enumerate(parts):
                at = pl.ds(t * rows, rows)
                S[p, at, :] = part + S[before, at, :]
            at = 6 * rows
            S[p, at : at + 1, :] = below_w + S[before, at : at + 1, :]
            S[p, at + 1 : at + 2, :] = below_w * (h[0:1, :] - below_h) + S[before, at + 1 : at + 2, :]

    terms(0, 0)

    @each(1, n)
    def _(i):
        heights(n - i).wait_recv()
        weights(n - i).wait_recv()
        terms(n - i, i)

    inv = 1.0 / SCALE

    def assemble(b, before):
        p = last_s[0, b]

        def field(t):
            return S[p, t * rows : (t + 1) * rows, :]

        at = 6 * rows
        t_east = field(3) / (field(2) + DAMPING)
        t_north = field(5) / (field(4) + DAMPING)
        t_below = S[p, at + 1 : at + 2, :] / (S[p, at : at + 1, :] + DAMPING)
        t_south = jnp.where(row_in == 0, t_below, pltpu.roll(t_north, 1, 0))
        rolled = pltpu.roll(t_east, 1, 1)
        t_west = jnp.where(lane == 0, before, rolled)
        right = MU_DATA * field(1) - (t_east - t_west) - (t_north - t_south)
        cols = pl.ds(pl.multiple_of((b + 1) * LANES, LANES), LANES)
        V[0, 8:top, cols] = right
        D[8:top, cols] = (MU_DATA * field(0) + (RIDGE + 4.0 - SHIFT)) * inv
        return rolled

    east_last = lax.fori_loop(0, blocks, assemble, jnp.zeros((rows, LANES), F32), unroll=8)

    first = slice(LANES, 2 * LANES)
    final = slice(blocks * LANES, (blocks + 1) * LANES)
    east_s[...] = jnp.where(
        lane >= LANES - 4,
        V[0, 8:top, final],
        jnp.where(
            lane >= LANES - 8,
            pltpu.roll(D[8:top, final], LANES - 4, 1),
            pltpu.roll(east_last, LANES - 9, 1),
        ),
    )
    west_s[...] = jnp.where(lane < 4, V[0, 8:top, first], pltpu.roll(D[8:top, first], 4, 1))
    east = remote(east_s, east_r, sem_l.at[0], sem_l.at[1], (lon_at(1), lat))
    west = remote(west_s, west_r, sem_l.at[2], sem_l.at[3], (lon_at(n - 1), lat))
    east.start()
    west.start()

    inner = slice(LANES, (blocks + 1) * LANES)
    lat_up_s[0:4, :] = D[top - 4 : top, inner]
    lat_up_s[4:8, :] = V[0, top - 4 : top, inner]
    lat_dn_s[0:4, :] = V[0, 8:12, inner]
    lat_dn_s[4:8, :] = D[8:12, inner]

    def rows_up():
        return remote(lat_up_s, lat_up_r, sem_t.at[0], sem_t.at[1], (lon, lat_at(1)))

    def rows_dn():
        return remote(lat_dn_s, lat_dn_r, sem_t.at[2], sem_t.at[3], (lon, lat_at(lats - 1)))

    def sides_up():
        return remote(side_up_s, side_up_r, sem_t.at[4], sem_t.at[5], (lon, lat_at(1)))

    def sides_dn():
        return remote(side_dn_s, side_dn_r, sem_t.at[6], sem_t.at[7], (lon, lat_at(lats - 1)))

    @pl.when(lat < lats - 1)
    def _():
        rows_up().start()

    @pl.when(lat > 0)
    def _():
        rows_dn().start()

    halo_w = slice(0, LANES)
    halo_e = slice((blocks + 1) * LANES, (blocks + 2) * LANES)
    east.wait_recv()
    got_east = east_r[...]
    V[0, 8:top, halo_w] = got_east
    D[8:top, halo_w] = pltpu.roll(got_east, 4, 1)
    V[0, 8:top, first] = V[0, 8:top, first] + jnp.where(lane == 0, pltpu.roll(got_east, 9, 1), 0.0)
    west.wait_recv()
    got_west = west_r[...]
    V[0, 8:top, halo_e] = got_west + jnp.where(lane == 0, east_last, 0.0)
    D[8:top, halo_e] = pltpu.roll(got_west, LANES - 4, 1)
    side_blocks = (halo_w, first, halo_e)
    for i, cols in enumerate(side_blocks):
        to = slice(i * LANES, (i + 1) * LANES)
        side_up_s[0:4, to] = D[top - 4 : top, cols]
        side_up_s[4:8, to] = V[0, top - 4 : top, cols]
        side_dn_s[0:4, to] = V[0, 8:12, cols]
        side_dn_s[4:8, to] = D[8:12, cols]

    @pl.when(lat < lats - 1)
    def _():
        sides_up().start()

    @pl.when(lat > 0)
    def _():
        sides_dn().start()

    def mirror(k):
        @pl.when(lat == 0)
        def _():
            V[k, 7:8, :] = V[k, 8:9, :]

        @pl.when(lat == lats - 1)
        def _():
            V[k, top : top + 1, :] = V[k, top - 1 : top, :]

    @pl.when(lat > 0)
    def _():
        rows_up().wait_recv()
        got = lat_up_r[...]
        V[0, 0:8, inner] = got
        D[0:8, inner] = pltpu.roll(got, 4, 0)
        sides_up().wait_recv()
        for i, cols in enumerate(side_blocks):
            got = side_up_r[:, i * LANES : (i + 1) * LANES]
            V[0, 0:8, cols] = got
            D[0:8, cols] = pltpu.roll(got, 4, 0)

    @pl.when(lat == 0)
    def _():
        V[0, 0:8, :] = jnp.zeros((8, ext * LANES), F32)
        D[0:8, :] = jnp.zeros((8, ext * LANES), F32)

    @pl.when(lat < lats - 1)
    def _():
        rows_dn().wait_recv()
        got = lat_dn_r[...]
        V[0, top : top + 8, inner] = got
        D[top : top + 8, inner] = pltpu.roll(got, 4, 0)
        sides_dn().wait_recv()
        for i, cols in enumerate(side_blocks):
            got = side_dn_r[:, i * LANES : (i + 1) * LANES]
            V[0, top : top + 8, cols] = got
            D[top : top + 8, cols] = pltpu.roll(got, 4, 0)

    @pl.when(lat == lats - 1)
    def _():
        V[0, top : top + 8, :] = jnp.zeros((8, ext * LANES), F32)
        D[top : top + 8, :] = jnp.zeros((8, ext * LANES), F32)

    mirror(0)

    tall = rows + 16
    lane_t = lax.broadcasted_iota(jnp.int32, (tall, LANES), 1)

    def at_block(b):
        return pl.ds(pl.multiple_of(b * LANES, LANES), LANES)

    def fold(value):
        total = value[0:8]
        for i in range(1, rows // 8):
            total = total + value[8 * i : 8 * i + 8]
        return total

    def apply(k):
        def one(b, here, before, ahead):
            nxt = V[k, :, at_block(jnp.minimum(b + 1, ext - 1))]
            ahead_next = pltpu.roll(nxt, LANES - 1, 1)
            rolled = pltpu.roll(here, 1, 1)
            sides = jnp.where(lane_t == 0, before, rolled)
            sides = sides + jnp.where(lane_t == LANES - 1, ahead_next, ahead)
            sides = sides + pltpu.roll(here, 1, 0) + pltpu.roll(here, tall - 1, 0)
            out = D[:, at_block(b)] * here - inv * sides
            V[k + 1, :, at_block(b)] = out
            return out, nxt, rolled, ahead_next

        def step(b, carry):
            here, before, ahead, cross, own, base = carry
            out, nxt, rolled, ahead_next = one(b, here, before, ahead)
            mine, image = here[8:top], out[8:top]
            cross = cross + fold(mine * image)
            own = own + fold(image * image)
            if k == 0:
                base = base + fold(mine * mine)
            return nxt, rolled, ahead_next, cross, own, base

        here = V[k, :, 0:LANES]
        ahead = pltpu.roll(here, LANES - 1, 1)
        _, here, before, ahead = one(0, here, ahead, ahead)
        zero = jnp.zeros((8, LANES), F32)
        here, before, ahead, cross, own, base = lax.fori_loop(
            1, blocks + 1, step, (here, before, ahead, zero, zero, zero), unroll=8
        )
        if k < ITERS - 1:
            one(ext - 1, here, before, ahead)
            mirror(k + 1)
        return cross, own, base

    sums = []
    for k in range(ITERS):
        cross, own, base = apply(k)
        if k == 0:
            sums.append(base)
        sums += [cross, own]

    mine = jnp.zeros((1, LANES), F32)
    for i, value in enumerate(sums):
        value = jnp.sum(jnp.sum(value, axis=0, keepdims=True), axis=1, keepdims=True)
        mine = jnp.where(lane1 == i, value, mine)
    red[...] = mine
    place = lon * lats + lat

    def share(j):
        return remote(red, rb.at[place], sem_b.at[0, j], sem_b.at[1, j], peer(j))

    @each(1, devices)
    def _(j):
        share(devices - j).start()

    rb[place] = mine

    @each(1, devices)
    def _(j):
        share(j).wait_recv()

    total = jnp.sum(rb[...], axis=0)
    mu = [
        jnp.broadcast_to(
            jnp.sum(jnp.where(lane1 == i, total, 0.0), axis=1, keepdims=True), (8, LANES)
        )
        for i in range(2 * ITERS + 1)
    ]
    field, residual = cg_coefficients(mu)
    for i, c in enumerate(field + residual):
        coef_ref[i : i + 1, :] = c[0:1, :]

    @each(1, n)
    def _(k):
        meta(k).wait_send()
        heights(k).wait_send()
        weights(k).wait_send()

    @each(1, devices)
    def _(j):
        share(j).wait_send()

    east.wait_send()
    west.wait_send()

    @pl.when(lat < lats - 1)
    def _():
        edge_up().wait_send()
        rows_up().wait_send()
        sides_up().wait_send()

    @pl.when(lat > 0)
    def _():
        edge_dn().wait_send()
        rows_dn().wait_send()
        sides_dn().wait_send()


def combine(rows, V, coef_ref, x_out, r_out, x_ref, r_ref, sem):
    coef = [coef_ref[i : i + 1, :] for i in range(2 * ITERS + 1)]
    coef = [jnp.broadcast_to(c, (rows, LANES)) for c in coef]
    field, residual = coef[:ITERS], coef[ITERS:]
    width = COLS_DEV // CHUNKS

    def copies(c):
        cols = pl.ds(c * width, width)
        return (
            pltpu.make_async_copy(x_ref.at[:, cols], x_out.at[:, cols], sem.at[0, c]),
            pltpu.make_async_copy(r_ref.at[:, cols], r_out.at[:, cols], sem.at[1, c]),
        )

    for c in range(CHUNKS):

        def one(b, carry):
            v = V[0, 8 : rows + 8, pl.ds(pl.multiple_of((b + 1) * LANES, LANES), LANES)]
            x, r = field[0] * v, residual[0] * v
            for k in range(1, ITERS + 1):
                v = V[k, 8 : rows + 8, pl.ds(pl.multiple_of((b + 1) * LANES, LANES), LANES)]
                r = r + residual[k] * v
                if k < ITERS:
                    x = x + field[k] * v
            cols = pl.ds(pl.multiple_of(b * LANES, LANES), LANES)
            x_ref[:, cols] = x
            r_ref[:, cols] = r
            return carry

        per = width // LANES
        lax.fori_loop(c * per, (c + 1) * per, one, 0, unroll=8)
        for copy in copies(c):
            copy.start()
    for c in range(CHUNKS):
        for copy in copies(c):
            copy.wait()


def body(n, lats, piece_height, piece_weight, piece_column, piece_width):
    pieces, rows, width = piece_height.shape
    ext = COLS_DEV + 2 * LANES
    vmem = pltpu.VMEM
    dma = pltpu.SemaphoreType.DMA
    scratch = [
        pltpu.SMEM((pieces,), jnp.int32),
        pltpu.SMEM((pieces,), jnp.int32),
        vmem((pieces, rows, LANES), F32),
        vmem((pieces, rows, LANES), F32),
        vmem((n, 2 * rows, LANES), F32),
        vmem((n, 2 * rows + 8, LANES), F32),
        vmem((n, 2 * rows, LANES), F32),
        vmem((n, 2 * rows + 8, LANES), F32),
        vmem((n, 1, LANES), jnp.int32),
        vmem((n, 1, LANES), jnp.int32),
        pltpu.SMEM((n, 1, LANES), jnp.int32),
        pltpu.SMEM((n, 4), jnp.int32),
        vmem((2, pieces, LANES), F32),
        vmem((2, pieces, LANES), F32),
        vmem((pieces, LANES), F32),
        vmem((pieces, LANES), F32),
        pltpu.SMEM((2 * n,), jnp.int32),
        pltpu.SMEM((2 * n,), jnp.int32),
        vmem((1, LANES), jnp.int32),
        pltpu.SMEM((1, LANES), jnp.int32),
        vmem((2 * n + 1, 6 * rows + 8, LANES), F32),
        vmem((rows + 16, ext), F32),
        vmem((rows, LANES), F32),
        vmem((rows, LANES), F32),
        vmem((rows, LANES), F32),
        vmem((rows, LANES), F32),
        vmem((8, COLS_DEV), F32),
        vmem((8, COLS_DEV), F32),
        vmem((8, COLS_DEV), F32),
        vmem((8, COLS_DEV), F32),
        vmem((8, 3 * LANES), F32),
        vmem((8, 3 * LANES), F32),
        vmem((8, 3 * LANES), F32),
        vmem((8, 3 * LANES), F32),
        vmem((1, LANES), F32),
        vmem((n * lats, 1, LANES), F32),
        dma((2, n)),
        dma((2, n)),
        dma((2, n)),
        dma((4,)),
        dma((4,)),
        dma((8,)),
        dma((2, n * lats)),
        dma((6,)),
    ]
    basis, coef = pl.pallas_call(
        functools.partial(kernel, n, lats, pieces, rows),
        out_shape=(
            jax.ShapeDtypeStruct((ITERS + 1, rows + 16, ext), F32),
            jax.ShapeDtypeStruct((16, LANES), F32),
        ),
        in_specs=[pl.BlockSpec(memory_space=pltpu.HBM)] * 4,
        out_specs=(pl.BlockSpec(memory_space=pltpu.VMEM),) * 2,
        scratch_shapes=scratch,
        compiler_params=pltpu.CompilerParams(
            collective_id=0, has_side_effects=True, vmem_limit_bytes=48 * 1024 * 1024
        ),
    )(*(pltpu.with_memory_space_constraint(a, pltpu.HBM) for a in (piece_column, piece_width, piece_height, piece_weight)))
    out = jax.ShapeDtypeStruct((rows, COLS_DEV), F32)
    return pl.pallas_call(
        functools.partial(combine, rows),
        out_shape=(out, out),
        in_specs=[pl.BlockSpec(memory_space=pltpu.VMEM)] * 2,
        out_specs=(pl.BlockSpec(memory_space=pltpu.HBM),) * 2,
        scratch_shapes=[
            vmem((rows, COLS_DEV), F32),
            vmem((rows, COLS_DEV), F32),
            dma((2, CHUNKS)),
        ],
        compiler_params=pltpu.CompilerParams(vmem_limit_bytes=16 * 1024 * 1024),
    )(basis, coef)


def solution(mesh):
    return jax.shard_map(
        functools.partial(body, mesh.shape["lon"], mesh.shape["lat"]),
        mesh=mesh,
        in_specs=(P("lon", "lat", None), P("lon", "lat", None), P("lon"), P("lon")),
        out_specs=(P("lat", "lon"), P("lat", "lon")),
        check_vma=False,
    )
```

```python
import functools

import jax
import jax.numpy as jnp
from jax import lax
from jax.experimental import pallas as pl
from jax.experimental.pallas import tpu as pltpu
from jax.sharding import PartitionSpec as P

COLS_DEV = 4096
ITERS = 4
MU_DATA = 0.5
DAMPING = 0.5
RIDGE = 0.05
SHIFT = 5.0
SCALE = 5.0

LANES = 128
CHUNKS = 4
MESH = pl.DeviceIdType.MESH
F32 = jnp.float32


def remote(src, dst, send, recv, device):
    return pltpu.make_async_remote_copy(
        src_ref=src, dst_ref=dst, send_sem=send, recv_sem=recv,
        device_id=device, device_id_type=MESH,
    )


def each(low, high):
    def run(step):
        if high - low <= 8:
            for i in range(low, high):
                step(i)
        else:
            pl.loop(low, high)(step)

    return run


def cg_coefficients(mu):
    def inner(a, b):
        total = None
        for i, x in enumerate(a):
            for j, y in enumerate(b):
                term = x * y * mu[i + j]
                total = term if total is None else total + term
        return total

    def apply(c):
        out = [SHIFT * x for x in c] + [jnp.zeros_like(c[0])]
        for i, x in enumerate(c):
            out[i + 1] = out[i + 1] + SCALE * x
        return out

    def add_scaled(y, a, x):
        out = []
        for i in range(max(len(x), len(y))):
            if i >= len(y):
                out.append(a * x[i])
            elif i >= len(x):
                out.append(y[i])
            else:
                out.append(y[i] + a * x[i])
        return out

    one = jnp.ones_like(mu[0])
    residual, direction, field = [one], [one], []
    norm = mu[0]
    for step in range(ITERS):
        image = apply(direction)
        alpha = norm / inner(direction, image)
        field = add_scaled(field, alpha, direction)
        residual = add_scaled(residual, -alpha, image)
        if step < ITERS - 1:
            fresh = inner(residual, residual)
            direction = add_scaled(residual, fresh / norm, direction)
            norm = fresh
    return field, residual


def kernel(
    n, lats, pieces, rows,
    col_in, wid_in, h_in, w_in, V, coef_ref,
    col_ref, wid_ref, h_ref, w_ref,
    hs, ws, hr, wr, ms, mr, msm, idx_s, up_s, up_r, dn_s, dn_r,
    blk_s, prev_s, last_v, last_s, S,
    D, east_s, east_r, west_s, west_r, lat_up_s, lat_up_r, lat_dn_s, lat_dn_r,
    side_up_s, side_up_r, side_dn_s, side_dn_r,
    red, rb, acc,
    sem_m, sem_h, sem_w, sem_e, sem_l, sem_t, sem_b, sem_loc,
):
    lon = lax.axis_index("lon")
    lat = lax.axis_index("lat")
    blocks = COLS_DEV // LANES
    ext = blocks + 2
    top = rows + 8
    slots = 2 * n
    lane = lax.broadcasted_iota(jnp.int32, (rows, LANES), 1)
    lane1 = lax.broadcasted_iota(jnp.int32, (1, LANES), 1)

    def lon_at(k):
        return lax.rem(lon + k, n)

    turns, bit = [], 1
    while bit < n:
        turns.append((1 - 2 * (lon // bit % 2)) * bit)
        bit *= 2

    def partner(k):
        other = lon
        for i, turn in enumerate(turns):
            if isinstance(k, int):
                other = other + turn if k >> i & 1 else other
            else:
                other = other + k // 2**i % 2 * turn
        return other

    def lat_at(k):
        if isinstance(k, int) and k == 0:
            return lat
        moved = lat + k
        return jnp.where(moved >= lats, moved - lats, moved)

    barrier = pltpu.get_barrier_semaphore()
    loads = [
        pltpu.make_async_copy(src, dst, sem_loc.at[2 + i])
        for i, (src, dst) in enumerate(
            ((col_in, col_ref), (wid_in, wid_ref), (h_in, h_ref), (w_in, w_ref))
        )
    ]
    for load in loads:
        load.start()

    devices = n * lats

    def all_peers(step):
        each(1, n)(lambda k: step(k * lats, (partner(k), lat)))

        @pl.loop(1, lats)
        def _(m):
            each(0, n)(lambda k: step(k * lats + m, (partner(k), lat_at(m))))

    all_peers(
        lambda j, device: pl.semaphore_signal(barrier, inc=1, device_id=device, device_id_type=MESH)
    )

    for load in loads:
        load.wait()

    @pl.loop(0, pieces)
    def _(i):
        up_s[0, pl.ds(i, 1), :] = h_ref[i, rows - 1 : rows, :]
        up_s[1, pl.ds(i, 1), :] = w_ref[i, rows - 1 : rows, :]
        dn_s[pl.ds(i, 1), :] = h_ref[i, 0:1, :]

    def fill(k, h_to, w_to, m_to):
        dest = partner(k)

        def scan(i, found):
            first, second = found
            match = (col_ref[i] >> 12) == dest
            second = jnp.where(match & (first >= 0) & (second < 0), i, second)
            first = jnp.where(match & (first < 0), i, first)
            return first, second

        found = lax.fori_loop(0, pieces, scan, (jnp.int32(-1), jnp.int32(-1)), unroll=8)
        tags = []
        for q in range(2):
            at = jnp.maximum(found[q], 0)
            limit = jnp.where(found[q] >= 0, wid_ref[at], 0)
            tags.append(jnp.where(found[q] >= 0, (col_ref[at] >> 7) & (blocks - 1), -1))
            idx_s[k, q] = at
            idx_s[k, 2 + q] = limit
            h_to[k, q * rows : (q + 1) * rows, :] = h_ref[at]
            w_to[k, q * rows : (q + 1) * rows, :] = jnp.where(lane < limit, w_ref[at], 0.0)
        m_to[k] = jnp.where(lane1 == 0, tags[0], jnp.where(lane1 == 1, tags[1], -1))

    far = n // 2

    @each(0, far)
    def _(i):
        fill(n - 1 - i, hs, ws, ms)

    pl.semaphore_wait(barrier, devices - 1)

    def edge_up():
        return remote(up_s, up_r, sem_e.at[0], sem_e.at[1], (lon, lat_at(1)))

    def edge_dn():
        return remote(dn_s, dn_r, sem_e.at[2], sem_e.at[3], (lon, lat_at(lats - 1)))

    def meta(k):
        return remote(ms.at[k], mr.at[k], sem_m.at[0, k], sem_m.at[1, k], (partner(k), lat))

    def heights(k):
        return remote(hs.at[k], hr.at[k], sem_h.at[0, k], sem_h.at[1, k], (partner(k), lat))

    def weights(k):
        return remote(ws.at[k], wr.at[k], sem_w.at[0, k], sem_w.at[1, k], (partner(k), lat))

    @pl.when(lat < lats - 1)
    def _():
        edge_up().start()

    @pl.when(lat > 0)
    def _():
        edge_dn().start()

    @each(0, far)
    def _(i):
        meta(n - 1 - i).start()
        heights(n - 1 - i).start()

    @each(far, n - 1)
    def _(i):
        fill(n - 1 - i, hs, ws, ms)
        meta(n - 1 - i).start()
        heights(n - 1 - i).start()

    fill(0, hr, wr, mr)

    @pl.when(lat > 0)
    def _():
        edge_up().wait_recv()

    @pl.when(lat == 0)
    def _():
        up_r[...] = jnp.zeros_like(up_r)

    @pl.when(lat < lats - 1)
    def _():
        edge_dn().wait_recv()

    @pl.when(lat == lats - 1)
    def _():
        dn_r[...] = jnp.zeros_like(dn_r)

    def extras(k, w_to):
        for q in range(2):
            at, limit = idx_s[k, q], idx_s[k, 2 + q]
            base = 2 * rows + q
            w_to[k, base : base + 1, :] = dn_r[pl.ds(at, 1), :]
            w_to[k, base + 2 : base + 3, :] = up_r[0, pl.ds(at, 1), :]
            w_to[k, base + 4 : base + 5, :] = jnp.where(lane1 < limit, up_r[1, pl.ds(at, 1), :], 0.0)
        w_to[k, 2 * rows + 6 : 2 * rows + 8, :] = jnp.zeros((2, LANES), F32)

    @each(1, n)
    def _(k):
        extras(n - k, ws)
        weights(n - k).start()

    extras(0, wr)

    @each(1, n)
    def _(k):
        meta(k).wait_recv()

    tags_in = pltpu.make_async_copy(mr, msm, sem_loc.at[0])
    tags_in.start()
    tags_in.wait()

    blk_s[0] = msm[0, 0, 0]
    blk_s[1] = msm[0, 0, 1]

    @each(1, n)
    def _(i):
        blk_s[2 * i] = msm[n - i, 0, 0]
        blk_s[2 * i + 1] = msm[n - i, 0, 1]

    def latest(p, last):
        tag = blk_s[p]

        def scan(j, found):
            return jnp.where((j < p) & (blk_s[j] == tag), j, found)

        prev_s[p] = lax.fori_loop(0, slots, scan, jnp.int32(slots), unroll=8)
        return jnp.where(lane1 == tag, p, last)

    nowhere = jnp.full((1, LANES), slots, jnp.int32)
    if slots <= 16:
        tags = [blk_s[p] for p in range(slots)]
        for p, tag in enumerate(tags):
            found = jnp.int32(slots)
            for j in range(p):
                found = jnp.where(tags[j] == tag, j, found)
            prev_s[p] = found
            nowhere = jnp.where(lane1 == tag, p, nowhere)
        last_v[...] = nowhere
    else:
        last_v[...] = lax.fori_loop(0, slots, latest, nowhere)
    last_in = pltpu.make_async_copy(last_v, last_s, sem_loc.at[1])
    last_in.start()
    last_in.wait()

    S[slots] = jnp.zeros((6 * rows + 8, LANES), F32)
    row_global = lat * rows + lax.broadcasted_iota(jnp.int32, (rows, LANES), 0)
    has_north = row_global < lats * rows - 1
    row_in = lax.broadcasted_iota(jnp.int32, (rows, LANES), 0)

    def terms(k, place):
        for q in range(2):
            p = 2 * place + q
            before = prev_s[p]
            h = hr[k, q * rows : (q + 1) * rows, :]
            w = wr[k, q * rows : (q + 1) * rows, :]
            base = 2 * rows + q
            above = wr[k, base : base + 1, :]
            below_h = wr[k, base + 2 : base + 3, :]
            below_w = wr[k, base + 4 : base + 5, :]
            h_north = jnp.where(row_in == rows - 1, above, pltpu.roll(h, rows - 1, 0))
            h_east = pltpu.roll(h, LANES - 1, 1)
            w_east = jnp.where((pltpu.roll(w, LANES - 1, 1) > 0.0) & (lane < LANES - 1), w, 0.0)
            w_north = jnp.where(has_north, w, 0.0)
            parts = (w, w * h, w_east, w_east * (h_east - h), w_north, w_north * (h_north - h))
            for t, part in enumerate(parts):
                at = pl.ds(t * rows, rows)
                S[p, at, :] = part + S[before, at, :]
            at = 6 * rows
            S[p, at : at + 1, :] = below_w + S[before, at : at + 1, :]
            S[p, at + 1 : at + 2, :] = below_w * (h[0:1, :] - below_h) + S[before, at + 1 : at + 2, :]

    terms(0, 0)

    @each(1, n)
    def _(i):
        heights(n - i).wait_recv()
        weights(n - i).wait_recv()
        terms(n - i, i)

    inv = 1.0 / SCALE

    def assemble(b, before):
        p = last_s[0, b]

        def field(t):
            return S[p, t * rows : (t + 1) * rows, :]

        at = 6 * rows
        t_east = field(3) / (field(2) + DAMPING)
        t_north = field(5) / (field(4) + DAMPING)
        t_below = S[p, at + 1 : at + 2, :] / (S[p, at : at + 1, :] + DAMPING)
        t_south = jnp.where(row_in == 0, t_below, pltpu.roll(t_north, 1, 0))
        rolled = pltpu.roll(t_east, 1, 1)
        t_west = jnp.where(lane == 0, before, rolled)
        right = MU_DATA * field(1) - (t_east - t_west) - (t_north - t_south)
        cols = pl.ds(pl.multiple_of((b + 1) * LANES, LANES), LANES)
        V[0, 8:top, cols] = right
        D[8:top, cols] = (MU_DATA * field(0) + (RIDGE + 4.0 - SHIFT)) * inv
        return rolled

    east_last = lax.fori_loop(0, blocks, assemble, jnp.zeros((rows, LANES), F32), unroll=4)

    first = slice(LANES, 2 * LANES)
    final = slice(blocks * LANES, (blocks + 1) * LANES)
    east_s[...] = jnp.where(
        lane >= LANES - 4,
        V[0, 8:top, final],
        jnp.where(
            lane >= LANES - 8,
            pltpu.roll(D[8:top, final], LANES - 4, 1),
            pltpu.roll(east_last, LANES - 9, 1),
        ),
    )
    west_s[...] = jnp.where(lane < 4, V[0, 8:top, first], pltpu.roll(D[8:top, first], 4, 1))
    east = remote(east_s, east_r, sem_l.at[0], sem_l.at[1], (lon_at(1), lat))
    west = remote(west_s, west_r, sem_l.at[2], sem_l.at[3], (lon_at(n - 1), lat))
    east.start()
    west.start()

    inner = slice(LANES, (blocks + 1) * LANES)
    lat_up_s[0:4, :] = D[top - 4 : top, inner]
    lat_up_s[4:8, :] = V[0, top - 4 : top, inner]
    lat_dn_s[0:4, :] = V[0, 8:12, inner]
    lat_dn_s[4:8, :] = D[8:12, inner]

    def rows_up():
        return remote(lat_up_s, lat_up_r, sem_t.at[0], sem_t.at[1], (lon, lat_at(1)))

    def rows_dn():
        return remote(lat_dn_s, lat_dn_r, sem_t.at[2], sem_t.at[3], (lon, lat_at(lats - 1)))

    def sides_up():
        return remote(side_up_s, side_up_r, sem_t.at[4], sem_t.at[5], (lon, lat_at(1)))

    def sides_dn():
        return remote(side_dn_s, side_dn_r, sem_t.at[6], sem_t.at[7], (lon, lat_at(lats - 1)))

    @pl.when(lat < lats - 1)
    def _():
        rows_up().start()

    @pl.when(lat > 0)
    def _():
        rows_dn().start()

    halo_w = slice(0, LANES)
    halo_e = slice((blocks + 1) * LANES, (blocks + 2) * LANES)
    east.wait_recv()
    got_east = east_r[...]
    V[0, 8:top, halo_w] = got_east
    D[8:top, halo_w] = pltpu.roll(got_east, 4, 1)
    V[0, 8:top, first] = V[0, 8:top, first] + jnp.where(lane == 0, pltpu.roll(got_east, 9, 1), 0.0)
    west.wait_recv()
    got_west = west_r[...]
    V[0, 8:top, halo_e] = got_west + jnp.where(lane == 0, east_last, 0.0)
    D[8:top, halo_e] = pltpu.roll(got_west, LANES - 4, 1)
    side_blocks = (halo_w, first, halo_e)
    for i, cols in enumerate(side_blocks):
        to = slice(i * LANES, (i + 1) * LANES)
        side_up_s[0:4, to] = D[top - 4 : top, cols]
        side_up_s[4:8, to] = V[0, top - 4 : top, cols]
        side_dn_s[0:4, to] = V[0, 8:12, cols]
        side_dn_s[4:8, to] = D[8:12, cols]

    @pl.when(lat < lats - 1)
    def _():
        sides_up().start()

    @pl.when(lat > 0)
    def _():
        sides_dn().start()

    def mirror(k):
        @pl.when(lat == 0)
        def _():
            V[k, 7:8, :] = V[k, 8:9, :]

        @pl.when(lat == lats - 1)
        def _():
            V[k, top : top + 1, :] = V[k, top - 1 : top, :]

    @pl.when(lat > 0)
    def _():
        rows_up().wait_recv()
        got = lat_up_r[...]
        V[0, 0:8, inner] = got
        D[0:8, inner] = pltpu.roll(got, 4, 0)
        sides_up().wait_recv()
        for i, cols in enumerate(side_blocks):
            got = side_up_r[:, i * LANES : (i + 1) * LANES]
            V[0, 0:8, cols] = got
            D[0:8, cols] = pltpu.roll(got, 4, 0)

    @pl.when(lat == 0)
    def _():
        V[0, 0:8, :] = jnp.zeros((8, ext * LANES), F32)
        D[0:8, :] = jnp.zeros((8, ext * LANES), F32)

    @pl.when(lat < lats - 1)
    def _():
        rows_dn().wait_recv()
        got = lat_dn_r[...]
        V[0, top : top + 8, inner] = got
        D[top : top + 8, inner] = pltpu.roll(got, 4, 0)
        sides_dn().wait_recv()
        for i, cols in enumerate(side_blocks):
            got = side_dn_r[:, i * LANES : (i + 1) * LANES]
            V[0, top : top + 8, cols] = got
            D[top : top + 8, cols] = pltpu.roll(got, 4, 0)

    @pl.when(lat == lats - 1)
    def _():
        V[0, top : top + 8, :] = jnp.zeros((8, ext * LANES), F32)
        D[top : top + 8, :] = jnp.zeros((8, ext * LANES), F32)

    mirror(0)

    tall = rows + 16
    lane_t = lax.broadcasted_iota(jnp.int32, (tall, LANES), 1)

    def at_block(b):
        return pl.ds(pl.multiple_of(b * LANES, LANES), LANES)

    def fold(value):
        total = value[0:8]
        for i in range(1, rows // 8):
            total = total + value[8 * i : 8 * i + 8]
        return total

    @pl.loop(0, ITERS)
    def _(k):
        def one(b, here, before, ahead):
            nxt = V[k, :, at_block(jnp.minimum(b + 1, ext - 1))]
            ahead_next = pltpu.roll(nxt, LANES - 1, 1)
            rolled = pltpu.roll(here, 1, 1)
            sides = jnp.where(lane_t == 0, before, rolled)
            sides = sides + jnp.where(lane_t == LANES - 1, ahead_next, ahead)
            sides = sides + pltpu.roll(here, 1, 0) + pltpu.roll(here, tall - 1, 0)
            out = D[:, at_block(b)] * here - inv * sides
            V[k + 1, :, at_block(b)] = out
            return out, nxt, rolled, ahead_next

        def step(b, carry):
            here, before, ahead, base, cross, own = carry
            out, nxt, rolled, ahead_next = one(b, here, before, ahead)
            mine, image = here[8:top], out[8:top]
            base = base + fold(mine * mine)
            cross = cross + fold(mine * image)
            own = own + fold(image * image)
            return nxt, rolled, ahead_next, base, cross, own

        here = V[k, :, 0:LANES]
        ahead = pltpu.roll(here, LANES - 1, 1)
        _, here, before, ahead = one(0, here, ahead, ahead)
        zero = jnp.zeros((8, LANES), F32)
        here, before, ahead, base, cross, own = lax.fori_loop(
            1, blocks + 1, step, (here, before, ahead, zero, zero, zero), unroll=4
        )
        one(ext - 1, here, before, ahead)
        mirror(k + 1)
        acc[2 * k] = base
        acc[2 * k + 1] = cross
        acc[2 * k + 2] = own

    mine = jnp.zeros((1, LANES), F32)
    for i in range(2 * ITERS + 1):
        value = jnp.sum(jnp.sum(acc[i], axis=0, keepdims=True), axis=1, keepdims=True)
        mine = jnp.where(lane1 == i, value, mine)
    red[...] = mine
    place = lon * lats + lat

    def share(j, device=(partner(1), lat)):
        return remote(red, rb.at[place], sem_b.at[0, j], sem_b.at[1, j], device)

    all_peers(lambda j, device: share(j, device).start())

    rb[place] = mine

    @each(1, devices)
    def _(j):
        share(j).wait_recv()

    total = jnp.sum(rb[...], axis=0)
    mu = [
        jnp.broadcast_to(
            jnp.sum(jnp.where(lane1 == i, total, 0.0), axis=1, keepdims=True), (8, LANES)
        )
        for i in range(2 * ITERS + 1)
    ]
    field, residual = cg_coefficients(mu)
    for i, c in enumerate(field + residual):
        coef_ref[i : i + 1, :] = c[0:1, :]

    @each(1, n)
    def _(k):
        meta(k).wait_send()
        heights(k).wait_send()
        weights(k).wait_send()

    @each(1, devices)
    def _(j):
        share(j).wait_send()

    east.wait_send()
    west.wait_send()

    @pl.when(lat < lats - 1)
    def _():
        edge_up().wait_send()
        rows_up().wait_send()
        sides_up().wait_send()

    @pl.when(lat > 0)
    def _():
        edge_dn().wait_send()
        rows_dn().wait_send()
        sides_dn().wait_send()


def combine(rows, V, coef_ref, x_out, r_out, x_ref, r_ref, sem):
    coef = [coef_ref[i : i + 1, :] for i in range(2 * ITERS + 1)]
    coef = [jnp.broadcast_to(c, (rows, LANES)) for c in coef]
    field, residual = coef[:ITERS], coef[ITERS:]
    width = COLS_DEV // CHUNKS

    def copies(c):
        cols = pl.ds(c * width, width)
        return (
            pltpu.make_async_copy(x_ref.at[:, cols], x_out.at[:, cols], sem.at[0, c]),
            pltpu.make_async_copy(r_ref.at[:, cols], r_out.at[:, cols], sem.at[1, c]),
        )

    for c in range(CHUNKS):

        def one(b, carry):
            v = V[0, 8 : rows + 8, pl.ds(pl.multiple_of((b + 1) * LANES, LANES), LANES)]
            x, r = field[0] * v, residual[0] * v
            for k in range(1, ITERS + 1):
                v = V[k, 8 : rows + 8, pl.ds(pl.multiple_of((b + 1) * LANES, LANES), LANES)]
                r = r + residual[k] * v
                if k < ITERS:
                    x = x + field[k] * v
            cols = pl.ds(pl.multiple_of(b * LANES, LANES), LANES)
            x_ref[:, cols] = x
            r_ref[:, cols] = r
            return carry

        per = width // LANES
        lax.fori_loop(c * per, (c + 1) * per, one, 0, unroll=4)
        for copy in copies(c):
            copy.start()
    for c in range(CHUNKS):
        for copy in copies(c):
            copy.wait()


def body(n, lats, piece_height, piece_weight, piece_column, piece_width):
    pieces, rows, width = piece_height.shape
    ext = COLS_DEV + 2 * LANES
    vmem = pltpu.VMEM
    dma = pltpu.SemaphoreType.DMA
    scratch = [
        pltpu.SMEM((pieces,), jnp.int32),
        pltpu.SMEM((pieces,), jnp.int32),
        vmem((pieces, rows, LANES), F32),
        vmem((pieces, rows, LANES), F32),
        vmem((n, 2 * rows, LANES), F32),
        vmem((n, 2 * rows + 8, LANES), F32),
        vmem((n, 2 * rows, LANES), F32),
        vmem((n, 2 * rows + 8, LANES), F32),
        vmem((n, 1, LANES), jnp.int32),
        vmem((n, 1, LANES), jnp.int32),
        pltpu.SMEM((n, 1, LANES), jnp.int32),
        pltpu.SMEM((n, 4), jnp.int32),
        vmem((2, pieces, LANES), F32),
        vmem((2, pieces, LANES), F32),
        vmem((pieces, LANES), F32),
        vmem((pieces, LANES), F32),
        pltpu.SMEM((2 * n,), jnp.int32),
        pltpu.SMEM((2 * n,), jnp.int32),
        vmem((1, LANES), jnp.int32),
        pltpu.SMEM((1, LANES), jnp.int32),
        vmem((2 * n + 1, 6 * rows + 8, LANES), F32),
        vmem((rows + 16, ext), F32),
        vmem((rows, LANES), F32),
        vmem((rows, LANES), F32),
        vmem((rows, LANES), F32),
        vmem((rows, LANES), F32),
        vmem((8, COLS_DEV), F32),
        vmem((8, COLS_DEV), F32),
        vmem((8, COLS_DEV), F32),
        vmem((8, COLS_DEV), F32),
        vmem((8, 3 * LANES), F32),
        vmem((8, 3 * LANES), F32),
        vmem((8, 3 * LANES), F32),
        vmem((8, 3 * LANES), F32),
        vmem((1, LANES), F32),
        vmem((n * lats, 1, LANES), F32),
        vmem((2 * ITERS + 1, 8, LANES), F32),
        dma((2, n)),
        dma((2, n)),
        dma((2, n)),
        dma((4,)),
        dma((4,)),
        dma((8,)),
        dma((2, n * lats)),
        dma((6,)),
    ]
    basis, coef = pl.pallas_call(
        functools.partial(kernel, n, lats, pieces, rows),
        out_shape=(
            jax.ShapeDtypeStruct((ITERS + 1, rows + 16, ext), F32),
            jax.ShapeDtypeStruct((16, LANES), F32),
        ),
        in_specs=[pl.BlockSpec(memory_space=pltpu.HBM)] * 4,
        out_specs=(pl.BlockSpec(memory_space=pltpu.VMEM),) * 2,
        scratch_shapes=scratch,
        compiler_params=pltpu.CompilerParams(
            collective_id=0, has_side_effects=True, vmem_limit_bytes=48 * 1024 * 1024
        ),
    )(*(pltpu.with_memory_space_constraint(a, pltpu.HBM) for a in (piece_column, piece_width, piece_height, piece_weight)))
    out = jax.ShapeDtypeStruct((rows, COLS_DEV), F32)
    return pl.pallas_call(
        functools.partial(combine, rows),
        out_shape=(out, out),
        in_specs=[pl.BlockSpec(memory_space=pltpu.VMEM)] * 2,
        out_specs=(pl.BlockSpec(memory_space=pltpu.HBM),) * 2,
        scratch_shapes=[
            vmem((rows, COLS_DEV), F32),
            vmem((rows, COLS_DEV), F32),
            dma((2, CHUNKS)),
        ],
        compiler_params=pltpu.CompilerParams(vmem_limit_bytes=16 * 1024 * 1024),
    )(basis, coef)


def solution(mesh):
    return jax.shard_map(
        functools.partial(body, mesh.shape["lon"], mesh.shape["lat"]),
        mesh=mesh,
        in_specs=(P("lon", "lat", None), P("lon", "lat", None), P("lon"), P("lon")),
        out_specs=(P("lat", "lon"), P("lat", "lon")),
        check_vma=False,
    )
```

```python
import functools

import jax
import jax.numpy as jnp
from jax import lax
from jax.experimental import pallas as pl
from jax.experimental.pallas import tpu as pltpu
from jax.sharding import PartitionSpec as P

COLS_DEV = 4096
ITERS = 4
MU_DATA = 0.5
DAMPING = 0.5
RIDGE = 0.05
SHIFT = 5.0
SCALE = 5.0

LANES = 128
CHUNKS = 4
MESH = pl.DeviceIdType.MESH
F32 = jnp.float32


def remote(src, dst, send, recv, device):
    return pltpu.make_async_remote_copy(
        src_ref=src, dst_ref=dst, send_sem=send, recv_sem=recv,
        device_id=device, device_id_type=MESH,
    )


def each(low, high):
    def run(step):
        if high - low <= 8:
            for i in range(low, high):
                step(i)
        else:
            pl.loop(low, high)(step)

    return run


def cg_coefficients(mu):
    def inner(a, b):
        total = None
        for i, x in enumerate(a):
            for j, y in enumerate(b):
                term = x * y * mu[i + j]
                total = term if total is None else total + term
        return total

    def apply(c):
        out = [SHIFT * x for x in c] + [jnp.zeros_like(c[0])]
        for i, x in enumerate(c):
            out[i + 1] = out[i + 1] + SCALE * x
        return out

    def add_scaled(y, a, x):
        out = []
        for i in range(max(len(x), len(y))):
            if i >= len(y):
                out.append(a * x[i])
            elif i >= len(x):
                out.append(y[i])
            else:
                out.append(y[i] + a * x[i])
        return out

    one = jnp.ones_like(mu[0])
    residual, direction, field = [one], [one], []
    norm = mu[0]
    for step in range(ITERS):
        image = apply(direction)
        alpha = norm / inner(direction, image)
        field = add_scaled(field, alpha, direction)
        residual = add_scaled(residual, -alpha, image)
        if step < ITERS - 1:
            fresh = inner(residual, residual)
            direction = add_scaled(residual, fresh / norm, direction)
            norm = fresh
    return field, residual


def kernel(
    n, lats, pieces, rows,
    col_in, wid_in, h_in, w_in, V, coef_ref,
    col_ref, wid_ref, h_ref, w_ref,
    hs, ws, hr, wr, ms, mr, msm, idx_s, up_s, up_r, dn_s, dn_r,
    blk_s, prev_s, last_v, last_s, S,
    D, east_s, east_r, west_s, west_r, lat_up_s, lat_up_r, lat_dn_s, lat_dn_r,
    side_up_s, side_up_r, side_dn_s, side_dn_r,
    red, rb, acc,
    sem_m, sem_h, sem_w, sem_e, sem_l, sem_t, sem_b, sem_loc,
):
    lon = lax.axis_index("lon")
    lat = lax.axis_index("lat")
    blocks = COLS_DEV // LANES
    ext = blocks + 2
    top = rows + 8
    slots = 2 * n
    lane = lax.broadcasted_iota(jnp.int32, (rows, LANES), 1)
    lane1 = lax.broadcasted_iota(jnp.int32, (1, LANES), 1)

    def lon_at(k):
        return lax.rem(lon + k, n)

    turns, bit = [], 1
    while bit < n:
        turns.append((1 - 2 * (lon // bit % 2)) * bit)
        bit *= 2

    def partner(k):
        other = lon
        for i, turn in enumerate(turns):
            if isinstance(k, int):
                other = other + turn if k >> i & 1 else other
            else:
                other = other + k // 2**i % 2 * turn
        return other

    def lat_at(k):
        if isinstance(k, int) and k == 0:
            return lat
        moved = lat + k
        return jnp.where(moved >= lats, moved - lats, moved)

    barrier = pltpu.get_barrier_semaphore()
    loads = [
        pltpu.make_async_copy(src, dst, sem_loc.at[2 + i])
        for i, (src, dst) in enumerate(
            ((col_in, col_ref), (wid_in, wid_ref), (h_in, h_ref), (w_in, w_ref))
        )
    ]
    for load in loads:
        load.start()

    devices = n * lats

    def all_peers(step):
        each(1, n)(lambda k: step(k * lats, (partner(k), lat)))

        @pl.loop(1, lats)
        def _(m):
            each(0, n)(lambda k: step(k * lats + m, (partner(k), lat_at(m))))

    all_peers(
        lambda j, device: pl.semaphore_signal(barrier, inc=1, device_id=device, device_id_type=MESH)
    )

    for load in loads:
        load.wait()

    @pl.loop(0, pieces)
    def _(i):
        up_s[0, pl.ds(i, 1), :] = h_ref[i, rows - 1 : rows, :]
        up_s[1, pl.ds(i, 1), :] = w_ref[i, rows - 1 : rows, :]
        dn_s[pl.ds(i, 1), :] = h_ref[i, 0:1, :]

    def fill(k, h_to, w_to, m_to):
        dest = partner(k)

        def scan(i, found):
            first, second = found
            match = (col_ref[i] >> 12) == dest
            second = jnp.where(match & (first >= 0) & (second < 0), i, second)
            first = jnp.where(match & (first < 0), i, first)
            return first, second

        found = lax.fori_loop(0, pieces, scan, (jnp.int32(-1), jnp.int32(-1)), unroll=8)
        tags = []
        for q in range(2):
            at = jnp.maximum(found[q], 0)
            limit = jnp.where(found[q] >= 0, wid_ref[at], 0)
            tags.append(jnp.where(found[q] >= 0, (col_ref[at] >> 7) & (blocks - 1), -1))
            idx_s[k, q] = at
            idx_s[k, 2 + q] = limit
            h_to[k, q * rows : (q + 1) * rows, :] = h_ref[at]
            w_to[k, q * rows : (q + 1) * rows, :] = jnp.where(lane < limit, w_ref[at], 0.0)
        m_to[k] = jnp.where(lane1 == 0, tags[0], jnp.where(lane1 == 1, tags[1], -1))

    far = n // 2

    @each(0, far)
    def _(i):
        fill(n - 1 - i, hs, ws, ms)

    pl.semaphore_wait(barrier, devices - 1)

    def edge_up():
        return remote(up_s, up_r, sem_e.at[0], sem_e.at[1], (lon, lat_at(1)))

    def edge_dn():
        return remote(dn_s, dn_r, sem_e.at[2], sem_e.at[3], (lon, lat_at(lats - 1)))

    def meta(k):
        return remote(ms.at[k], mr.at[k], sem_m.at[0, k], sem_m.at[1, k], (partner(k), lat))

    def heights(k):
        return remote(hs.at[k], hr.at[k], sem_h.at[0, k], sem_h.at[1, k], (partner(k), lat))

    def weights(k):
        return remote(ws.at[k], wr.at[k], sem_w.at[0, k], sem_w.at[1, k], (partner(k), lat))

    @pl.when(lat < lats - 1)
    def _():
        edge_up().start()

    @pl.when(lat > 0)
    def _():
        edge_dn().start()

    @each(0, far)
    def _(i):
        meta(n - 1 - i).start()
        heights(n - 1 - i).start()

    @each(far, n - 1)
    def _(i):
        fill(n - 1 - i, hs, ws, ms)
        meta(n - 1 - i).start()
        heights(n - 1 - i).start()

    fill(0, hr, wr, mr)

    @pl.when(lat > 0)
    def _():
        edge_up().wait_recv()

    @pl.when(lat == 0)
    def _():
        up_r[...] = jnp.zeros_like(up_r)

    @pl.when(lat < lats - 1)
    def _():
        edge_dn().wait_recv()

    @pl.when(lat == lats - 1)
    def _():
        dn_r[...] = jnp.zeros_like(dn_r)

    def extras(k, w_to):
        for q in range(2):
            at, limit = idx_s[k, q], idx_s[k, 2 + q]
            base = 2 * rows + q
            w_to[k, base : base + 1, :] = dn_r[pl.ds(at, 1), :]
            w_to[k, base + 2 : base + 3, :] = up_r[0, pl.ds(at, 1), :]
            w_to[k, base + 4 : base + 5, :] = jnp.where(lane1 < limit, up_r[1, pl.ds(at, 1), :], 0.0)
        w_to[k, 2 * rows + 6 : 2 * rows + 8, :] = jnp.zeros((2, LANES), F32)

    @each(1, n)
    def _(k):
        extras(n - k, ws)
        weights(n - k).start()

    extras(0, wr)

    @each(1, n)
    def _(k):
        meta(k).wait_recv()

    tags_in = pltpu.make_async_copy(mr, msm, sem_loc.at[0])
    tags_in.start()
    tags_in.wait()

    blk_s[0] = msm[0, 0, 0]
    blk_s[1] = msm[0, 0, 1]

    @each(1, n)
    def _(i):
        blk_s[2 * i] = msm[n - i, 0, 0]
        blk_s[2 * i + 1] = msm[n - i, 0, 1]

    def latest(p, last):
        tag = blk_s[p]

        def scan(j, found):
            return jnp.where((j < p) & (blk_s[j] == tag), j, found)

        prev_s[p] = lax.fori_loop(0, slots, scan, jnp.int32(slots), unroll=8)
        return jnp.where(lane1 == tag, p, last)

    nowhere = jnp.full((1, LANES), slots, jnp.int32)
    if slots <= 16:
        tags = [blk_s[p] for p in range(slots)]
        for p, tag in enumerate(tags):
            found = jnp.int32(slots)
            for j in range(p):
                found = jnp.where(tags[j] == tag, j, found)
            prev_s[p] = found
            nowhere = jnp.where(lane1 == tag, p, nowhere)
        last_v[...] = nowhere
    else:
        last_v[...] = lax.fori_loop(0, slots, latest, nowhere)
    last_in = pltpu.make_async_copy(last_v, last_s, sem_loc.at[1])
    last_in.start()
    last_in.wait()

    S[slots] = jnp.zeros((6 * rows + 8, LANES), F32)
    row_global = lat * rows + lax.broadcasted_iota(jnp.int32, (rows, LANES), 0)
    has_north = row_global < lats * rows - 1
    row_in = lax.broadcasted_iota(jnp.int32, (rows, LANES), 0)

    def terms(k, place):
        for q in range(2):
            p = 2 * place + q
            before = prev_s[p]
            h = hr[k, q * rows : (q + 1) * rows, :]
            w = wr[k, q * rows : (q + 1) * rows, :]
            base = 2 * rows + q
            above = wr[k, base : base + 1, :]
            below_h = wr[k, base + 2 : base + 3, :]
            below_w = wr[k, base + 4 : base + 5, :]
            h_north = jnp.where(row_in == rows - 1, above, pltpu.roll(h, rows - 1, 0))
            h_east = pltpu.roll(h, LANES - 1, 1)
            w_east = jnp.where((pltpu.roll(w, LANES - 1, 1) > 0.0) & (lane < LANES - 1), w, 0.0)
            w_north = jnp.where(has_north, w, 0.0)
            parts = (w, w * h, w_east, w_east * (h_east - h), w_north, w_north * (h_north - h))
            for t, part in enumerate(parts):
                at = pl.ds(t * rows, rows)
                S[p, at, :] = part + S[before, at, :]
            at = 6 * rows
            S[p, at : at + 1, :] = below_w + S[before, at : at + 1, :]
            S[p, at + 1 : at + 2, :] = below_w * (h[0:1, :] - below_h) + S[before, at + 1 : at + 2, :]

    terms(0, 0)

    @each(1, n)
    def _(i):
        heights(n - i).wait_recv()
        weights(n - i).wait_recv()
        terms(n - i, i)

    inv = 1.0 / SCALE

    def assemble(b, before):
        p = last_s[0, b]

        def field(t):
            return S[p, t * rows : (t + 1) * rows, :]

        at = 6 * rows
        t_east = field(3) / (field(2) + DAMPING)
        t_north = field(5) / (field(4) + DAMPING)
        t_below = S[p, at + 1 : at + 2, :] / (S[p, at : at + 1, :] + DAMPING)
        t_south = jnp.where(row_in == 0, t_below, pltpu.roll(t_north, 1, 0))
        rolled = pltpu.roll(t_east, 1, 1)
        t_west = jnp.where(lane == 0, before, rolled)
        right = MU_DATA * field(1) - (t_east - t_west) - (t_north - t_south)
        cols = pl.ds(pl.multiple_of((b + 1) * LANES, LANES), LANES)
        V[0, 8:top, cols] = right
        D[8:top, cols] = (MU_DATA * field(0) + (RIDGE + 4.0 - SHIFT)) * inv
        return rolled

    east_last = lax.fori_loop(0, blocks, assemble, jnp.zeros((rows, LANES), F32), unroll=16)

    first = slice(LANES, 2 * LANES)
    final = slice(blocks * LANES, (blocks + 1) * LANES)
    east_s[...] = jnp.where(
        lane >= LANES - 4,
        V[0, 8:top, final],
        jnp.where(
            lane >= LANES - 8,
            pltpu.roll(D[8:top, final], LANES - 4, 1),
            pltpu.roll(east_last, LANES - 9, 1),
        ),
    )
    west_s[...] = jnp.where(lane < 4, V[0, 8:top, first], pltpu.roll(D[8:top, first], 4, 1))
    east = remote(east_s, east_r, sem_l.at[0], sem_l.at[1], (lon_at(1), lat))
    west = remote(west_s, west_r, sem_l.at[2], sem_l.at[3], (lon_at(n - 1), lat))
    east.start()
    west.start()

    inner = slice(LANES, (blocks + 1) * LANES)
    lat_up_s[0:4, :] = D[top - 4 : top, inner]
    lat_up_s[4:8, :] = V[0, top - 4 : top, inner]
    lat_dn_s[0:4, :] = V[0, 8:12, inner]
    lat_dn_s[4:8, :] = D[8:12, inner]

    def rows_up():
        return remote(lat_up_s, lat_up_r, sem_t.at[0], sem_t.at[1], (lon, lat_at(1)))

    def rows_dn():
        return remote(lat_dn_s, lat_dn_r, sem_t.at[2], sem_t.at[3], (lon, lat_at(lats - 1)))

    def sides_up():
        return remote(side_up_s, side_up_r, sem_t.at[4], sem_t.at[5], (lon, lat_at(1)))

    def sides_dn():
        return remote(side_dn_s, side_dn_r, sem_t.at[6], sem_t.at[7], (lon, lat_at(lats - 1)))

    @pl.when(lat < lats - 1)
    def _():
        rows_up().start()

    @pl.when(lat > 0)
    def _():
        rows_dn().start()

    halo_w = slice(0, LANES)
    halo_e = slice((blocks + 1) * LANES, (blocks + 2) * LANES)
    east.wait_recv()
    got_east = east_r[...]
    V[0, 8:top, halo_w] = got_east
    D[8:top, halo_w] = pltpu.roll(got_east, 4, 1)
    V[0, 8:top, first] = V[0, 8:top, first] + jnp.where(lane == 0, pltpu.roll(got_east, 9, 1), 0.0)
    west.wait_recv()
    got_west = west_r[...]
    V[0, 8:top, halo_e] = got_west + jnp.where(lane == 0, east_last, 0.0)
    D[8:top, halo_e] = pltpu.roll(got_west, LANES - 4, 1)
    side_blocks = (halo_w, first, halo_e)
    for i, cols in enumerate(side_blocks):
        to = slice(i * LANES, (i + 1) * LANES)
        side_up_s[0:4, to] = D[top - 4 : top, cols]
        side_up_s[4:8, to] = V[0, top - 4 : top, cols]
        side_dn_s[0:4, to] = V[0, 8:12, cols]
        side_dn_s[4:8, to] = D[8:12, cols]

    @pl.when(lat < lats - 1)
    def _():
        sides_up().start()

    @pl.when(lat > 0)
    def _():
        sides_dn().start()

    def mirror(k):
        @pl.when(lat == 0)
        def _():
            V[k, 7:8, :] = V[k, 8:9, :]

        @pl.when(lat == lats - 1)
        def _():
            V[k, top : top + 1, :] = V[k, top - 1 : top, :]

    @pl.when(lat > 0)
    def _():
        rows_up().wait_recv()
        got = lat_up_r[...]
        V[0, 0:8, inner] = got
        D[0:8, inner] = pltpu.roll(got, 4, 0)
        sides_up().wait_recv()
        for i, cols in enumerate(side_blocks):
            got = side_up_r[:, i * LANES : (i + 1) * LANES]
            V[0, 0:8, cols] = got
            D[0:8, cols] = pltpu.roll(got, 4, 0)

    @pl.when(lat == 0)
    def _():
        V[0, 0:8, :] = jnp.zeros((8, ext * LANES), F32)
        D[0:8, :] = jnp.zeros((8, ext * LANES), F32)

    @pl.when(lat < lats - 1)
    def _():
        rows_dn().wait_recv()
        got = lat_dn_r[...]
        V[0, top : top + 8, inner] = got
        D[top : top + 8, inner] = pltpu.roll(got, 4, 0)
        sides_dn().wait_recv()
        for i, cols in enumerate(side_blocks):
            got = side_dn_r[:, i * LANES : (i + 1) * LANES]
            V[0, top : top + 8, cols] = got
            D[top : top + 8, cols] = pltpu.roll(got, 4, 0)

    @pl.when(lat == lats - 1)
    def _():
        V[0, top : top + 8, :] = jnp.zeros((8, ext * LANES), F32)
        D[top : top + 8, :] = jnp.zeros((8, ext * LANES), F32)

    mirror(0)

    tall = rows + 16
    lane_t = lax.broadcasted_iota(jnp.int32, (tall, LANES), 1)

    def at_block(b):
        return pl.ds(pl.multiple_of(b * LANES, LANES), LANES)

    def fold(value):
        total = value[0:8]
        for i in range(1, rows // 8):
            total = total + value[8 * i : 8 * i + 8]
        return total

    @pl.loop(0, ITERS)
    def _(k):
        def one(b, here, before, ahead):
            nxt = V[k, :, at_block(jnp.minimum(b + 1, ext - 1))]
            ahead_next = pltpu.roll(nxt, LANES - 1, 1)
            rolled = pltpu.roll(here, 1, 1)
            sides = jnp.where(lane_t == 0, before, rolled)
            sides = sides + jnp.where(lane_t == LANES - 1, ahead_next, ahead)
            sides = sides + pltpu.roll(here, 1, 0) + pltpu.roll(here, tall - 1, 0)
            out = D[:, at_block(b)] * here - inv * sides
            V[k + 1, :, at_block(b)] = out
            return out, nxt, rolled, ahead_next

        def step(b, carry):
            here, before, ahead, base, cross, own = carry
            out, nxt, rolled, ahead_next = one(b, here, before, ahead)
            mine, image = here[8:top], out[8:top]
            base = base + fold(mine * mine)
            cross = cross + fold(mine * image)
            own = own + fold(image * image)
            return nxt, rolled, ahead_next, base, cross, own

        here = V[k, :, 0:LANES]
        ahead = pltpu.roll(here, LANES - 1, 1)
        _, here, before, ahead = one(0, here, ahead, ahead)
        zero = jnp.zeros((8, LANES), F32)
        here, before, ahead, base, cross, own = lax.fori_loop(
            1, blocks + 1, step, (here, before, ahead, zero, zero, zero), unroll=32
        )
        one(ext - 1, here, before, ahead)
        mirror(k + 1)
        acc[2 * k] = base
        acc[2 * k + 1] = cross
        acc[2 * k + 2] = own

    mine = jnp.zeros((1, LANES), F32)
    for i in range(2 * ITERS + 1):
        value = jnp.sum(jnp.sum(acc[i], axis=0, keepdims=True), axis=1, keepdims=True)
        mine = jnp.where(lane1 == i, value, mine)
    red[...] = mine
    place = lon * lats + lat

    def share(j, device=(partner(1), lat)):
        return remote(red, rb.at[place], sem_b.at[0, j], sem_b.at[1, j], device)

    all_peers(lambda j, device: share(j, device).start())

    rb[place] = mine

    @each(1, devices)
    def _(j):
        share(j).wait_recv()

    total = jnp.sum(rb[...], axis=0)
    mu = [
        jnp.broadcast_to(
            jnp.sum(jnp.where(lane1 == i, total, 0.0), axis=1, keepdims=True), (8, LANES)
        )
        for i in range(2 * ITERS + 1)
    ]
    field, residual = cg_coefficients(mu)
    for i, c in enumerate(field + residual):
        coef_ref[i : i + 1, :] = c[0:1, :]

    @each(1, n)
    def _(k):
        meta(k).wait_send()
        heights(k).wait_send()
        weights(k).wait_send()

    @each(1, devices)
    def _(j):
        share(j).wait_send()

    east.wait_send()
    west.wait_send()

    @pl.when(lat < lats - 1)
    def _():
        edge_up().wait_send()
        rows_up().wait_send()
        sides_up().wait_send()

    @pl.when(lat > 0)
    def _():
        edge_dn().wait_send()
        rows_dn().wait_send()
        sides_dn().wait_send()


def combine(rows, V, coef_ref, x_out, r_out, x_ref, r_ref, sem):
    coef = [coef_ref[i : i + 1, :] for i in range(2 * ITERS + 1)]
    coef = [jnp.broadcast_to(c, (rows, LANES)) for c in coef]
    field, residual = coef[:ITERS], coef[ITERS:]
    width = COLS_DEV // CHUNKS

    def copies(c):
        cols = pl.ds(c * width, width)
        return (
            pltpu.make_async_copy(x_ref.at[:, cols], x_out.at[:, cols], sem.at[0, c]),
            pltpu.make_async_copy(r_ref.at[:, cols], r_out.at[:, cols], sem.at[1, c]),
        )

    for c in range(CHUNKS):

        def one(b, carry):
            v = V[0, 8 : rows + 8, pl.ds(pl.multiple_of((b + 1) * LANES, LANES), LANES)]
            x, r = field[0] * v, residual[0] * v
            for k in range(1, ITERS + 1):
                v = V[k, 8 : rows + 8, pl.ds(pl.multiple_of((b + 1) * LANES, LANES), LANES)]
                r = r + residual[k] * v
                if k < ITERS:
                    x = x + field[k] * v
            cols = pl.ds(pl.multiple_of(b * LANES, LANES), LANES)
            x_ref[:, cols] = x
            r_ref[:, cols] = r
            return carry

        per = width // LANES
        lax.fori_loop(c * per, (c + 1) * per, one, 0, unroll=8)
        for copy in copies(c):
            copy.start()
    for c in range(CHUNKS):
        for copy in copies(c):
            copy.wait()


def body(n, lats, piece_height, piece_weight, piece_column, piece_width):
    pieces, rows, width = piece_height.shape
    ext = COLS_DEV + 2 * LANES
    vmem = pltpu.VMEM
    dma = pltpu.SemaphoreType.DMA
    scratch = [
        pltpu.SMEM((pieces,), jnp.int32),
        pltpu.SMEM((pieces,), jnp.int32),
        vmem((pieces, rows, LANES), F32),
        vmem((pieces, rows, LANES), F32),
        vmem((n, 2 * rows, LANES), F32),
        vmem((n, 2 * rows + 8, LANES), F32),
        vmem((n, 2 * rows, LANES), F32),
        vmem((n, 2 * rows + 8, LANES), F32),
        vmem((n, 1, LANES), jnp.int32),
        vmem((n, 1, LANES), jnp.int32),
        pltpu.SMEM((n, 1, LANES), jnp.int32),
        pltpu.SMEM((n, 4), jnp.int32),
        vmem((2, pieces, LANES), F32),
        vmem((2, pieces, LANES), F32),
        vmem((pieces, LANES), F32),
        vmem((pieces, LANES), F32),
        pltpu.SMEM((2 * n,), jnp.int32),
        pltpu.SMEM((2 * n,), jnp.int32),
        vmem((1, LANES), jnp.int32),
        pltpu.SMEM((1, LANES), jnp.int32),
        vmem((2 * n + 1, 6 * rows + 8, LANES), F32),
        vmem((rows + 16, ext), F32),
        vmem((rows, LANES), F32),
        vmem((rows, LANES), F32),
        vmem((rows, LANES), F32),
        vmem((rows, LANES), F32),
        vmem((8, COLS_DEV), F32),
        vmem((8, COLS_DEV), F32),
        vmem((8, COLS_DEV), F32),
        vmem((8, COLS_DEV), F32),
        vmem((8, 3 * LANES), F32),
        vmem((8, 3 * LANES), F32),
        vmem((8, 3 * LANES), F32),
        vmem((8, 3 * LANES), F32),
        vmem((1, LANES), F32),
        vmem((n * lats, 1, LANES), F32),
        vmem((2 * ITERS + 1, 8, LANES), F32),
        dma((2, n)),
        dma((2, n)),
        dma((2, n)),
        dma((4,)),
        dma((4,)),
        dma((8,)),
        dma((2, n * lats)),
        dma((6,)),
    ]
    basis, coef = pl.pallas_call(
        functools.partial(kernel, n, lats, pieces, rows),
        out_shape=(
            jax.ShapeDtypeStruct((ITERS + 1, rows + 16, ext), F32),
            jax.ShapeDtypeStruct((16, LANES), F32),
        ),
        in_specs=[pl.BlockSpec(memory_space=pltpu.HBM)] * 4,
        out_specs=(pl.BlockSpec(memory_space=pltpu.VMEM),) * 2,
        scratch_shapes=scratch,
        compiler_params=pltpu.CompilerParams(
            collective_id=0, has_side_effects=True, vmem_limit_bytes=48 * 1024 * 1024
        ),
    )(*(pltpu.with_memory_space_constraint(a, pltpu.HBM) for a in (piece_column, piece_width, piece_height, piece_weight)))
    out = jax.ShapeDtypeStruct((rows, COLS_DEV), F32)
    return pl.pallas_call(
        functools.partial(combine, rows),
        out_shape=(out, out),
        in_specs=[pl.BlockSpec(memory_space=pltpu.VMEM)] * 2,
        out_specs=(pl.BlockSpec(memory_space=pltpu.HBM),) * 2,
        scratch_shapes=[
            vmem((rows, COLS_DEV), F32),
            vmem((rows, COLS_DEV), F32),
            dma((2, CHUNKS)),
        ],
        compiler_params=pltpu.CompilerParams(vmem_limit_bytes=16 * 1024 * 1024),
    )(basis, coef)


def solution(mesh):
    return jax.shard_map(
        functools.partial(body, mesh.shape["lon"], mesh.shape["lat"]),
        mesh=mesh,
        in_specs=(P("lon", "lat", None), P("lon", "lat", None), P("lon"), P("lon")),
        out_specs=(P("lat", "lon"), P("lat", "lon")),
        check_vma=False,
    )
```

```python
import functools

import jax
import jax.numpy as jnp
from jax import lax
from jax.experimental import pallas as pl
from jax.experimental.pallas import tpu as pltpu
from jax.sharding import PartitionSpec as P

COLS_DEV = 4096
ITERS = 4
MU_DATA = 0.5
DAMPING = 0.5
RIDGE = 0.05
SHIFT = 5.0
SCALE = 5.0

LANES = 128
CHUNKS = 4
MESH = pl.DeviceIdType.MESH
F32 = jnp.float32


def remote(src, dst, send, recv, device):
    return pltpu.make_async_remote_copy(
        src_ref=src, dst_ref=dst, send_sem=send, recv_sem=recv,
        device_id=device, device_id_type=MESH,
    )


def each(low, high):
    def run(step):
        if high - low <= 8:
            for i in range(low, high):
                step(i)
        else:
            pl.loop(low, high)(step)

    return run


def cg_coefficients(mu):
    def inner(a, b):
        total = None
        for i, x in enumerate(a):
            for j, y in enumerate(b):
                term = x * y * mu[i + j]
                total = term if total is None else total + term
        return total

    def apply(c):
        out = [SHIFT * x for x in c] + [jnp.zeros_like(c[0])]
        for i, x in enumerate(c):
            out[i + 1] = out[i + 1] + SCALE * x
        return out

    def add_scaled(y, a, x):
        out = []
        for i in range(max(len(x), len(y))):
            if i >= len(y):
                out.append(a * x[i])
            elif i >= len(x):
                out.append(y[i])
            else:
                out.append(y[i] + a * x[i])
        return out

    one = jnp.ones_like(mu[0])
    residual, direction, field = [one], [one], []
    norm = mu[0]
    for step in range(ITERS):
        image = apply(direction)
        alpha = norm / inner(direction, image)
        field = add_scaled(field, alpha, direction)
        residual = add_scaled(residual, -alpha, image)
        if step < ITERS - 1:
            fresh = inner(residual, residual)
            direction = add_scaled(residual, fresh / norm, direction)
            norm = fresh
    return field, residual


def kernel(
    n, lats, pieces, rows,
    col_in, wid_in, h_in, w_in, V, coef_ref,
    col_ref, wid_ref, h_ref, w_ref,
    hs, ws, hr, wr, ms, mr, msm, idx_s, up_s, up_r, dn_s, dn_r,
    blk_s, prev_s, last_v, last_s, S,
    D, east_s, east_r, west_s, west_r, lat_up_s, lat_up_r, lat_dn_s, lat_dn_r,
    side_up_s, side_up_r, side_dn_s, side_dn_r,
    red, rb, acc,
    sem_m, sem_h, sem_w, sem_e, sem_l, sem_t, sem_b, sem_loc,
):
    lon = lax.axis_index("lon")
    lat = lax.axis_index("lat")
    blocks = COLS_DEV // LANES
    ext = blocks + 2
    top = rows + 8
    slots = 2 * n
    lane = lax.broadcasted_iota(jnp.int32, (rows, LANES), 1)
    lane1 = lax.broadcasted_iota(jnp.int32, (1, LANES), 1)

    def lon_at(k):
        return lax.rem(lon + k, n)

    turns, bit = [], 1
    while bit < n:
        turns.append((1 - 2 * (lon // bit % 2)) * bit)
        bit *= 2

    def partner(k):
        other = lon
        for i, turn in enumerate(turns):
            if isinstance(k, int):
                other = other + turn if k >> i & 1 else other
            else:
                other = other + k // 2**i % 2 * turn
        return other

    def lat_at(k):
        if isinstance(k, int) and k == 0:
            return lat
        moved = lat + k
        return jnp.where(moved >= lats, moved - lats, moved)

    barrier = pltpu.get_barrier_semaphore()
    loads = [
        pltpu.make_async_copy(src, dst, sem_loc.at[2 + i])
        for i, (src, dst) in enumerate(
            ((col_in, col_ref), (wid_in, wid_ref), (h_in, h_ref), (w_in, w_ref))
        )
    ]
    for load in loads:
        load.start()

    devices = n * lats

    def all_peers(step):
        each(1, n)(lambda k: step(k * lats, (partner(k), lat)))

        @pl.loop(1, lats)
        def _(m):
            each(0, n)(lambda k: step(k * lats + m, (partner(k), lat_at(m))))

    all_peers(
        lambda j, device: pl.semaphore_signal(barrier, inc=1, device_id=device, device_id_type=MESH)
    )

    for load in loads:
        load.wait()

    @pl.loop(0, pieces)
    def _(i):
        up_s[0, pl.ds(i, 1), :] = h_ref[i, rows - 1 : rows, :]
        up_s[1, pl.ds(i, 1), :] = w_ref[i, rows - 1 : rows, :]
        dn_s[pl.ds(i, 1), :] = h_ref[i, 0:1, :]

    def fill(k, h_to, w_to, m_to):
        dest = partner(k)

        def scan(i, found):
            first, second = found
            match = (col_ref[i] >> 12) == dest
            second = jnp.where(match & (first >= 0) & (second < 0), i, second)
            first = jnp.where(match & (first < 0), i, first)
            return first, second

        found = lax.fori_loop(0, pieces, scan, (jnp.int32(-1), jnp.int32(-1)), unroll=8)
        tags = []
        for q in range(2):
            at = jnp.maximum(found[q], 0)
            limit = jnp.where(found[q] >= 0, wid_ref[at], 0)
            tags.append(jnp.where(found[q] >= 0, (col_ref[at] >> 7) & (blocks - 1), -1))
            idx_s[k, q] = at
            idx_s[k, 2 + q] = limit
            h_to[k, q * rows : (q + 1) * rows, :] = h_ref[at]
            w_to[k, q * rows : (q + 1) * rows, :] = jnp.where(lane < limit, w_ref[at], 0.0)
        m_to[k] = jnp.where(lane1 == 0, tags[0], jnp.where(lane1 == 1, tags[1], -1))

    far = n // 2

    @each(0, far)
    def _(i):
        fill(n - 1 - i, hs, ws, ms)

    pl.semaphore_wait(barrier, devices - 1)

    def edge_up():
        return remote(up_s, up_r, sem_e.at[0], sem_e.at[1], (lon, lat_at(1)))

    def edge_dn():
        return remote(dn_s, dn_r, sem_e.at[2], sem_e.at[3], (lon, lat_at(lats - 1)))

    def meta(k):
        return remote(ms.at[k], mr.at[k], sem_m.at[0, k], sem_m.at[1, k], (partner(k), lat))

    def heights(k):
        return remote(hs.at[k], hr.at[k], sem_h.at[0, k], sem_h.at[1, k], (partner(k), lat))

    def weights(k):
        return remote(ws.at[k], wr.at[k], sem_w.at[0, k], sem_w.at[1, k], (partner(k), lat))

    @pl.when(lat < lats - 1)
    def _():
        edge_up().start()

    @pl.when(lat > 0)
    def _():
        edge_dn().start()

    @each(0, far)
    def _(i):
        meta(n - 1 - i).start()
        heights(n - 1 - i).start()

    @each(far, n - 1)
    def _(i):
        fill(n - 1 - i, hs, ws, ms)
        meta(n - 1 - i).start()
        heights(n - 1 - i).start()

    fill(0, hr, wr, mr)

    @pl.when(lat > 0)
    def _():
        edge_up().wait_recv()

    @pl.when(lat == 0)
    def _():
        up_r[...] = jnp.zeros_like(up_r)

    @pl.when(lat < lats - 1)
    def _():
        edge_dn().wait_recv()

    @pl.when(lat == lats - 1)
    def _():
        dn_r[...] = jnp.zeros_like(dn_r)

    def extras(k, w_to):
        for q in range(2):
            at, limit = idx_s[k, q], idx_s[k, 2 + q]
            base = 2 * rows + q
            w_to[k, base : base + 1, :] = dn_r[pl.ds(at, 1), :]
            w_to[k, base + 2 : base + 3, :] = up_r[0, pl.ds(at, 1), :]
            w_to[k, base + 4 : base + 5, :] = jnp.where(lane1 < limit, up_r[1, pl.ds(at, 1), :], 0.0)
        w_to[k, 2 * rows + 6 : 2 * rows + 8, :] = jnp.zeros((2, LANES), F32)

    @each(1, n)
    def _(k):
        extras(n - k, ws)
        weights(n - k).start()

    extras(0, wr)

    @each(1, n)
    def _(k):
        meta(k).wait_recv()

    tags_in = pltpu.make_async_copy(mr, msm, sem_loc.at[0])
    tags_in.start()
    tags_in.wait()

    blk_s[0] = msm[0, 0, 0]
    blk_s[1] = msm[0, 0, 1]

    @each(1, n)
    def _(i):
        blk_s[2 * i] = msm[n - i, 0, 0]
        blk_s[2 * i + 1] = msm[n - i, 0, 1]

    def latest(p, last):
        tag = blk_s[p]

        def scan(j, found):
            return jnp.where((j < p) & (blk_s[j] == tag), j, found)

        prev_s[p] = lax.fori_loop(0, slots, scan, jnp.int32(slots), unroll=8)
        return jnp.where(lane1 == tag, p, last)

    nowhere = jnp.full((1, LANES), slots, jnp.int32)
    if slots <= 16:
        tags = [blk_s[p] for p in range(slots)]
        for p, tag in enumerate(tags):
            found = jnp.int32(slots)
            for j in range(p):
                found = jnp.where(tags[j] == tag, j, found)
            prev_s[p] = found
            nowhere = jnp.where(lane1 == tag, p, nowhere)
        last_v[...] = nowhere
    else:
        last_v[...] = lax.fori_loop(0, slots, latest, nowhere)
    last_in = pltpu.make_async_copy(last_v, last_s, sem_loc.at[1])
    last_in.start()
    last_in.wait()

    S[slots] = jnp.zeros((6 * rows + 8, LANES), F32)
    row_global = lat * rows + lax.broadcasted_iota(jnp.int32, (rows, LANES), 0)
    has_north = row_global < lats * rows - 1
    row_in = lax.broadcasted_iota(jnp.int32, (rows, LANES), 0)

    def terms(k, place):
        for q in range(2):
            p = 2 * place + q
            before = prev_s[p]
            so_far = [S[before, t * rows : (t + 1) * rows, :] for t in range(6)]
            below_w_sum = S[before, 6 * rows : 6 * rows + 1, :]
            below_sum = S[before, 6 * rows + 1 : 6 * rows + 2, :]
            h = hr[k, q * rows : (q + 1) * rows, :]
            w = wr[k, q * rows : (q + 1) * rows, :]
            base = 2 * rows + q
            above = wr[k, base : base + 1, :]
            below_h = wr[k, base + 2 : base + 3, :]
            below_w = wr[k, base + 4 : base + 5, :]
            h_north = jnp.where(row_in == rows - 1, above, pltpu.roll(h, rows - 1, 0))
            h_east = pltpu.roll(h, LANES - 1, 1)
            w_east = jnp.where((pltpu.roll(w, LANES - 1, 1) > 0.0) & (lane < LANES - 1), w, 0.0)
            w_north = jnp.where(has_north, w, 0.0)
            parts = (w, w * h, w_east, w_east * (h_east - h), w_north, w_north * (h_north - h))
            for t, part in enumerate(parts):
                at = pl.ds(t * rows, rows)
                S[p, at, :] = part + so_far[t]
            at = 6 * rows
            S[p, at : at + 1, :] = below_w + below_w_sum
            S[p, at + 1 : at + 2, :] = below_w * (h[0:1, :] - below_h) + below_sum

    terms(0, 0)

    @each(1, n)
    def _(i):
        heights(n - i).wait_recv()
        weights(n - i).wait_recv()
        terms(n - i, i)

    inv = 1.0 / SCALE

    def assemble(b, before):
        p = last_s[0, b]

        def field(t):
            return S[p, t * rows : (t + 1) * rows, :]

        at = 6 * rows
        t_east = field(3) / (field(2) + DAMPING)
        t_north = field(5) / (field(4) + DAMPING)
        t_below = S[p, at + 1 : at + 2, :] / (S[p, at : at + 1, :] + DAMPING)
        t_south = jnp.where(row_in == 0, t_below, pltpu.roll(t_north, 1, 0))
        rolled = pltpu.roll(t_east, 1, 1)
        t_west = jnp.where(lane == 0, before, rolled)
        right = MU_DATA * field(1) - (t_east - t_west) - (t_north - t_south)
        cols = pl.ds(pl.multiple_of((b + 1) * LANES, LANES), LANES)
        V[0, 8:top, cols] = right
        D[8:top, cols] = (MU_DATA * field(0) + (RIDGE + 4.0 - SHIFT)) * inv
        return rolled

    east_last = lax.fori_loop(0, blocks, assemble, jnp.zeros((rows, LANES), F32), unroll=32)

    first = slice(LANES, 2 * LANES)
    final = slice(blocks * LANES, (blocks + 1) * LANES)
    east_s[...] = jnp.where(
        lane >= LANES - 4,
        V[0, 8:top, final],
        jnp.where(
            lane >= LANES - 8,
            pltpu.roll(D[8:top, final], LANES - 4, 1),
            pltpu.roll(east_last, LANES - 9, 1),
        ),
    )
    west_s[...] = jnp.where(lane < 4, V[0, 8:top, first], pltpu.roll(D[8:top, first], 4, 1))
    east = remote(east_s, east_r, sem_l.at[0], sem_l.at[1], (lon_at(1), lat))
    west = remote(west_s, west_r, sem_l.at[2], sem_l.at[3], (lon_at(n - 1), lat))
    east.start()
    west.start()

    inner = slice(LANES, (blocks + 1) * LANES)
    lat_up_s[0:4, :] = D[top - 4 : top, inner]
    lat_up_s[4:8, :] = V[0, top - 4 : top, inner]
    lat_dn_s[0:4, :] = V[0, 8:12, inner]
    lat_dn_s[4:8, :] = D[8:12, inner]

    def rows_up():
        return remote(lat_up_s, lat_up_r, sem_t.at[0], sem_t.at[1], (lon, lat_at(1)))

    def rows_dn():
        return remote(lat_dn_s, lat_dn_r, sem_t.at[2], sem_t.at[3], (lon, lat_at(lats - 1)))

    def sides_up():
        return remote(side_up_s, side_up_r, sem_t.at[4], sem_t.at[5], (lon, lat_at(1)))

    def sides_dn():
        return remote(side_dn_s, side_dn_r, sem_t.at[6], sem_t.at[7], (lon, lat_at(lats - 1)))

    @pl.when(lat < lats - 1)
    def _():
        rows_up().start()

    @pl.when(lat > 0)
    def _():
        rows_dn().start()

    halo_w = slice(0, LANES)
    halo_e = slice((blocks + 1) * LANES, (blocks + 2) * LANES)
    east.wait_recv()
    got_east = east_r[...]
    V[0, 8:top, halo_w] = got_east
    D[8:top, halo_w] = pltpu.roll(got_east, 4, 1)
    V[0, 8:top, first] = V[0, 8:top, first] + jnp.where(lane == 0, pltpu.roll(got_east, 9, 1), 0.0)
    west.wait_recv()
    got_west = west_r[...]
    V[0, 8:top, halo_e] = got_west + jnp.where(lane == 0, east_last, 0.0)
    D[8:top, halo_e] = pltpu.roll(got_west, LANES - 4, 1)
    side_blocks = (halo_w, first, halo_e)
    for i, cols in enumerate(side_blocks):
        to = slice(i * LANES, (i + 1) * LANES)
        side_up_s[0:4, to] = D[top - 4 : top, cols]
        side_up_s[4:8, to] = V[0, top - 4 : top, cols]
        side_dn_s[0:4, to] = V[0, 8:12, cols]
        side_dn_s[4:8, to] = D[8:12, cols]

    @pl.when(lat < lats - 1)
    def _():
        sides_up().start()

    @pl.when(lat > 0)
    def _():
        sides_dn().start()

    def mirror(k):
        @pl.when(lat == 0)
        def _():
            V[k, 7:8, :] = V[k, 8:9, :]

        @pl.when(lat == lats - 1)
        def _():
            V[k, top : top + 1, :] = V[k, top - 1 : top, :]

    @pl.when(lat > 0)
    def _():
        rows_up().wait_recv()
        got = lat_up_r[...]
        V[0, 0:8, inner] = got
        D[0:8, inner] = pltpu.roll(got, 4, 0)
        sides_up().wait_recv()
        for i, cols in enumerate(side_blocks):
            got = side_up_r[:, i * LANES : (i + 1) * LANES]
            V[0, 0:8, cols] = got
            D[0:8, cols] = pltpu.roll(got, 4, 0)

    @pl.when(lat == 0)
    def _():
        V[0, 0:8, :] = jnp.zeros((8, ext * LANES), F32)
        D[0:8, :] = jnp.zeros((8, ext * LANES), F32)

    @pl.when(lat < lats - 1)
    def _():
        rows_dn().wait_recv()
        got = lat_dn_r[...]
        V[0, top : top + 8, inner] = got
        D[top : top + 8, inner] = pltpu.roll(got, 4, 0)
        sides_dn().wait_recv()
        for i, cols in enumerate(side_blocks):
            got = side_dn_r[:, i * LANES : (i + 1) * LANES]
            V[0, top : top + 8, cols] = got
            D[top : top + 8, cols] = pltpu.roll(got, 4, 0)

    @pl.when(lat == lats - 1)
    def _():
        V[0, top : top + 8, :] = jnp.zeros((8, ext * LANES), F32)
        D[top : top + 8, :] = jnp.zeros((8, ext * LANES), F32)

    mirror(0)

    tall = rows + 16
    lane_t = lax.broadcasted_iota(jnp.int32, (tall, LANES), 1)

    def at_block(b):
        return pl.ds(pl.multiple_of(b * LANES, LANES), LANES)

    def fold(value):
        total = value[0:8]
        for i in range(1, rows // 8):
            total = total + value[8 * i : 8 * i + 8]
        return total

    @pl.loop(0, ITERS)
    def _(k):
        def one(b, here, before, ahead):
            nxt = V[k, :, at_block(jnp.minimum(b + 1, ext - 1))]
            ahead_next = pltpu.roll(nxt, LANES - 1, 1)
            rolled = pltpu.roll(here, 1, 1)
            sides = jnp.where(lane_t == 0, before, rolled)
            sides = sides + jnp.where(lane_t == LANES - 1, ahead_next, ahead)
            sides = sides + pltpu.roll(here, 1, 0) + pltpu.roll(here, tall - 1, 0)
            out = D[:, at_block(b)] * here - inv * sides
            V[k + 1, :, at_block(b)] = out
            return out, nxt, rolled, ahead_next

        def step(b, carry):
            here, before, ahead, base, cross, own = carry
            out, nxt, rolled, ahead_next = one(b, here, before, ahead)
            mine, image = here[8:top], out[8:top]
            base = base + fold(mine * mine)
            cross = cross + fold(mine * image)
            own = own + fold(image * image)
            return nxt, rolled, ahead_next, base, cross, own

        here = V[k, :, 0:LANES]
        ahead = pltpu.roll(here, LANES - 1, 1)
        _, here, before, ahead = one(0, here, ahead, ahead)
        zero = jnp.zeros((8, LANES), F32)
        here, before, ahead, base, cross, own = lax.fori_loop(
            1, blocks + 1, step, (here, before, ahead, zero, zero, zero), unroll=32
        )
        one(ext - 1, here, before, ahead)
        mirror(k + 1)
        acc[2 * k] = base
        acc[2 * k + 1] = cross
        acc[2 * k + 2] = own

    mine = jnp.zeros((1, LANES), F32)
    for i in range(2 * ITERS + 1):
        value = jnp.sum(jnp.sum(acc[i], axis=0, keepdims=True), axis=1, keepdims=True)
        mine = jnp.where(lane1 == i, value, mine)
    red[...] = mine
    place = lon * lats + lat

    def share(j, device=(partner(1), lat)):
        return remote(red, rb.at[place], sem_b.at[0, j], sem_b.at[1, j], device)

    all_peers(lambda j, device: share(j, device).start())

    rb[place] = mine

    @each(1, devices)
    def _(j):
        share(j).wait_recv()

    total = jnp.sum(rb[...], axis=0)
    mu = [
        jnp.broadcast_to(
            jnp.sum(jnp.where(lane1 == i, total, 0.0), axis=1, keepdims=True), (8, LANES)
        )
        for i in range(2 * ITERS + 1)
    ]
    field, residual = cg_coefficients(mu)
    for i, c in enumerate(field + residual):
        coef_ref[i : i + 1, :] = c[0:1, :]

    @each(1, n)
    def _(k):
        meta(k).wait_send()
        heights(k).wait_send()
        weights(k).wait_send()

    @each(1, devices)
    def _(j):
        share(j).wait_send()

    east.wait_send()
    west.wait_send()

    @pl.when(lat < lats - 1)
    def _():
        edge_up().wait_send()
        rows_up().wait_send()
        sides_up().wait_send()

    @pl.when(lat > 0)
    def _():
        edge_dn().wait_send()
        rows_dn().wait_send()
        sides_dn().wait_send()


def combine(rows, V, coef_ref, x_out, r_out, x_ref, r_ref, sem):
    coef = [coef_ref[i : i + 1, :] for i in range(2 * ITERS + 1)]
    coef = [jnp.broadcast_to(c, (rows, LANES)) for c in coef]
    field, residual = coef[:ITERS], coef[ITERS:]
    width = COLS_DEV // CHUNKS

    def copies(c):
        cols = pl.ds(c * width, width)
        return (
            pltpu.make_async_copy(x_ref.at[:, cols], x_out.at[:, cols], sem.at[0, c]),
            pltpu.make_async_copy(r_ref.at[:, cols], r_out.at[:, cols], sem.at[1, c]),
        )

    for c in range(CHUNKS):

        def one(b, carry):
            v = V[0, 8 : rows + 8, pl.ds(pl.multiple_of((b + 1) * LANES, LANES), LANES)]
            x, r = field[0] * v, residual[0] * v
            for k in range(1, ITERS + 1):
                v = V[k, 8 : rows + 8, pl.ds(pl.multiple_of((b + 1) * LANES, LANES), LANES)]
                r = r + residual[k] * v
                if k < ITERS:
                    x = x + field[k] * v
            cols = pl.ds(pl.multiple_of(b * LANES, LANES), LANES)
            x_ref[:, cols] = x
            r_ref[:, cols] = r
            return carry

        per = width // LANES
        lax.fori_loop(c * per, (c + 1) * per, one, 0, unroll=8)
        for copy in copies(c):
            copy.start()
    for c in range(CHUNKS):
        for copy in copies(c):
            copy.wait()


def body(n, lats, piece_height, piece_weight, piece_column, piece_width):
    pieces, rows, width = piece_height.shape
    ext = COLS_DEV + 2 * LANES
    vmem = pltpu.VMEM
    dma = pltpu.SemaphoreType.DMA
    scratch = [
        pltpu.SMEM((pieces,), jnp.int32),
        pltpu.SMEM((pieces,), jnp.int32),
        vmem((pieces, rows, LANES), F32),
        vmem((pieces, rows, LANES), F32),
        vmem((n, 2 * rows, LANES), F32),
        vmem((n, 2 * rows + 8, LANES), F32),
        vmem((n, 2 * rows, LANES), F32),
        vmem((n, 2 * rows + 8, LANES), F32),
        vmem((n, 1, LANES), jnp.int32),
        vmem((n, 1, LANES), jnp.int32),
        pltpu.SMEM((n, 1, LANES), jnp.int32),
        pltpu.SMEM((n, 4), jnp.int32),
        vmem((2, pieces, LANES), F32),
        vmem((2, pieces, LANES), F32),
        vmem((pieces, LANES), F32),
        vmem((pieces, LANES), F32),
        pltpu.SMEM((2 * n,), jnp.int32),
        pltpu.SMEM((2 * n,), jnp.int32),
        vmem((1, LANES), jnp.int32),
        pltpu.SMEM((1, LANES), jnp.int32),
        vmem((2 * n + 1, 6 * rows + 8, LANES), F32),
        vmem((rows + 16, ext), F32),
        vmem((rows, LANES), F32),
        vmem((rows, LANES), F32),
        vmem((rows, LANES), F32),
        vmem((rows, LANES), F32),
        vmem((8, COLS_DEV), F32),
        vmem((8, COLS_DEV), F32),
        vmem((8, COLS_DEV), F32),
        vmem((8, COLS_DEV), F32),
        vmem((8, 3 * LANES), F32),
        vmem((8, 3 * LANES), F32),
        vmem((8, 3 * LANES), F32),
        vmem((8, 3 * LANES), F32),
        vmem((1, LANES), F32),
        vmem((n * lats, 1, LANES), F32),
        vmem((2 * ITERS + 1, 8, LANES), F32),
        dma((2, n)),
        dma((2, n)),
        dma((2, n)),
        dma((4,)),
        dma((4,)),
        dma((8,)),
        dma((2, n * lats)),
        dma((6,)),
    ]
    basis, coef = pl.pallas_call(
        functools.partial(kernel, n, lats, pieces, rows),
        out_shape=(
            jax.ShapeDtypeStruct((ITERS + 1, rows + 16, ext), F32),
            jax.ShapeDtypeStruct((16, LANES), F32),
        ),
        in_specs=[pl.BlockSpec(memory_space=pltpu.HBM)] * 4,
        out_specs=(pl.BlockSpec(memory_space=pltpu.VMEM),) * 2,
        scratch_shapes=scratch,
        compiler_params=pltpu.CompilerParams(
            collective_id=0, has_side_effects=True, vmem_limit_bytes=48 * 1024 * 1024
        ),
    )(*(pltpu.with_memory_space_constraint(a, pltpu.HBM) for a in (piece_column, piece_width, piece_height, piece_weight)))
    out = jax.ShapeDtypeStruct((rows, COLS_DEV), F32)
    return pl.pallas_call(
        functools.partial(combine, rows),
        out_shape=(out, out),
        in_specs=[pl.BlockSpec(memory_space=pltpu.VMEM)] * 2,
        out_specs=(pl.BlockSpec(memory_space=pltpu.HBM),) * 2,
        scratch_shapes=[
            vmem((rows, COLS_DEV), F32),
            vmem((rows, COLS_DEV), F32),
            dma((2, CHUNKS)),
        ],
        compiler_params=pltpu.CompilerParams(vmem_limit_bytes=16 * 1024 * 1024),
    )(basis, coef)


def solution(mesh):
    return jax.shard_map(
        functools.partial(body, mesh.shape["lon"], mesh.shape["lat"]),
        mesh=mesh,
        in_specs=(P("lon", "lat", None), P("lon", "lat", None), P("lon"), P("lon")),
        out_specs=(P("lat", "lon"), P("lat", "lon")),
        check_vma=False,
    )
```
